256 devices in a mesh: gx: 64 (over x, z, core), gy: 4 (over y).
Axes of the slice: x: 4, y: 4, z: 8, core: 2. Of those that a mesh axis runs over, the one named last changes fastest.
Arguments:
- populations: float32 [19, 128, 40, 512], P(None, 'gx', None, 'gy'), may hold values from 0.5 to 1.5
- mass: float32 [128, 40, 512], P('gx', None, 'gy'), may hold values from 0.05 to 1
- cell_type: int32 [128, 40, 512], P('gx', None, 'gy'), may hold values from 0 to 2, as said below
- bubble_id: int32 [128, 40, 512], P('gx', None, 'gy'), may hold values from 0 to 63, as said below
- slab_source: int32 [64], replicated, may hold values from 0 to 63, each once
- gas_density: float32 [64], replicated, may hold values from 0.8 to 1.2
Outputs:
- distributions: float32 [19, 128, 40, 512], P(None, 'gx', None, 'gy')
- fluid_mass: float32 [128, 40, 512], P('gx', None, 'gy')
- gas_fraction: float32 [64], replicated
The draws below stay inside these ranges and needn't reach their ends.
Inputs may be any that keep to these rules, and one draw needn't show every extreme that they name: `slab_source`: a permutation. `cell_type`: 0 gas, 1 interface, 2 liquid; the gas cells form 64 connected ellipsoidal blobs, and a gas cell's 18 lattice neighbours are gas or interface, never liquid. `bubble_id`: constant on the gas cells of one blob; every bubble has gas cells.
All inputs are finite; a program needn't handle non-finite values.
Results may differ from the reference program's by a relative error of at most 0.0003.
Values sent between devices are 32-bit elements; how exact they have to be, the bound alone decides.
A program may use at most 64 MiB of HBM per device.

```python
import jax
import jax.numpy as jnp
from jax import lax

CX = 2
NZ = 40
BUBBLES = 64
ITERS = 3
SLABS = 64
NX = 128
NY = 512


NEIGHBOURS = ((1, 0, 0), (-1, 0, 0), (0, 1, 0), (0, -1, 0), (0, 0, 1), (0, 0, -1), (1, 1, 0), (-1, -1, 0), (1, -1, 0), (-1, 1, 0), (1, 0, 1), (-1, 0, -1), (1, 0, -1), (-1, 0, 1), (0, 1, 1), (0, -1, -1), (0, 1, -1), (0, -1, 1))


def blob_fields(key):
    count_y = BUBBLES // 8
    tile_x = NX // 8
    tile_y = NY // count_y
    keys = jax.random.split(key, 5)
    jitter_x = jax.random.randint(keys[0], (BUBBLES,), -(tile_x // 8), tile_x // 8 + 1)
    semi_x = jax.random.randint(keys[1], (BUBBLES,), max(1, tile_x // 5), max(2, tile_x // 2 - tile_x // 8 - 1))
    semi_y = jax.random.randint(keys[2], (BUBBLES,), max(1, tile_y // 5), max(2, tile_y // 2 - 1))
    semi_z = jax.random.randint(keys[3], (BUBBLES,), max(1, NZ // 4), max(2, NZ // 2 + 1))
    centre_z = NZ // 2 + jax.random.randint(keys[4], (BUBBLES,), -(NZ // 4), NZ // 4 + 1)
    xs = jnp.arange(NX, dtype=jnp.int32)[:, None, None]
    zs = jnp.arange(NZ, dtype=jnp.int32)[None, :, None]
    ys = jnp.arange(NY, dtype=jnp.int32)[None, None, :]
    block_x = xs // tile_x
    block_y = jnp.clip((ys + tile_y // 2) // tile_y, 0, count_y - 1)
    tile = jnp.broadcast_to(block_x * count_y + block_y, (NX, NZ, NY)).astype(jnp.int32)
    centre_x = block_x * tile_x + tile_x // 2 + jitter_x[tile]
    centre_y = block_y * tile_y
    span_x = semi_x[tile]
    span_y = semi_y[tile]
    span_z = semi_z[tile]
    off_x = jnp.clip(xs - centre_x, -(span_x + 1), span_x + 1)
    off_y = jnp.clip(ys - centre_y, -(span_y + 1), span_y + 1)
    off_z = jnp.clip(zs - centre_z[tile], -(span_z + 1), span_z + 1)
    sq_x = span_x * span_x
    sq_y = span_y * span_y
    sq_z = span_z * span_z
    level = off_x * off_x * sq_y * sq_z + off_y * off_y * sq_x * sq_z + off_z * off_z * sq_x * sq_y
    gas = level <= sq_x * sq_y * sq_z
    padded_gas = jnp.pad(gas, ((0, 0), (1, 1), (1, 1)))
    near = jnp.zeros_like(gas)
    for step_x, step_y, step_z in NEIGHBOURS:
        rolled = jnp.roll(padded_gas, step_x, axis=0)
        near = near | rolled[:, 1 + step_z:1 + step_z + NZ, 1 + step_y:1 + step_y + NY]
    kinds = jnp.where(gas, 0, jnp.where(near, 1, 2)).astype(jnp.int32)
    return (kinds, tile)


def draw_cell_type(key, part):
    kinds, tile = blob_fields(key)
    return kinds


def draw_bubble_id(key, part):
    kinds, tile = blob_fields(key)
    label_key = jax.random.fold_in(key, 7)
    labels = jax.random.permutation(label_key, jnp.arange(BUBBLES, dtype=jnp.int32))
    return labels[tile].astype(jnp.int32)


def steps_of(key, extent, cuts, smallest, largest):
    gain, own = 1.0, jax.random.fold_in(key, 6)
    for axis_at, blocks in cuts:
        draws = jnp.exp(jax.random.uniform(jax.random.fold_in(own, axis_at), (blocks,), jnp.float32, smallest / len(cuts), largest / len(cuts)))
        gain = gain * jnp.repeat(draws, extent[axis_at] // blocks).reshape([-1 if axis == axis_at else 1 for axis in range(len(extent))])
    return gain


def setup_inputs(seed: int = 0) -> dict:
    key_of = jax.random.split(jax.random.key(seed), 7)
    return {
        "populations": jnp.clip(1.0 + 0.1 * jax.random.normal(key_of[0], (19, NX, NZ, NY), jnp.float32), 0.5, 1.5),
        "mass": jnp.clip(0.05 + 0.95 * jax.random.uniform(key_of[1], (NX, NZ, NY), jnp.float32) ** steps_of(key_of[1], (NX, NZ, NY), ((0, 64), (2, 4)), -0.2, 0.2), 0.05, 1.0),
        "cell_type": draw_cell_type(jax.random.fold_in(key_of[6], 71), 0),
        "bubble_id": draw_bubble_id(jax.random.fold_in(key_of[6], 71), 0),
        "slab_source": jax.random.permutation(key_of[4], SLABS).astype(jnp.int32),
        "gas_density": jnp.clip(jax.random.uniform(key_of[5], (BUBBLES,), jnp.float32, 0.8, 1.2), 0.8, 1.2),
    }


LATTICE = ((0, 0, 0), (1, 0, 0), (-1, 0, 0), (0, 1, 0), (0, -1, 0), (0, 0, 1), (0, 0, -1),
           (1, 1, 0), (-1, -1, 0), (1, -1, 0), (-1, 1, 0), (1, 0, 1), (-1, 0, -1), (1, 0, -1),
           (-1, 0, 1), (0, 1, 1), (0, -1, -1), (0, 1, -1), (0, -1, 1))
OPPOSITE = (0, 2, 1, 4, 3, 6, 5, 8, 7, 10, 9, 12, 11, 14, 13, 16, 15, 18, 17)
WEIGHTS = (1.0 / 3.0,) + (1.0 / 18.0,) * 6 + (1.0 / 36.0,) * 12
OMEGA = 1.6


def equilibrium(rho, speed_x, speed_y, speed_z):
    usq = speed_x * speed_x + speed_y * speed_y + speed_z * speed_z
    terms = []
    for index in range(19):
        step_x, step_y, step_z = LATTICE[index]
        along = step_x * speed_x + step_y * speed_y + step_z * speed_z
        terms.append(WEIGHTS[index] * rho * (1.0 + 3.0 * along + 4.5 * along * along - 1.5 * usq))
    return jnp.stack(terms)


def moments(dist):
    rho = jnp.sum(dist, axis=0)
    speeds = []
    for axis_pos in range(3):
        column = jnp.array([entry[axis_pos] for entry in LATTICE], jnp.float32)
        speeds.append(jnp.einsum("q,q...->...", column, dist, precision=lax.Precision.HIGHEST) / rho)
    return rho, speeds


def padded(field, value):
    wrapped = jnp.concatenate([field[..., -1:, :, :], field, field[..., :1, :, :]], axis=-3)
    widths = [(0, 0)] * (field.ndim - 2) + [(1, 1), (1, 1)]
    return jnp.pad(wrapped, widths, constant_values=value)


def reference(populations, mass, cell_type, bubble_id, slab_source, gas_density):
    def placed(array, axis):
        shape = array.shape
        parts = shape[:axis] + (SLABS, CX) + shape[axis + 1:]
        return jnp.take(array.reshape(parts), slab_source, axis=axis).reshape(shape)

    weight_col = jnp.array(WEIGHTS, jnp.float32).reshape(19, 1, 1, 1)
    dist = placed(populations, 1) * weight_col
    liquid_mass = placed(mass, 0)
    kind = placed(cell_type, 0)
    bubble = placed(bubble_id, 0)
    gas = kind == 0
    face = kind == 1
    liquid = kind == 2
    fluid = kind >= 1
    kind_pad = padded(kind, -1)

    def volumes(fill):
        share = jnp.where(gas, 1.0, jnp.where(face, 1.0 - fill, 0.0)).astype(jnp.float32)
        return jax.ops.segment_sum(share.reshape(-1), bubble.reshape(-1), num_segments=BUBBLES)

    rho = jnp.sum(dist, axis=0)
    fill = jnp.where(liquid, 1.0, jnp.where(face, liquid_mass / rho, 0.0))
    start = volumes(fill)
    density = gas_density
    volume = start
    for step in range(ITERS):
        rho, speeds = moments(dist)
        speed_x, speed_y, speed_z = speeds
        post = jnp.where(fluid[None], dist - OMEGA * (dist - equilibrium(rho, speed_x, speed_y, speed_z)), dist)
        gas_rho = density[bubble]
        gas_eq = equilibrium(gas_rho, speed_x, speed_y, speed_z)
        post_pad = padded(post, 0.0)
        fill_pad = padded(fill, 0.0)
        incoming = []
        gained = jnp.zeros_like(rho)
        for index in range(19):
            step_x, step_y, step_z = LATTICE[index]
            back = OPPOSITE[index]
            window = (slice(1 - step_x, 1 - step_x + NX), slice(1 - step_z, 1 - step_z + NZ),
                      slice(1 - step_y, 1 - step_y + NY))
            source = post_pad[index][window]
            near = kind_pad[window]
            near_fill = fill_pad[window]
            rebuilt = gas_eq[index] + gas_eq[back] - post[back]
            incoming.append(jnp.where(near >= 1, source, jnp.where(near == 0, rebuilt, post[back])))
            share = jnp.where(near == 2, 1.0, jnp.where(near == 1, 0.5 * (fill + near_fill), 0.0))
            gained = gained + share * (source - post[back])
        read = jnp.stack(incoming)
        new_rho = jnp.sum(read, axis=0)
        liquid_mass = jnp.where(face, liquid_mass + gained, jnp.where(liquid, new_rho, 0.0))
        fill = jnp.where(liquid, 1.0, jnp.where(face, liquid_mass / new_rho, 0.0))
        volume = volumes(fill)
        density = gas_density * start / volume
        dist = jnp.where(gas[None], weight_col * density[bubble][None], read)
    return dist / weight_col, liquid_mass, volume * (BUBBLES / (NX * NY * NZ))
```

```python
import functools

import jax
import jax.numpy as jnp
from jax import lax
from jax.experimental import pallas as pl
from jax.experimental.pallas import tpu as pltpu
from jax.sharding import PartitionSpec as P

BUBBLES = 64
ITERS = 3
OMEGA = 1.6
MESH = pl.DeviceIdType.MESH
F32 = jnp.float32

LATTICE = (
    (0, 0, 0),
    (1, 0, 0),
    (-1, 0, 0),
    (0, 1, 0),
    (0, -1, 0),
    (0, 0, 1),
    (0, 0, -1),
    (1, 1, 0),
    (-1, -1, 0),
    (1, -1, 0),
    (-1, 1, 0),
    (1, 0, 1),
    (-1, 0, -1),
    (1, 0, -1),
    (-1, 0, 1),
    (0, 1, 1),
    (0, -1, -1),
    (0, 1, -1),
    (0, -1, 1),
)
HALF = 19
ORDER = (1, 7, 9, 11, 13, HALF, 2, 8, 10, 12, 14, 0, 3, 4, 5, 6, 15, 16, 17, 18)
AT = {field: pos for pos, field in enumerate(ORDER)}
KIND = 20
COLS_UP = (3, 7, 10, 15, 17, HALF, KIND)
COLS_DOWN = (4, 8, 9, 16, 18, HALF, KIND)
PAIRS = ((1, 2), (3, 4), (5, 6), (7, 8), (9, 10), (11, 12), (13, 14), (15, 16), (17, 18))
PAD = 8


def pair_speeds(ux, uy, uz):
    return (ux, uy, uz, ux + uy, ux - uy, ux + uz, ux - uz, uy + uz, uy - uz)


def kernel(
    shape,
    pop,
    mass,
    cell,
    label,
    source,
    gas_density,
    out_g,
    out_m,
    out_v,
    stage,
    got,
    sorted_pieces,
    home,
    post,
    kinds,
    near,
    waiting,
    speed,
    bubble,
    reversed_label,
    fluid_mass,
    share,
    base_rho,
    gas_rho,
    gain,
    gas_here,
    members,
    cols_out,
    cols_in,
    cols,
    sums_a,
    sums_b,
    part,
    send,
    recv,
):
    nx, nz, ny = shape
    ngx = nx * nz * 2
    chips = nx * nz
    per = tiles_per_chip(chips)
    big = (per + 1) // 2
    small = per - big
    gx = lax.axis_index("gx")
    gy = lax.axis_index("gy")
    core = gx % 2
    chip = gx // 2
    pos_x = chip // nz
    pos_z = chip % nz
    right = (gx + 1) % ngx
    left = (gx + ngx - 1) % ngx
    lane = lax.broadcasted_iota(jnp.int32, (8, 128), 1)

    SPREAD, GATHER, KINDS = 0, 1, 2

    def x_sem(step, side):
        return 4 + step * 8 + side

    def y_sem(step, side):
        return 4 + step * 8 + 2 + side

    def a_sem(step):
        return 4 + step * 8 + 4

    def b_sem(step):
        return 4 + step * 8 + 5

    def remote(src, dst, sem, to_x, to_y):
        return pltpu.make_async_remote_copy(
            src_ref=src,
            dst_ref=dst,
            send_sem=send.at[sem],
            recv_sem=recv.at[sem],
            device_id=(to_x, to_y),
            device_id_type=MESH,
        )

    def wait_bytes(ref, sem):
        pltpu.make_async_copy(ref, ref, sem).wait()

    barrier = pltpu.get_barrier_semaphore()

    def greet_x(k, carry):
        pl.semaphore_signal(
            barrier, inc=1, device_id=((gx + k) % ngx, gy), device_id_type=MESH
        )
        return carry

    lax.fori_loop(1, ngx, greet_x, 0)
    group_a = nz * 2
    group_b = nx * ny
    at_a = gx % group_a
    at_b = pos_x * ny + gy

    def peer_b(k):
        other = (at_b + k) % group_b
        return (other // ny) * group_a + at_a, other % ny

    greeted = ngx - 1

    def greet_b(k, carry):
        to_x, to_y = peer_b(k)

        @pl.when(to_y != gy)
        def _():
            pl.semaphore_signal(barrier, inc=1, device_id=(to_x, to_y), device_id_type=MESH)

        return carry

    lax.fori_loop(1, group_b, greet_b, 0)
    greeted += group_b - nx
    for to_x in (left, right):
        for to_y in ((gy + 1) % ny, (gy + ny - 1) % ny):
            pl.semaphore_signal(barrier, inc=1, device_id=(to_x, to_y), device_id_type=MESH)
    greeted += 4

    stage[0:190] = pop[...]
    stage[190:200] = mass[...]
    stage[200:210] = cell[...].astype(F32)
    stage[210:220] = label[...].astype(F32)
    walls = jnp.full((PAD, 128), -1.0, F32)
    for slot in range(4):
        kinds[slot, 0:PAD] = walls
        kinds[slot, PAD + 40 : PAD + 48] = walls
    for side in range(2):
        cols[side, 0:PAD] = walls
        cols[side, PAD + 40 : PAD + 48] = walls
    pl.semaphore_wait(barrier, greeted)

    def peer_chip(k):
        dz = (3 * (k // nx) + nz // 2) % nz
        dx = k % nx
        return ((pos_x + dx) % nx) * nz + (pos_z + dz) % nz

    def spread(k, carry):
        to = peer_chip(k)
        for side, tiles in ((0, big), (1, small)):
            peer = to * 2 + side

            @pl.when(peer != gx)
            def _():
                remote(
                    stage.at[pl.ds(to * per + side * big, tiles)],
                    got.at[gx, pl.ds(0, tiles)],
                    SPREAD,
                    peer,
                    gy,
                ).start()

        return carry

    lax.fori_loop(0, chips, spread, 0)
    mine = chip * per + core * big
    got[gx] = stage[pl.ds(mine, big)]

    def take(k, carry):
        sorted_pieces[k] = got[source[k]]
        return carry

    for side, tiles in ((0, big), (1, small)):

        @pl.when(core == side)
        def _():
            wait_bytes(got.at[pl.ds(0, ngx - 1), pl.ds(0, tiles)], recv.at[SPREAD])

    lax.fori_loop(0, ngx, take, 0, unroll=4)

    def gather(k, carry):
        to = peer_chip(k)
        for other in range(2):
            peer = to * 2 + other
            for side, tiles in ((0, big), (1, small)):

                @pl.when((peer != gx) & (core == side))
                def _():
                    remote(
                        sorted_pieces.at[peer, pl.ds(0, tiles)],
                        home.at[pl.ds(chip * per + side * big, tiles)],
                        GATHER,
                        peer,
                        gy,
                    ).start()

        return carry

    lax.fori_loop(0, chips, gather, 0)
    for side, tiles in ((0, big), (1, small)):

        @pl.when(core == side)
        def _():
            home[pl.ds(chip * per + side * big, tiles)] = sorted_pieces[gx, 0:tiles]
            wait_bytes(home.at[pl.ds(0, chips * per - tiles)], recv.at[GATHER])

    for x in range(2):
        for z in range(5):
            kinds[x + 1, PAD + z * 8 : PAD + z * 8 + 8] = home[200 + x * 5 + z]
    rows = pl.ds(PAD, 40)
    kinds_right = remote(kinds.at[2, rows], kinds.at[0, rows], KINDS, right, gy)
    kinds_left = remote(kinds.at[1, rows], kinds.at[3, rows], KINDS + 1, left, gy)
    kinds_right.start()
    kinds_left.start()

    def collide(step, i, g):
        x, z = i // 5, i % 5
        diff = [g[a] - g[b] for a, b in PAIRS]
        total = [g[a] + g[b] for a, b in PAIRS]
        faces = total[0] + total[1] + total[2]
        edges = (total[3] + total[4]) + (total[5] + total[6]) + (total[7] + total[8])
        rho = g[0] * (1.0 / 3.0) + faces * (1.0 / 18.0) + edges * (1.0 / 36.0)
        inv = 1.0 / rho
        ux = (diff[0] * (1.0 / 18.0) + (diff[3] + diff[4] + diff[5] + diff[6]) * (1.0 / 36.0)) * inv
        uy = (diff[1] * (1.0 / 18.0) + (diff[3] - diff[4] + diff[7] + diff[8]) * (1.0 / 36.0)) * inv
        uz = (diff[2] * (1.0 / 18.0) + (diff[5] - diff[6] + diff[7] - diff[8]) * (1.0 / 36.0)) * inv
        speed[0, i] = ux
        speed[1, i] = uy
        speed[2, i] = uz
        scaled = OMEGA * rho
        flat = scaled * (1.0 - 1.5 * (ux * ux + uy * uy + uz * uz))
        at = pl.ds(pl.multiple_of(PAD + z * 8, 8), 8)
        post[step, x + 1, AT[0], at] = flat + (1.0 - OMEGA) * g[0]
        square = 4.5 * scaled
        line = 3.0 * scaled
        for (a, b), along in zip(PAIRS, pair_speeds(ux, uy, uz)):
            even = flat + square * (along * along)
            odd = line * along
            post[step, x + 1, AT[a], at] = even + odd + (1.0 - OMEGA) * g[a]
            post[step, x + 1, AT[b], at] = even - odd + (1.0 - OMEGA) * g[b]
        return rho

    def put_half(step, i, value):
        x, z = i // 5, i % 5
        post[step, x + 1, AT[HALF], pl.ds(pl.multiple_of(PAD + z * 8, 8), 8)] = 0.5 * value

    def level(kind, liquid_mass, rho):
        phi = jnp.where(kind == 2.0, 1.0, jnp.where(kind == 1.0, liquid_mass / rho, 0.0))
        part_gas = jnp.where(kind == 0.0, 1.0, jnp.where(kind == 1.0, 1.0 - phi, 0.0))
        return phi, part_gas

    def send_faces(step):
        plus = remote(
            post.at[step, 2, pl.ds(0, 6), rows],
            post.at[step, 0, pl.ds(0, 6), rows],
            x_sem(step, 0),
            right,
            gy,
        )
        minus = remote(
            post.at[step, 1, pl.ds(5, 6), rows],
            post.at[step, 3, pl.ds(5, 6), rows],
            x_sem(step, 1),
            left,
            gy,
        )
        plus.start()
        minus.start()

        def pack(z, carry):
            at = pl.ds(pl.multiple_of(PAD + z * 8, 8), 8)
            up = jnp.zeros((8, 128), F32)
            down = jnp.zeros((8, 128), F32)
            for j in range(7 if step == 0 else 6):
                for x in range(2):
                    spot = j * 4 + x + 1
                    if COLS_UP[j] == KIND:
                        high = low = kinds[x + 1, at]
                    else:
                        high = post[step, x + 1, AT[COLS_UP[j]], at]
                        low = post[step, x + 1, AT[COLS_DOWN[j]], at]
                    up = jnp.where(lane == spot, pltpu.roll(high, spot + 1, 1), up)
                    down = jnp.where(lane == spot, pltpu.roll(low, spot, 1), down)
            to = pl.ds(pl.multiple_of(z * 8, 8), 8)
            cols_out[step, 0, to] = up
            cols_out[step, 1, to] = down
            return carry

        lax.fori_loop(0, 5, pack, 0)
        for side, there, to_y in ((0, gy < ny - 1, gy + 1), (1, gy > 0, gy - 1)):

            @pl.when(there)
            def _():
                for shift, to_x in ((-1, left), (0, gx), (1, right)):
                    remote(
                        cols_out.at[step, side],
                        cols_in.at[step, side, 1 - shift],
                        y_sem(step, side),
                        to_x,
                        to_y,
                    ).start()

        return plus, minus

    def wait_columns(step):
        for side, there in ((0, gy > 0), (1, gy < ny - 1)):

            @pl.when(there)
            def _():
                wait_bytes(cols_in.at[step, side], recv.at[y_sem(step, side)])

            def merge(z, carry):
                of = pl.ds(pl.multiple_of(z * 8, 8), 8)
                before = pltpu.roll(cols_in[step, side, 0, of], 126, 1)
                after = pltpu.roll(cols_in[step, side, 2, of], 2, 1)
                slot = lane % 4
                here = cols_in[step, side, 1, of]
                cols[side, pl.ds(pl.multiple_of(PAD + z * 8, 8), 8)] = jnp.where(
                    slot == 0, before, jnp.where(slot == 3, after, here)
                )
                return carry

            lax.fori_loop(0, 5, merge, 0)

    def shifted(value, step_y, j, slot, at, outside):
        if step_y == 0:
            return value
        if step_y == 1:
            edge = pltpu.roll(cols[0, at], 128 - (j * 4 + slot), 1)
            if outside is not None:
                edge = jnp.where(outside[0], -1.0, edge)
            return jnp.where(lane == 0, edge, pltpu.roll(value, 1, 1))
        edge = pltpu.roll(cols[1, at], 127 - (j * 4 + slot), 1)
        if outside is not None:
            edge = jnp.where(outside[1], -1.0, edge)
        return jnp.where(lane == 127, edge, pltpu.roll(value, 127, 1))

    def find_near(i, carry):
        x, z = i // 5, i % 5
        row = PAD + z * 8
        for d in range(1, 19):
            step_x, step_y, step_z = LATTICE[d]
            slot = x + 1 - step_x
            at = pl.ds(row - step_z, 8)
            near[d, i] = shifted(kinds[slot, at], step_y, 6, slot, at, (gy == 0, gy == ny - 1))
        return carry

    def twice_even(i):
        ux, uy, uz = speed[0, i], speed[1, i], speed[2, i]
        flat = 2.0 - 3.0 * (ux * ux + uy * uy + uz * uz)
        return [flat + 9.0 * (along * along) for along in pair_speeds(ux, uy, uz)]

    def stream(step, i):
        x, z = i // 5, i % 5
        row = PAD + z * 8
        own = pl.ds(pl.multiple_of(row, 8), 8)
        half = post[step, x + 1, AT[HALF], own]
        rest = post[step, x + 1, AT[0], own]
        waiting[0, i] = rest
        zero = jnp.zeros((8, 128), F32)
        rho_sum = [zero, zero]
        gas_sum = [zero, zero]
        gain_sum = [zero, zero]
        for k, ((a, b), even) in enumerate(zip(PAIRS, twice_even(i))):
            kind_of = 0 if k < 3 else 1
            here = {a: post[step, x + 1, AT[a], own], b: post[step, x + 1, AT[b], own]}
            for d, back in ((a, b), (b, a)):
                step_x, step_y, step_z = LATTICE[d]
                slot = x + 1 - step_x
                at = pl.ds(row - step_z, 8)
                j = 0 if step_y == 0 else (COLS_UP if step_y == 1 else COLS_DOWN).index(d)
                came = shifted(post[step, slot, AT[d], at], step_y, j, slot, at, None)
                near_half = shifted(post[step, slot, AT[HALF], at], step_y, 5, slot, at, None)
                kind = near[d, i]
                bounced = here[back]
                value = jnp.where(kind >= 1.0, came, bounced)
                gas = kind == 0.0
                known = jnp.where(gas, -bounced, value)
                waiting[d, i] = known
                rho_sum[kind_of] = rho_sum[kind_of] + known
                gas_sum[kind_of] = gas_sum[kind_of] + jnp.where(gas, even, 0.0)
                part_of = jnp.where(
                    kind == 2.0, 1.0, jnp.where(kind == 1.0, half + near_half, 0.0)
                )
                gain_sum[kind_of] = gain_sum[kind_of] + part_of * (value - bounced)
        base_rho[i] = (
            rest * (1.0 / 3.0) + rho_sum[0] * (1.0 / 18.0) + rho_sum[1] * (1.0 / 36.0)
        )
        gas_rho[i] = gas_sum[0] * (1.0 / 18.0) + gas_sum[1] * (1.0 / 36.0)
        gain[i] = gain_sum[0] * (1.0 / 18.0) + gain_sum[1] * (1.0 / 36.0)

    def arrived(i):
        density = gas_here[i]
        g = [waiting[0, i]] + [None] * 18
        for (a, b), even in zip(PAIRS, twice_even(i)):
            lift = density * even
            for d in (a, b):
                known = waiting[d, i]
                g[d] = jnp.where(near[d, i] == 0.0, known + lift, known)
        return g

    def lookup(table):
        def one(i, carry):
            gas_here[i] = jnp.take_along_axis(
                table, bubble[i], axis=1, mode="promise_in_bounds"
            )
            return carry

        lax.fori_loop(0, 10, one, 0, unroll=5)

    def member_sums():
        def one(b, carry):
            members[b] = jnp.sum(jnp.where(reversed_label[...] == b, share[...], 0.0), axis=0)
            return carry

        lax.fori_loop(0, BUBBLES, one, 0, unroll=8)
        now = members[...]
        for bit in range(6):
            half = now.shape[0] // 2
            first, second = now[:half], now[half:]
            odd = ((lax.broadcasted_iota(jnp.int32, first.shape, 2) >> bit) & 1) == 1
            keep = jnp.where(odd, second, first)
            move = jnp.where(odd, first, second)
            now = keep + pltpu.roll(move, 128 - (1 << bit), 2)
        now = now[0]
        return now + pltpu.roll(now, 64, 1)

    def send_sums(dst, own, sem, step, stage_no, count, peer_of):
        def one(k, carry):
            to_x, to_y = peer_of(k)
            remote(part.at[step, stage_no], dst.at[step, own], sem, to_x, to_y).start()
            return carry

        lax.fori_loop(1, count, one, 0)

    def peer_a(k):
        return gx - at_a + (at_a + k) % group_a, gy

    def begin_sum(step, value):
        part[step, 0] = value
        sums_a[step, at_a] = value
        send_sums(sums_a, at_a, a_sem(step), step, 0, group_a, peer_a)

    def middle_sum(step):
        wait_bytes(sums_a.at[step, pl.ds(0, group_a - 1)], recv.at[a_sem(step)])
        value = jnp.sum(sums_a[step], axis=0)
        part[step, 1] = value
        sums_b[step, at_b] = value
        send_sums(sums_b, at_b, b_sem(step), step, 1, group_b, peer_b)

    def end_sum(step):
        wait_bytes(sums_b.at[step, pl.ds(0, group_b - 1)], recv.at[b_sem(step)])
        value = jnp.sum(jnp.sum(sums_b[step], axis=0), axis=0, keepdims=True)
        return jnp.broadcast_to(value, (8, 128))

    def first(i, carry):
        rho = collide(0, i, [home[q * 10 + i] for q in range(19)])
        kind = home[200 + i]
        phi, part_gas = level(kind, home[190 + i], rho)
        put_half(0, i, phi)
        share[i] = part_gas
        fluid_mass[i] = home[190 + i]
        return carry

    lax.fori_loop(0, 10, first, 0)
    faces = send_faces(0)
    started = [faces]
    label_now = home[210:220].astype(jnp.int32)
    bubble[...] = label_now
    turned = jnp.zeros_like(label_now)
    for bit in range(6):
        turned = turned | (((label_now >> bit) & 1) << (5 - bit))
    reversed_label[...] = turned
    volume_start = member_sums()
    bubble_lane = lane & (BUBBLES - 1)
    table = jnp.zeros((8, 128), F32)
    for b in range(BUBBLES):
        table = jnp.where(bubble_lane == b, gas_density[b], table)
    density_start = table
    lookup(table)

    kinds_right.wait_recv()
    kinds_left.wait_recv()
    wait_columns(0)
    lax.fori_loop(0, 10, find_near, 0)
    for face in faces:
        face.wait_recv()

    def stream_all(step):
        def one(i, carry):
            stream(step, i)
            return carry

        lax.fori_loop(0, 10, one, 0)

    stream_all(0)
    start_total = None
    for step in range(ITERS):

        def settle(i, carry):
            kind = home[200 + i]
            rho = base_rho[i] + gas_here[i] * gas_rho[i]
            liquid_mass = jnp.where(
                kind == 1.0, fluid_mass[i] + gain[i], jnp.where(kind == 2.0, rho, 0.0)
            )
            fluid_mass[i] = liquid_mass
            phi, part_gas = level(kind, liquid_mass, rho)
            if step < ITERS - 1:
                put_half(step + 1, i, phi)
            share[i] = part_gas
            return carry

        lax.fori_loop(0, 10, settle, 0, unroll=5)
        volume = member_sums()
        if step == 0:
            volume = jnp.where(lane < BUBBLES, volume, volume_start)
        begin_sum(step, volume)

        if step < ITERS - 1:

            def again(i, carry):
                collide(step + 1, i, arrived(i))
                return carry

            lax.fori_loop(0, 10, again, 0)
            faces = send_faces(step + 1)
            started.append(faces)
            middle_sum(step)
            wait_columns(step + 1)
            for face in faces:
                face.wait_recv()
            stream_all(step + 1)
        else:

            def last(i, carry):
                for q, value in enumerate(arrived(i)):
                    out_g[q * 10 + i] = value
                return carry

            lax.fori_loop(0, 10, last, 0)
            middle_sum(step)
        total = end_sum(step)
        if step == 0:
            other = pltpu.roll(total, 64, 1)
            start_total = jnp.where(lane < BUBBLES, other, total)
            total = jnp.where(lane < BUBBLES, total, other)
        lookup(density_start * start_total / total)

    def finish(i, carry):
        gas = home[200 + i] == 0.0
        density = gas_here[i]
        for q in range(19):
            out_g[q * 10 + i] = jnp.where(gas, density, out_g[q * 10 + i])
        return carry

    lax.fori_loop(0, 10, finish, 0)
    out_m[...] = fluid_mass[...]
    out_v[...] = total * (BUBBLES / (ngx * ny * 2 * 40 * 128))

    for side, tiles in ((0, big), (1, small)):

        @pl.when(core == side)
        def _():
            wait_bytes(stage.at[pl.ds(0, chips * per - tiles)], send.at[SPREAD])
            wait_bytes(sorted_pieces.at[pl.ds(0, ngx - 1), pl.ds(0, tiles)], send.at[GATHER])

    kinds_right.wait_send()
    kinds_left.wait_send()
    for step in range(ITERS):
        for face in started[step]:
            face.wait_send()
        for side, there in ((0, gy < ny - 1), (1, gy > 0)):

            @pl.when(there)
            def _():
                wait_bytes(cols_in.at[step, side], send.at[y_sem(step, side)])

        wait_bytes(sums_a.at[step, pl.ds(0, group_a - 1)], send.at[a_sem(step)])
        wait_bytes(sums_b.at[step, pl.ds(0, group_b - 1)], send.at[b_sem(step)])


def tiles_per_chip(chips):
    return -(-220 // chips)


def solution(mesh):
    ngx, ny = mesh.shape["gx"], mesh.shape["gy"]
    nx, nz = (4, 8) if ngx == 64 else (1, ngx // 2)
    chips = ngx // 2
    per = tiles_per_chip(chips)
    big = (per + 1) // 2
    spare = 2 * big - per

    def per_device(populations, mass, cell_type, bubble_id, slab_source, gas_density):
        vmem = pl.BlockSpec(memory_space=pltpu.VMEM)
        smem = pl.BlockSpec(memory_space=pltpu.SMEM)

        def tiles(count, dtype=F32):
            return pltpu.VMEM((count, 8, 128), dtype)

        g, m, v = pl.pallas_call(
            functools.partial(kernel, (nx, nz, ny)),
            out_shape=(
                jax.ShapeDtypeStruct((190, 8, 128), F32),
                jax.ShapeDtypeStruct((10, 8, 128), F32),
                jax.ShapeDtypeStruct((8, 128), F32),
            ),
            in_specs=[vmem] * 4 + [smem] * 2,
            out_specs=(vmem, vmem, vmem),
            scratch_shapes=[
                tiles(chips * per + spare),
                pltpu.VMEM((ngx, big, 8, 128), F32),
                pltpu.VMEM((ngx, big, 8, 128), F32),
                tiles(chips * per),
                pltpu.VMEM((ITERS, 4, 20, 56, 128), F32),
                pltpu.VMEM((4, 56, 128), F32),
                pltpu.VMEM((19, 10, 8, 128), F32),
                pltpu.VMEM((19, 10, 8, 128), F32),
                pltpu.VMEM((3, 10, 8, 128), F32),
                tiles(10, jnp.int32),
                tiles(10, jnp.int32),
                tiles(10),
                tiles(10),
                tiles(10),
                tiles(10),
                tiles(10),
                tiles(10),
                tiles(BUBBLES),
                pltpu.VMEM((ITERS, 2, 40, 128), F32),
                pltpu.VMEM((ITERS, 2, 3, 40, 128), F32),
                pltpu.VMEM((2, 56, 128), F32),
                pltpu.VMEM((ITERS, nz * 2, 8, 128), F32),
                pltpu.VMEM((ITERS, nx * ny, 8, 128), F32),
                pltpu.VMEM((ITERS, 2, 8, 128), F32),
                pltpu.SemaphoreType.DMA((4 + ITERS * 8,)),
                pltpu.SemaphoreType.DMA((4 + ITERS * 8,)),
            ],
            compiler_params=pltpu.CompilerParams(
                collective_id=0, has_side_effects=True, vmem_limit_bytes=40 * 2**20
            ),
        )(
            populations.reshape(190, 8, 128),
            mass.reshape(10, 8, 128),
            cell_type.reshape(10, 8, 128),
            bubble_id.reshape(10, 8, 128),
            slab_source,
            gas_density,
        )
        return g.reshape(populations.shape), m.reshape(mass.shape), v[0, :BUBBLES]

    return jax.shard_map(
        per_device,
        mesh=mesh,
        in_specs=(
            P(None, "gx", None, "gy"),
            P("gx", None, "gy"),
            P("gx", None, "gy"),
            P("gx", None, "gy"),
            P(),
            P(),
        ),
        out_specs=(P(None, "gx", None, "gy"), P("gx", None, "gy"), P()),
        check_vma=False,
    )
```

```python
import functools

import jax
import jax.numpy as jnp
from jax import lax
from jax.experimental import pallas as pl
from jax.experimental.pallas import tpu as pltpu
from jax.sharding import PartitionSpec as P

BUBBLES = 64
ITERS = 3
OMEGA = 1.6
MESH = pl.DeviceIdType.MESH
F32 = jnp.float32

LATTICE = (
    (0, 0, 0),
    (1, 0, 0),
    (-1, 0, 0),
    (0, 1, 0),
    (0, -1, 0),
    (0, 0, 1),
    (0, 0, -1),
    (1, 1, 0),
    (-1, -1, 0),
    (1, -1, 0),
    (-1, 1, 0),
    (1, 0, 1),
    (-1, 0, -1),
    (1, 0, -1),
    (-1, 0, 1),
    (0, 1, 1),
    (0, -1, -1),
    (0, 1, -1),
    (0, -1, 1),
)
HALF = 19
ORDER = (1, 7, 9, 11, 13, HALF, 2, 8, 10, 12, 14, 0, 3, 4, 5, 6, 15, 16, 17, 18)
AT = {field: pos for pos, field in enumerate(ORDER)}
KIND = 20
COLS_UP = (3, 7, 10, 15, 17, HALF, KIND)
COLS_DOWN = (4, 8, 9, 16, 18, HALF, KIND)
PAIRS = ((1, 2), (3, 4), (5, 6), (7, 8), (9, 10), (11, 12), (13, 14), (15, 16), (17, 18))
PAD = 8


def pair_speeds(ux, uy, uz):
    return (ux, uy, uz, ux + uy, ux - uy, ux + uz, ux - uz, uy + uz, uy - uz)


def far_first(size):
    return sorted(range(size), key=lambda d: -min(d, size - d))


def kernel(
    shape,
    pop,
    mass,
    cell,
    label,
    source_in,
    density_in,
    out_g,
    out_m,
    out_v,
    stage,
    ints,
    source,
    gas_density,
    got_a,
    got_b,
    sorted_a,
    sorted_b,
    home,
    post,
    kinds,
    near,
    waiting,
    speed,
    bubble,
    reversed_label,
    fluid_mass,
    share,
    base_rho,
    gas_rho,
    gain,
    gas_here,
    members,
    cols_out,
    cols_in,
    cols,
    mate_sum,
    sums,
    part,
    fetch,
    send,
    recv,
    row_ready,
):
    nx, nz, ny = shape
    ngx = nx * nz * 2
    chips = nx * nz
    gx = lax.axis_index("gx")
    gy = lax.axis_index("gy")
    core = gx % 2
    chip = gx // 2
    pos_x = chip // nz
    pos_z = chip % nz
    mate = gx + 1 - 2 * core
    right = (gx + 1) % ngx
    left = (gx + ngx - 1) % ngx
    lane = lax.broadcasted_iota(jnp.int32, (8, 128), 1)

    SPREAD, GATHER, KINDS = 0, 2, 4

    def x_sem(step, side):
        return 8 + step * 8 + side

    def y_sem(step, side):
        return 8 + step * 8 + 2 + side

    def mate_sem(step):
        return 8 + step * 8 + 4

    def all_sem(step):
        return 8 + step * 8 + 5

    def remote(src, dst, sem, to_x, to_y):
        return pltpu.make_async_remote_copy(
            src_ref=src,
            dst_ref=dst,
            send_sem=send.at[sem],
            recv_sem=recv.at[sem],
            device_id=(to_x, to_y),
            device_id_type=MESH,
        )

    def wait_bytes(ref, sem):
        pltpu.make_async_copy(ref, ref, sem).wait()

    at_x = [lax.rem(pos_x + d, nx) * nz for d in range(nx)]
    at_z = [lax.rem(pos_z + d, nz) for d in range(nz)]
    at_y = [lax.rem(gy + d, ny) for d in range(ny)]
    far_chips = [(dz, dx) for dz in far_first(nz) for dx in far_first(nx)]
    peers = [
        (at_x[dx] + at_z[dz], other, dx == dz == 0 and other is core)
        for dz, dx in far_chips
        for other in (1 - core, core)
    ]

    fetches = [
        pltpu.make_async_copy(src, dst, fetch.at[k])
        for k, (src, dst) in enumerate(
            (
                (cell, ints.at[0:10]),
                (label, ints.at[10:20]),
                (pop, stage.at[30:220]),
                (mass, stage.at[20:30]),
                (source_in, source),
                (density_in, gas_density),
            )
        )
    ]
    for one in fetches:
        one.start()

    barrier = pltpu.get_barrier_semaphore()

    for to_chip, to_core, near_by in peers:
        if not near_by:
            pl.semaphore_signal(
                barrier, inc=1, device_id=(to_chip * 2 + to_core, gy), device_id_type=MESH
            )
    for k in range(1, ny):
        pl.semaphore_signal(
            barrier, inc=1, device_id=(gx, (gy + k) % ny), device_id_type=MESH
        )

    walls = jnp.full((PAD, 128), -1.0, F32)
    for slot in range(4):
        kinds[slot, 0:PAD] = walls
        kinds[slot, PAD + 40 : PAD + 48] = walls
    for side in range(2):
        cols[side, 0:PAD] = walls
        cols[side, PAD + 40 : PAD + 48] = walls
    for one in fetches:
        one.wait()
    stage[0:20] = ints[...].astype(F32)
    pl.semaphore_wait(barrier, ngx - 1 + ny - 1)
    for k in range(1, ny):
        pl.semaphore_signal(
            row_ready, inc=1, device_id=(gx, (gy + k) % ny), device_id_type=MESH
        )

    chunks = []
    base = 0
    for per, got, pieces in zip(chunk_tiles(chips), (got_a, got_b), (sorted_a, sorted_b)):
        big = (per + 1) // 2
        chunks.append((base, per, big, ((0, big), (1, per - big)), got, pieces))
        base += per * chips

    def spread(which):
        base, per, big, sides, got, pieces = chunks[which]

        for own, _ in sides:

            @pl.when(core == own)
            def _():
                for dz, dx in far_chips:
                    to = at_x[dx] + at_z[dz]
                    for side, tiles in sides:
                        if dx == dz == 0 and side == own:
                            continue
                        remote(
                            stage.at[pl.ds(base + to * per + side * big, tiles)],
                            got.at[gx, pl.ds(0, tiles)],
                            SPREAD + which,
                            to * 2 + side,
                            gy,
                        ).start()

        got[gx] = stage[pl.ds(base + chip * per + core * big, big)]

    def pick(which):
        base, per, big, sides, got, pieces = chunks[which]
        for side, tiles in sides:

            @pl.when(core == side)
            def _():
                wait_bytes(got.at[pl.ds(0, ngx - 1), pl.ds(0, tiles)], recv.at[SPREAD + which])

        def one(k, carry):
            pieces[k] = got[source[k]]
            return carry

        lax.fori_loop(0, ngx, one, 0, unroll=8)

    def gather(which):
        base, per, big, sides, got, pieces = chunks[which]
        for side, tiles in sides:

            @pl.when(core == side)
            def _():
                at = pl.ds(base + chip * per + side * big, tiles)

                for dz, dx in far_chips:
                    for other in range(2):
                        if dx == dz == 0 and side == other:
                            continue
                        peer = (at_x[dx] + at_z[dz]) * 2 + other
                        remote(
                            pieces.at[peer, pl.ds(0, tiles)],
                            home.at[at],
                            GATHER + which,
                            peer,
                            gy,
                        ).start()
                home[at] = pieces[gx, 0:tiles]

    def gathered(which):
        base, per, big, sides, got, pieces = chunks[which]
        for side, tiles in sides:

            @pl.when(core == side)
            def _():
                wait_bytes(
                    home.at[pl.ds(base, chips * per - tiles)], recv.at[GATHER + which]
                )

    spread(0)
    spread(1)
    pick(0)
    gather(0)
    pick(1)
    gather(1)

    gathered(0)
    for x in range(2):
        for z in range(5):
            kinds[x + 1, PAD + z * 8 : PAD + z * 8 + 8] = home[x * 5 + z]
    rows = pl.ds(PAD, 40)
    kinds_right = remote(kinds.at[2, rows], kinds.at[0, rows], KINDS, right, gy)
    kinds_left = remote(kinds.at[1, rows], kinds.at[3, rows], KINDS + 1, left, gy)
    kinds_right.start()
    kinds_left.start()
    label_now = home[10:20].astype(jnp.int32)
    bubble[...] = label_now
    turned = jnp.zeros_like(label_now)
    for bit in range(6):
        turned = turned | (((label_now >> bit) & 1) << (5 - bit))
    reversed_label[...] = turned
    fluid_mass[...] = home[20:30]

    def collide(step, i, g):
        x, z = i // 5, i % 5
        diff = [g[a] - g[b] for a, b in PAIRS]
        total = [g[a] + g[b] for a, b in PAIRS]
        faces = total[0] + total[1] + total[2]
        edges = (total[3] + total[4]) + (total[5] + total[6]) + (total[7] + total[8])
        rho = g[0] * (1.0 / 3.0) + faces * (1.0 / 18.0) + edges * (1.0 / 36.0)
        inv = 1.0 / rho
        ux = (diff[0] * (1.0 / 18.0) + (diff[3] + diff[4] + diff[5] + diff[6]) * (1.0 / 36.0)) * inv
        uy = (diff[1] * (1.0 / 18.0) + (diff[3] - diff[4] + diff[7] + diff[8]) * (1.0 / 36.0)) * inv
        uz = (diff[2] * (1.0 / 18.0) + (diff[5] - diff[6] + diff[7] - diff[8]) * (1.0 / 36.0)) * inv
        speed[0, i] = ux
        speed[1, i] = uy
        speed[2, i] = uz
        scaled = OMEGA * rho
        flat = scaled * (1.0 - 1.5 * (ux * ux + uy * uy + uz * uz))
        at = pl.ds(pl.multiple_of(PAD + z * 8, 8), 8)
        post[step, x + 1, AT[0], at] = flat + (1.0 - OMEGA) * g[0]
        square = 4.5 * scaled
        line = 3.0 * scaled
        for (a, b), along in zip(PAIRS, pair_speeds(ux, uy, uz)):
            even = flat + square * (along * along)
            odd = line * along
            post[step, x + 1, AT[a], at] = even + odd + (1.0 - OMEGA) * g[a]
            post[step, x + 1, AT[b], at] = even - odd + (1.0 - OMEGA) * g[b]
        return rho

    def put_half(step, i, value):
        x, z = i // 5, i % 5
        post[step, x + 1, AT[HALF], pl.ds(pl.multiple_of(PAD + z * 8, 8), 8)] = 0.5 * value

    def level(kind, liquid_mass, rho):
        phi = jnp.where(kind == 2.0, 1.0, jnp.where(kind == 1.0, liquid_mass / rho, 0.0))
        part_gas = jnp.where(kind == 0.0, 1.0, jnp.where(kind == 1.0, 1.0 - phi, 0.0))
        return phi, part_gas

    def send_faces(step):
        plus = remote(
            post.at[step, 2, pl.ds(0, 6), rows],
            post.at[step, 0, pl.ds(0, 6), rows],
            x_sem(step, 0),
            right,
            gy,
        )
        minus = remote(
            post.at[step, 1, pl.ds(5, 6), rows],
            post.at[step, 3, pl.ds(5, 6), rows],
            x_sem(step, 1),
            left,
            gy,
        )
        plus.start()
        minus.start()
        return plus, minus

    def send_columns(step):
        def pack(z, carry):
            at = pl.ds(pl.multiple_of(PAD + z * 8, 8), 8)
            up = jnp.zeros((8, 128), F32)
            down = jnp.zeros((8, 128), F32)
            for j in range(7 if step == 0 else 6):
                for x in range(2):
                    spot = j * 4 + x + 1
                    if COLS_UP[j] == KIND:
                        high = low = kinds[x + 1, at]
                    else:
                        high = post[step, x + 1, AT[COLS_UP[j]], at]
                        low = post[step, x + 1, AT[COLS_DOWN[j]], at]
                    up = jnp.where(lane == spot, pltpu.roll(high, spot + 1, 1), up)
                    down = jnp.where(lane == spot, pltpu.roll(low, spot, 1), down)
            to = pl.ds(pl.multiple_of(z * 8, 8), 8)
            cols_out[step, 0, to] = up
            cols_out[step, 1, to] = down
            return carry

        lax.fori_loop(0, 5, pack, 0, unroll=5)
        for side, there, to_y in ((0, gy < ny - 1, gy + 1), (1, gy > 0, gy - 1)):

            @pl.when(there)
            def _():
                for shift, to_x in ((-1, left), (0, gx), (1, right)):
                    remote(
                        cols_out.at[step, side],
                        cols_in.at[step, side, 1 - shift],
                        y_sem(step, side),
                        to_x,
                        to_y,
                    ).start()

    def wait_columns(step):
        for side, there in ((0, gy > 0), (1, gy < ny - 1)):

            @pl.when(there)
            def _():
                wait_bytes(cols_in.at[step, side], recv.at[y_sem(step, side)])

            def merge(z, carry):
                of = pl.ds(pl.multiple_of(z * 8, 8), 8)
                before = pltpu.roll(cols_in[step, side, 0, of], 126, 1)
                after = pltpu.roll(cols_in[step, side, 2, of], 2, 1)
                slot = lane % 4
                here = cols_in[step, side, 1, of]
                cols[side, pl.ds(pl.multiple_of(PAD + z * 8, 8), 8)] = jnp.where(
                    slot == 0, before, jnp.where(slot == 3, after, here)
                )
                return carry

            lax.fori_loop(0, 5, merge, 0, unroll=5)

    def shifted(value, step_y, j, slot, at, outside):
        if step_y == 0:
            return value
        if step_y == 1:
            edge = pltpu.roll(cols[0, at], 128 - (j * 4 + slot), 1)
            if outside is not None:
                edge = jnp.where(outside[0], -1.0, edge)
            return jnp.where(lane == 0, edge, pltpu.roll(value, 1, 1))
        edge = pltpu.roll(cols[1, at], 127 - (j * 4 + slot), 1)
        if outside is not None:
            edge = jnp.where(outside[1], -1.0, edge)
        return jnp.where(lane == 127, edge, pltpu.roll(value, 127, 1))

    def find_near(i, carry):
        x, z = i // 5, i % 5
        row = PAD + z * 8
        for d in range(1, 19):
            step_x, step_y, step_z = LATTICE[d]
            slot = x + 1 - step_x
            at = pl.ds(row - step_z, 8)
            near[d, i] = shifted(kinds[slot, at], step_y, 6, slot, at, (gy == 0, gy == ny - 1))
        return carry

    def twice_even(i):
        ux, uy, uz = speed[0, i], speed[1, i], speed[2, i]
        flat = 2.0 - 3.0 * (ux * ux + uy * uy + uz * uz)
        return [flat + 9.0 * (along * along) for along in pair_speeds(ux, uy, uz)]

    def stream(step, i):
        x, z = i // 5, i % 5
        row = PAD + z * 8
        own = pl.ds(pl.multiple_of(row, 8), 8)
        half = post[step, x + 1, AT[HALF], own]
        rest = post[step, x + 1, AT[0], own]
        waiting[0, i] = rest
        zero = jnp.zeros((8, 128), F32)
        rho_sum = [zero, zero]
        gas_sum = [zero, zero]
        gain_sum = [zero, zero]
        for k, ((a, b), even) in enumerate(zip(PAIRS, twice_even(i))):
            kind_of = 0 if k < 3 else 1
            here = {a: post[step, x + 1, AT[a], own], b: post[step, x + 1, AT[b], own]}
            for d, back in ((a, b), (b, a)):
                step_x, step_y, step_z = LATTICE[d]
                slot = x + 1 - step_x
                at = pl.ds(row - step_z, 8)
                j = 0 if step_y == 0 else (COLS_UP if step_y == 1 else COLS_DOWN).index(d)
                came = shifted(post[step, slot, AT[d], at], step_y, j, slot, at, None)
                near_half = shifted(post[step, slot, AT[HALF], at], step_y, 5, slot, at, None)
                kind = near[d, i]
                bounced = here[back]
                value = jnp.where(kind >= 1.0, came, bounced)
                gas = kind == 0.0
                known = jnp.where(gas, -bounced, value)
                waiting[d, i] = known
                rho_sum[kind_of] = rho_sum[kind_of] + known
                gas_sum[kind_of] = gas_sum[kind_of] + jnp.where(gas, even, 0.0)
                part_of = jnp.where(
                    kind == 2.0, 1.0, jnp.where(kind == 1.0, half + near_half, 0.0)
                )
                gain_sum[kind_of] = gain_sum[kind_of] + part_of * (value - bounced)
        base_rho[i] = (
            rest * (1.0 / 3.0) + rho_sum[0] * (1.0 / 18.0) + rho_sum[1] * (1.0 / 36.0)
        )
        gas_rho[i] = gas_sum[0] * (1.0 / 18.0) + gas_sum[1] * (1.0 / 36.0)
        gain[i] = gain_sum[0] * (1.0 / 18.0) + gain_sum[1] * (1.0 / 36.0)

    def arrived(i):
        density = gas_here[i]
        g = [waiting[0, i]] + [None] * 18
        for (a, b), even in zip(PAIRS, twice_even(i)):
            lift = density * even
            for d in (a, b):
                known = waiting[d, i]
                g[d] = jnp.where(near[d, i] == 0.0, known + lift, known)
        return g

    def lookup(table):
        def one(i, carry):
            gas_here[i] = jnp.take_along_axis(
                table, bubble[i], axis=1, mode="promise_in_bounds"
            )
            return carry

        lax.fori_loop(0, 10, one, 0, unroll=5)

    def member_sums():
        def one(b, carry):
            members[b] = jnp.sum(jnp.where(reversed_label[...] == b, share[...], 0.0), axis=0)
            return carry

        lax.fori_loop(0, BUBBLES, one, 0, unroll=8)
        now = members[...]
        for bit in range(6):
            half = now.shape[0] // 2
            first, second = now[:half], now[half:]
            odd = ((lax.broadcasted_iota(jnp.int32, first.shape, 2) >> bit) & 1) == 1
            keep = jnp.where(odd, second, first)
            move = jnp.where(odd, first, second)
            now = keep + pltpu.roll(move, 128 - (1 << bit), 2)
        now = now[0]
        return now + pltpu.roll(now, 64, 1)

    def begin_sum(step, value):
        part[step, 0] = jnp.sum(value, axis=0, keepdims=True)
        remote(part.at[step, 0], mate_sum.at[step], mate_sem(step), mate, gy).start()

    def middle_sum(step):
        wait_bytes(mate_sum.at[step], recv.at[mate_sem(step)])
        value = part[step, 0] + mate_sum[step]
        part[step, 1] = value
        mine = chip * ny + gy
        sums[step, mine] = value

        for dz, dx in far_chips:
            to_x = (at_x[dx] + at_z[dz]) * 2 + core
            for dy in far_first(ny):
                if dx == dy == dz == 0:
                    continue
                remote(
                    part.at[step, 1], sums.at[step, mine], all_sem(step), to_x, at_y[dy]
                ).start()

    def end_sum(step):
        wait_bytes(sums.at[step, pl.ds(0, chips * ny - 1)], recv.at[all_sem(step)])
        return jnp.broadcast_to(jnp.sum(sums[step], axis=0), (8, 128))

    def first(i, carry):
        rho = collide(0, i, [home[30 + q * 10 + i] for q in range(19)])
        kind = home[i]
        phi, part_gas = level(kind, fluid_mass[i], rho)
        put_half(0, i, phi)
        share[i] = part_gas
        return carry

    gathered(1)
    lax.fori_loop(0, 10, first, 0)
    pl.semaphore_wait(row_ready, ny - 1)
    faces = send_faces(0)
    send_columns(0)
    started = [faces]
    volume_start = member_sums()
    bubble_lane = lane & (BUBBLES - 1)
    table = jnp.zeros((8, 128), F32)
    for b in range(BUBBLES):
        table = jnp.where(bubble_lane == b, gas_density[b], table)
    density_start = table
    lookup(table)

    kinds_right.wait_recv()
    kinds_left.wait_recv()
    wait_columns(0)
    lax.fori_loop(0, 10, find_near, 0)
    for face in faces:
        face.wait_recv()

    def stream_all(step):
        def one(i, carry):
            stream(step, i)
            return carry

        lax.fori_loop(0, 10, one, 0)

    stream_all(0)
    start_total = None
    for step in range(ITERS):

        def settle(i, carry):
            kind = home[i]
            rho = base_rho[i] + gas_here[i] * gas_rho[i]
            liquid_mass = jnp.where(
                kind == 1.0, fluid_mass[i] + gain[i], jnp.where(kind == 2.0, rho, 0.0)
            )
            fluid_mass[i] = liquid_mass
            phi, part_gas = level(kind, liquid_mass, rho)
            if step < ITERS - 1:
                put_half(step + 1, i, phi)
            share[i] = part_gas
            return carry

        lax.fori_loop(0, 10, settle, 0, unroll=5)
        volume = member_sums()
        if step == 0:
            volume = jnp.where(lane < BUBBLES, volume, volume_start)
        begin_sum(step, volume)

        if step < ITERS - 1:

            def again(i, carry):
                collide(step + 1, i, arrived(i))
                return carry

            lax.fori_loop(0, 10, again, 0)
            faces = send_faces(step + 1)
            started.append(faces)
            middle_sum(step)
            send_columns(step + 1)
            wait_columns(step + 1)
            for face in faces:
                face.wait_recv()
            stream_all(step + 1)
        else:

            def last(i, carry):
                for q, value in enumerate(arrived(i)):
                    out_g[q * 10 + i] = value
                return carry

            lax.fori_loop(0, 10, last, 0)
            middle_sum(step)
        total = end_sum(step)
        if step == 0:
            other = pltpu.roll(total, 64, 1)
            start_total = jnp.where(lane < BUBBLES, other, total)
            total = jnp.where(lane < BUBBLES, total, other)
        lookup(density_start * start_total / total)

    def finish(i, carry):
        gas = home[i] == 0.0
        density = gas_here[i]
        for q in range(19):
            out_g[q * 10 + i] = jnp.where(gas, density, out_g[q * 10 + i])
        return carry

    lax.fori_loop(0, 10, finish, 0)
    out_m[...] = fluid_mass[...]
    out_v[...] = total * (BUBBLES / (ngx * ny * 2 * 40 * 128))

    for which in range(2):
        base, per, big, sides, got, pieces = chunks[which]
        for side, tiles in sides:

            @pl.when(core == side)
            def _():
                wait_bytes(stage.at[pl.ds(0, chips * per - tiles)], send.at[SPREAD + which])
                wait_bytes(
                    pieces.at[pl.ds(0, ngx - 1), pl.ds(0, tiles)], send.at[GATHER + which]
                )

    kinds_right.wait_send()
    kinds_left.wait_send()
    for step in range(ITERS):
        for face in started[step]:
            face.wait_send()
        for side, there in ((0, gy < ny - 1), (1, gy > 0)):

            @pl.when(there)
            def _():
                wait_bytes(cols_in.at[step, side], send.at[y_sem(step, side)])

        wait_bytes(mate_sum.at[step], send.at[mate_sem(step)])
        wait_bytes(sums.at[step, pl.ds(0, chips * ny - 1)], send.at[all_sem(step)])


def chunk_tiles(chips):
    per = -(-220 // chips)
    return (per * 4 + 6) // 7, per - (per * 4 + 6) // 7


def solution(mesh):
    ngx, ny = mesh.shape["gx"], mesh.shape["gy"]
    nx, nz = (4, 8) if ngx == 64 else (1, ngx // 2)
    chips = ngx // 2
    per_a, per_b = chunk_tiles(chips)
    big_a, big_b = (per_a + 1) // 2, (per_b + 1) // 2

    def per_device(populations, mass, cell_type, bubble_id, slab_source, gas_density):
        vmem = pl.BlockSpec(memory_space=pltpu.VMEM)
        hbm = pl.BlockSpec(memory_space=pltpu.HBM)

        def tiles(count, dtype=F32):
            return pltpu.VMEM((count, 8, 128), dtype)

        g, m, v = pl.pallas_call(
            functools.partial(kernel, (nx, nz, ny)),
            out_shape=(
                jax.ShapeDtypeStruct((190, 8, 128), F32),
                jax.ShapeDtypeStruct((10, 8, 128), F32),
                jax.ShapeDtypeStruct((8, 128), F32),
            ),
            in_specs=[hbm] * 6,
            out_specs=(vmem, vmem, vmem),
            scratch_shapes=[
                tiles(chips * (per_a + per_b) + 1),
                tiles(20, jnp.int32),
                pltpu.SMEM((ngx,), jnp.int32),
                pltpu.SMEM((BUBBLES,), F32),
                pltpu.VMEM((ngx, big_a, 8, 128), F32),
                pltpu.VMEM((ngx, big_b, 8, 128), F32),
                pltpu.VMEM((ngx, big_a, 8, 128), F32),
                pltpu.VMEM((ngx, big_b, 8, 128), F32),
                tiles(chips * (per_a + per_b)),
                pltpu.VMEM((ITERS, 4, 20, 56, 128), F32),
                pltpu.VMEM((4, 56, 128), F32),
                pltpu.VMEM((19, 10, 8, 128), F32),
                pltpu.VMEM((19, 10, 8, 128), F32),
                pltpu.VMEM((3, 10, 8, 128), F32),
                tiles(10, jnp.int32),
                tiles(10, jnp.int32),
                tiles(10),
                tiles(10),
                tiles(10),
                tiles(10),
                tiles(10),
                tiles(10),
                tiles(BUBBLES),
                pltpu.VMEM((ITERS, 2, 40, 128), F32),
                pltpu.VMEM((ITERS, 2, 3, 40, 128), F32),
                pltpu.VMEM((2, 56, 128), F32),
                pltpu.VMEM((ITERS, 1, 128), F32),
                pltpu.VMEM((ITERS, chips * ny, 1, 128), F32),
                pltpu.VMEM((ITERS, 2, 1, 128), F32),
                pltpu.SemaphoreType.DMA((6,)),
                pltpu.SemaphoreType.DMA((8 + ITERS * 8,)),
                pltpu.SemaphoreType.DMA((8 + ITERS * 8,)),
                pltpu.SemaphoreType.REGULAR,
            ],
            compiler_params=pltpu.CompilerParams(
                collective_id=0, has_side_effects=True, vmem_limit_bytes=40 * 2**20
            ),
        )(
            populations.reshape(190, 8, 128),
            mass.reshape(10, 8, 128),
            cell_type.reshape(10, 8, 128),
            bubble_id.reshape(10, 8, 128),
            slab_source,
            gas_density,
        )
        return g.reshape(populations.shape), m.reshape(mass.shape), v[0, :BUBBLES]

    return jax.shard_map(
        per_device,
        mesh=mesh,
        in_specs=(
            P(None, "gx", None, "gy"),
            P("gx", None, "gy"),
            P("gx", None, "gy"),
            P("gx", None, "gy"),
            P(),
            P(),
        ),
        out_specs=(P(None, "gx", None, "gy"), P("gx", None, "gy"), P()),
        check_vma=False,
    )
```

```python
import functools

import jax
import jax.numpy as jnp
from jax import lax
from jax.experimental import pallas as pl
from jax.experimental.pallas import tpu as pltpu
from jax.sharding import PartitionSpec as P

BUBBLES = 64
ITERS = 3
OMEGA = 1.6
VMEM_LIMIT = 56 * 2**20
MESH = pl.DeviceIdType.MESH
F32 = jnp.float32

LATTICE = (
    (0, 0, 0),
    (1, 0, 0),
    (-1, 0, 0),
    (0, 1, 0),
    (0, -1, 0),
    (0, 0, 1),
    (0, 0, -1),
    (1, 1, 0),
    (-1, -1, 0),
    (1, -1, 0),
    (-1, 1, 0),
    (1, 0, 1),
    (-1, 0, -1),
    (1, 0, -1),
    (-1, 0, 1),
    (0, 1, 1),
    (0, -1, -1),
    (0, 1, -1),
    (0, -1, 1),
)
HALF = 19
ORDER = (1, 7, 9, 11, 13, HALF, 2, 8, 10, 12, 14, 0, 3, 4, 5, 6, 15, 16, 17, 18)
AT = {field: pos for pos, field in enumerate(ORDER)}
COLS_UP = (3, 7, 10, 15, 17, HALF)
COLS_DOWN = (4, 8, 9, 16, 18, HALF)
PAIRS = ((1, 2), (3, 4), (5, 6), (7, 8), (9, 10), (11, 12), (13, 14), (15, 16), (17, 18))
PAD = 8


def pair_speeds(ux, uy, uz):
    return (ux, uy, uz, ux + uy, ux - uy, ux + uz, ux - uz, uy + uz, uy - uz)


def far_first(size):
    return sorted(range(size), key=lambda d: -min(d, size - d))


def kernel(
    shape,
    pop,
    mass,
    cell,
    label,
    source_in,
    density_in,
    out_g,
    out_m,
    out_v,
    stage,
    ints,
    source,
    gas_density,
    got_a,
    got_b,
    sorted_a,
    sorted_b,
    home,
    post,
    kinds,
    near,
    waiting,
    speed,
    bubble,
    reversed_label,
    fluid_mass,
    share,
    base_rho,
    gas_rho,
    gain,
    gas_here,
    members,
    cols_out,
    cols_in,
    cols,
    kind_cols_out,
    kind_cols_in,
    kind_cols,
    mate_sum,
    sums,
    part,
    fetch,
    send,
    recv,
    row_ready,
):
    nx, nz, ny = shape
    ngx = nx * nz * 2
    chips = nx * nz
    gx = lax.axis_index("gx")
    gy = lax.axis_index("gy")
    core = gx % 2
    chip = gx // 2
    pos_x = chip // nz
    pos_z = chip % nz
    mate = gx + 1 - 2 * core
    right = (gx + 1) % ngx
    left = (gx + ngx - 1) % ngx
    lane = lax.broadcasted_iota(jnp.int32, (8, 128), 1)

    SPREAD, GATHER, KINDS = 0, 2, 4

    def x_sem(step, side):
        return 8 + step * 8 + side

    def y_sem(step, side):
        return 8 + step * 8 + 2 + side

    def mate_sem(step):
        return 8 + step * 8 + 4

    def all_sem(step):
        return 8 + step * 8 + 5

    def remote(src, dst, sem, to_x, to_y):
        return pltpu.make_async_remote_copy(
            src_ref=src,
            dst_ref=dst,
            send_sem=send.at[sem],
            recv_sem=recv.at[sem],
            device_id=(to_x, to_y),
            device_id_type=MESH,
        )

    def wait_bytes(ref, sem):
        pltpu.make_async_copy(ref, ref, sem).wait()

    at_x = [lax.rem(pos_x + d, nx) * nz for d in range(nx)]
    at_z = [lax.rem(pos_z + d, nz) for d in range(nz)]
    at_y = [lax.rem(gy + d, ny) for d in range(ny)]
    far_chips = [(dz, dx) for dz in far_first(nz) for dx in far_first(nx)]
    peers = [
        (at_x[dx] + at_z[dz], other, dx == dz == 0 and other is core)
        for dz, dx in far_chips
        for other in (1 - core, core)
    ]

    def send_columns(out, into, sem, up_fields, down_fields):
        for z in range(5):
            up = jnp.zeros((8, 128), F32)
            down = jnp.zeros((8, 128), F32)
            for j, (high, low) in enumerate(zip(up_fields, down_fields)):
                for x in range(2):
                    spot = j * 4 + x + 1
                    at = pl.ds(PAD + z * 8, 8)
                    up = jnp.where(lane == spot, pltpu.roll(high(x + 1, at), spot + 1, 1), up)
                    down = jnp.where(lane == spot, pltpu.roll(low(x + 1, at), spot, 1), down)
            out[0, z * 8 : z * 8 + 8] = up
            out[1, z * 8 : z * 8 + 8] = down
        for side, there, to_y in ((0, gy < ny - 1, gy + 1), (1, gy > 0, gy - 1)):

            @pl.when(there)
            def _():
                for shift, to_x in ((-1, left), (0, gx), (1, right)):
                    remote(out.at[side], into.at[side, 1 - shift], sem + side, to_x, to_y).start()

    def wait_columns(into, whole, sem):
        for side, there in ((0, gy > 0), (1, gy < ny - 1)):

            @pl.when(there)
            def _():
                wait_bytes(into.at[side], recv.at[sem + side])

        slot = lane % 4
        for side in range(2):
            for z in range(5):
                of = pl.ds(z * 8, 8)
                before = pltpu.roll(into[side, 0, of], 126, 1)
                after = pltpu.roll(into[side, 2, of], 2, 1)
                whole[side, PAD + z * 8 : PAD + z * 8 + 8] = jnp.where(
                    slot == 0, before, jnp.where(slot == 3, after, into[side, 1, of])
                )

    def columns_sent(into, sem):
        for side, there in ((0, gy < ny - 1), (1, gy > 0)):

            @pl.when(there)
            def _():
                wait_bytes(into.at[side], send.at[sem + side])

    def post_columns(step):
        def fields(order):
            return [
                lambda slot, at, f=f: post[step, slot, AT[f], at] for f in order
            ]

        send_columns(
            cols_out.at[step], cols_in.at[step], y_sem(step, 0), fields(COLS_UP), fields(COLS_DOWN)
        )

    fetches = [
        pltpu.make_async_copy(src, dst, fetch.at[k])
        for k, (src, dst) in enumerate(
            (
                (cell, ints.at[0:10]),
                (label, ints.at[10:20]),
                (pop, stage.at[30:220]),
                (mass, stage.at[20:30]),
                (source_in, source),
                (density_in, gas_density),
            )
        )
    ]
    for one in fetches:
        one.start()

    barrier = pltpu.get_barrier_semaphore()

    for to_chip, to_core, near_by in peers:
        if not near_by:
            pl.semaphore_signal(
                barrier, inc=1, device_id=(to_chip * 2 + to_core, gy), device_id_type=MESH
            )
    for k in range(1, ny):
        pl.semaphore_signal(
            barrier, inc=1, device_id=(gx, (gy + k) % ny), device_id_type=MESH
        )

    walls = jnp.full((PAD, 128), -1.0, F32)
    for slot in range(4):
        kinds[slot, 0:PAD] = walls
        kinds[slot, PAD + 40 : PAD + 48] = walls
    for side in range(2):
        for edge in (cols, kind_cols):
            edge[side, 0:PAD] = walls
            edge[side, PAD + 40 : PAD + 48] = walls
    for one in fetches:
        one.wait()
    stage[0:20] = ints[...].astype(F32)
    pl.semaphore_wait(barrier, ngx - 1 + ny - 1)
    for k in range(1, ny):
        pl.semaphore_signal(
            row_ready, inc=1, device_id=(gx, (gy + k) % ny), device_id_type=MESH
        )

    chunks = []
    base = 0
    for per, got, pieces in zip(chunk_tiles(chips), (got_a, got_b), (sorted_a, sorted_b)):
        big = (per + 1) // 2
        chunks.append((base, per, big, ((0, big), (1, per - big)), got, pieces))
        base += per * chips

    def spread(which):
        base, per, big, sides, got, pieces = chunks[which]

        for own, _ in sides:

            @pl.when(core == own)
            def _():
                for dz, dx in far_chips:
                    to = at_x[dx] + at_z[dz]
                    for side, tiles in sides:
                        if dx == dz == 0 and side == own:
                            continue
                        remote(
                            stage.at[pl.ds(base + to * per + side * big, tiles)],
                            got.at[gx, pl.ds(0, tiles)],
                            SPREAD + which,
                            to * 2 + side,
                            gy,
                        ).start()

        got[gx] = stage[pl.ds(base + chip * per + core * big, big)]

    def pick(which):
        base, per, big, sides, got, pieces = chunks[which]
        for side, tiles in sides:

            @pl.when(core == side)
            def _():
                wait_bytes(got.at[pl.ds(0, ngx - 1), pl.ds(0, tiles)], recv.at[SPREAD + which])

        def one(k, carry):
            pieces[k] = got[source[k]]
            return carry

        lax.fori_loop(0, ngx, one, 0, unroll=8)

    def gather(which):
        base, per, big, sides, got, pieces = chunks[which]
        for side, tiles in sides:

            @pl.when(core == side)
            def _():
                at = pl.ds(base + chip * per + side * big, tiles)

                for dz, dx in far_chips:
                    for other in range(2):
                        if dx == dz == 0 and side == other:
                            continue
                        peer = (at_x[dx] + at_z[dz]) * 2 + other
                        remote(
                            pieces.at[peer, pl.ds(0, tiles)],
                            home.at[at],
                            GATHER + which,
                            peer,
                            gy,
                        ).start()
                home[at] = pieces[gx, 0:tiles]

    def gathered(which):
        base, per, big, sides, got, pieces = chunks[which]
        for side, tiles in sides:

            @pl.when(core == side)
            def _():
                wait_bytes(
                    home.at[pl.ds(base, chips * per - tiles)], recv.at[GATHER + which]
                )

    spread(0)
    spread(1)
    pick(0)
    gather(0)
    pick(1)
    gather(1)

    gathered(0)
    for x in range(2):
        for z in range(5):
            kinds[x + 1, PAD + z * 8 : PAD + z * 8 + 8] = home[x * 5 + z]
    rows = pl.ds(PAD, 40)
    kinds_right = remote(kinds.at[2, rows], kinds.at[0, rows], KINDS, right, gy)
    kinds_left = remote(kinds.at[1, rows], kinds.at[3, rows], KINDS + 1, left, gy)
    kinds_right.start()
    kinds_left.start()
    pl.semaphore_wait(row_ready, ny - 1)
    kind_fields = [lambda slot, at: kinds[slot, at]]
    send_columns(kind_cols_out, kind_cols_in, KINDS + 2, kind_fields, kind_fields)
    label_now = home[10:20].astype(jnp.int32)
    bubble[...] = label_now
    turned = jnp.zeros_like(label_now)
    for bit in range(6):
        turned = turned | (((label_now >> bit) & 1) << (5 - bit))
    reversed_label[...] = turned
    fluid_mass[...] = home[20:30]

    def collide(step, i, g):
        x, z = i // 5, i % 5
        diff = [g[a] - g[b] for a, b in PAIRS]
        total = [g[a] + g[b] for a, b in PAIRS]
        faces = total[0] + total[1] + total[2]
        edges = (total[3] + total[4]) + (total[5] + total[6]) + (total[7] + total[8])
        rho = g[0] * (1.0 / 3.0) + faces * (1.0 / 18.0) + edges * (1.0 / 36.0)
        inv = 1.0 / rho
        ux = (diff[0] * (1.0 / 18.0) + (diff[3] + diff[4] + diff[5] + diff[6]) * (1.0 / 36.0)) * inv
        uy = (diff[1] * (1.0 / 18.0) + (diff[3] - diff[4] + diff[7] + diff[8]) * (1.0 / 36.0)) * inv
        uz = (diff[2] * (1.0 / 18.0) + (diff[5] - diff[6] + diff[7] - diff[8]) * (1.0 / 36.0)) * inv
        speed[0, i] = ux
        speed[1, i] = uy
        speed[2, i] = uz
        scaled = OMEGA * rho
        flat = scaled * (1.0 - 1.5 * (ux * ux + uy * uy + uz * uz))
        at = pl.ds(pl.multiple_of(PAD + z * 8, 8), 8)
        post[step, x + 1, AT[0], at] = flat + (1.0 - OMEGA) * g[0]
        square = 4.5 * scaled
        line = 3.0 * scaled
        for (a, b), along in zip(PAIRS, pair_speeds(ux, uy, uz)):
            even = flat + square * (along * along)
            odd = line * along
            post[step, x + 1, AT[a], at] = even + odd + (1.0 - OMEGA) * g[a]
            post[step, x + 1, AT[b], at] = even - odd + (1.0 - OMEGA) * g[b]
        return rho

    def put_half(step, i, value):
        x, z = i // 5, i % 5
        post[step, x + 1, AT[HALF], pl.ds(pl.multiple_of(PAD + z * 8, 8), 8)] = 0.5 * value

    def level(kind, liquid_mass, rho):
        phi = jnp.where(kind == 2.0, 1.0, jnp.where(kind == 1.0, liquid_mass / rho, 0.0))
        part_gas = jnp.where(kind == 0.0, 1.0, jnp.where(kind == 1.0, 1.0 - phi, 0.0))
        return phi, part_gas

    def send_faces(step):
        plus = remote(
            post.at[step, 2, pl.ds(0, 6), rows],
            post.at[step, 0, pl.ds(0, 6), rows],
            x_sem(step, 0),
            right,
            gy,
        )
        minus = remote(
            post.at[step, 1, pl.ds(5, 6), rows],
            post.at[step, 3, pl.ds(5, 6), rows],
            x_sem(step, 1),
            left,
            gy,
        )
        plus.start()
        minus.start()
        return plus, minus

    def shifted(value, cols, step_y, j, slot, at, outside):
        if step_y == 0:
            return value
        if step_y == 1:
            edge = pltpu.roll(cols[0, at], 128 - (j * 4 + slot), 1)
            if outside is not None:
                edge = jnp.where(outside[0], -1.0, edge)
            return jnp.where(lane == 0, edge, pltpu.roll(value, 1, 1))
        edge = pltpu.roll(cols[1, at], 127 - (j * 4 + slot), 1)
        if outside is not None:
            edge = jnp.where(outside[1], -1.0, edge)
        return jnp.where(lane == 127, edge, pltpu.roll(value, 127, 1))

    def find_near(i, carry):
        x, z = i // 5, i % 5
        row = PAD + z * 8
        for d in range(1, 19):
            step_x, step_y, step_z = LATTICE[d]
            slot = x + 1 - step_x
            at = pl.ds(row - step_z, 8)
            near[d, i] = shifted(
                kinds[slot, at], kind_cols, step_y, 0, slot, at, (gy == 0, gy == ny - 1)
            )
        return carry

    def twice_even(i):
        ux, uy, uz = speed[0, i], speed[1, i], speed[2, i]
        flat = 2.0 - 3.0 * (ux * ux + uy * uy + uz * uz)
        return [flat + 9.0 * (along * along) for along in pair_speeds(ux, uy, uz)]

    def stream(step, i):
        x, z = i // 5, i % 5
        row = PAD + z * 8
        own = pl.ds(pl.multiple_of(row, 8), 8)
        half = post[step, x + 1, AT[HALF], own]
        rest = post[step, x + 1, AT[0], own]
        waiting[0, i] = rest
        zero = jnp.zeros((8, 128), F32)
        rho_sum = [zero, zero]
        gas_sum = [zero, zero]
        gain_sum = [zero, zero]
        for k, ((a, b), even) in enumerate(zip(PAIRS, twice_even(i))):
            kind_of = 0 if k < 3 else 1
            here = {a: post[step, x + 1, AT[a], own], b: post[step, x + 1, AT[b], own]}
            for d, back in ((a, b), (b, a)):
                step_x, step_y, step_z = LATTICE[d]
                slot = x + 1 - step_x
                at = pl.ds(row - step_z, 8)
                j = 0 if step_y == 0 else (COLS_UP if step_y == 1 else COLS_DOWN).index(d)
                came = shifted(post[step, slot, AT[d], at], cols, step_y, j, slot, at, None)
                near_half = shifted(post[step, slot, AT[HALF], at], cols, step_y, 5, slot, at, None)
                kind = near[d, i]
                bounced = here[back]
                value = jnp.where(kind >= 1.0, came, bounced)
                gas = kind == 0.0
                known = jnp.where(gas, -bounced, value)
                waiting[d, i] = known
                rho_sum[kind_of] = rho_sum[kind_of] + known
                gas_sum[kind_of] = gas_sum[kind_of] + jnp.where(gas, even, 0.0)
                part_of = jnp.where(
                    kind == 2.0, 1.0, jnp.where(kind == 1.0, half + near_half, 0.0)
                )
                gain_sum[kind_of] = gain_sum[kind_of] + part_of * (value - bounced)
        base_rho[i] = (
            rest * (1.0 / 3.0) + rho_sum[0] * (1.0 / 18.0) + rho_sum[1] * (1.0 / 36.0)
        )
        gas_rho[i] = gas_sum[0] * (1.0 / 18.0) + gas_sum[1] * (1.0 / 36.0)
        gain[i] = gain_sum[0] * (1.0 / 18.0) + gain_sum[1] * (1.0 / 36.0)

    def arrived(i):
        density = gas_here[i]
        g = [waiting[0, i]] + [None] * 18
        for (a, b), even in zip(PAIRS, twice_even(i)):
            lift = density * even
            for d in (a, b):
                known = waiting[d, i]
                g[d] = jnp.where(near[d, i] == 0.0, known + lift, known)
        return g

    def lookup(table):
        def one(i, carry):
            gas_here[i] = jnp.take_along_axis(
                table, bubble[i], axis=1, mode="promise_in_bounds"
            )
            return carry

        lax.fori_loop(0, 10, one, 0, unroll=5)

    def member_sums():
        labels = [reversed_label[i] for i in range(10)]
        shares = [share[i] for i in range(10)]

        def one(b, carry):
            parts = [jnp.where(which == b, part_of, 0.0) for which, part_of in zip(labels, shares)]
            while len(parts) > 1:
                parts = [sum(parts[k : k + 2]) for k in range(0, len(parts), 2)]
            members[b] = parts[0]
            return carry

        lax.fori_loop(0, BUBBLES, one, 0, unroll=8)
        now = members[...]
        for bit in range(6):
            half = now.shape[0] // 2
            first, second = now[:half], now[half:]
            odd = ((lax.broadcasted_iota(jnp.int32, first.shape, 2) >> bit) & 1) == 1
            keep = jnp.where(odd, second, first)
            move = jnp.where(odd, first, second)
            now = keep + pltpu.roll(move, 128 - (1 << bit), 2)
        now = now[0]
        return now + pltpu.roll(now, 64, 1)

    def begin_sum(step, value):
        part[step, 0] = jnp.sum(value, axis=0, keepdims=True)
        remote(part.at[step, 0], mate_sum.at[step], mate_sem(step), mate, gy).start()

    def middle_sum(step):
        wait_bytes(mate_sum.at[step], recv.at[mate_sem(step)])
        value = part[step, 0] + mate_sum[step]
        part[step, 1] = value
        mine = chip * ny + gy
        sums[step, mine] = value

        for dz, dx in far_chips:
            to_x = (at_x[dx] + at_z[dz]) * 2 + core
            for dy in far_first(ny):
                if dx == dy == dz == 0:
                    continue
                remote(
                    part.at[step, 1], sums.at[step, mine], all_sem(step), to_x, at_y[dy]
                ).start()

    def end_sum(step):
        wait_bytes(sums.at[step, pl.ds(0, chips * ny - 1)], recv.at[all_sem(step)])
        return jnp.broadcast_to(jnp.sum(sums[step], axis=0), (8, 128))

    def first(i, carry):
        rho = collide(0, i, [home[30 + q * 10 + i] for q in range(19)])
        kind = home[i]
        phi, part_gas = level(kind, fluid_mass[i], rho)
        put_half(0, i, phi)
        share[i] = part_gas
        return carry

    bubble_lane = lane & (BUBBLES - 1)
    table = jnp.zeros((8, 128), F32)
    for b in range(BUBBLES):
        table = jnp.where(bubble_lane == b, gas_density[b], table)
    density_start = table
    lookup(table)

    gathered(1)
    lax.fori_loop(0, 10, first, 0)
    faces = send_faces(0)
    post_columns(0)
    started = [faces]
    kinds_right.wait_recv()
    kinds_left.wait_recv()
    wait_columns(kind_cols_in, kind_cols, KINDS + 2)
    lax.fori_loop(0, 10, find_near, 0)
    volume_start = member_sums()
    wait_columns(cols_in.at[0], cols, y_sem(0, 0))
    for face in faces:
        face.wait_recv()

    def stream_all(step):
        def one(i, carry):
            stream(step, i)
            return carry

        lax.fori_loop(0, 10, one, 0)

    stream_all(0)
    start_total = None
    for step in range(ITERS):

        def settle(i, carry):
            kind = home[i]
            rho = base_rho[i] + gas_here[i] * gas_rho[i]
            liquid_mass = jnp.where(
                kind == 1.0, fluid_mass[i] + gain[i], jnp.where(kind == 2.0, rho, 0.0)
            )
            fluid_mass[i] = liquid_mass
            phi, part_gas = level(kind, liquid_mass, rho)
            if step < ITERS - 1:
                put_half(step + 1, i, phi)
            share[i] = part_gas
            return carry

        lax.fori_loop(0, 10, settle, 0, unroll=5)
        volume = member_sums()
        if step == 0:
            volume = jnp.where(lane < BUBBLES, volume, volume_start)
        begin_sum(step, volume)

        if step < ITERS - 1:

            def again(i, carry):
                collide(step + 1, i, arrived(i))
                return carry

            lax.fori_loop(0, 10, again, 0)
            faces = send_faces(step + 1)
            started.append(faces)
            middle_sum(step)
            post_columns(step + 1)
            wait_columns(cols_in.at[step + 1], cols, y_sem(step + 1, 0))
            for face in faces:
                face.wait_recv()
            stream_all(step + 1)
        else:

            def last(i, carry):
                for q, value in enumerate(arrived(i)):
                    out_g[q * 10 + i] = value
                return carry

            lax.fori_loop(0, 10, last, 0)
            middle_sum(step)
        total = end_sum(step)
        if step == 0:
            other = pltpu.roll(total, 64, 1)
            start_total = jnp.where(lane < BUBBLES, other, total)
            total = jnp.where(lane < BUBBLES, total, other)
        lookup(density_start * start_total / total)

    def finish(i, carry):
        gas = home[i] == 0.0
        density = gas_here[i]
        for q in range(19):
            out_g[q * 10 + i] = jnp.where(gas, density, out_g[q * 10 + i])
        return carry

    lax.fori_loop(0, 10, finish, 0)
    out_m[...] = fluid_mass[...]
    out_v[...] = total[0:1, :BUBBLES] * (BUBBLES / (ngx * ny * 2 * 40 * 128))

    for which in range(2):
        base, per, big, sides, got, pieces = chunks[which]
        for side, tiles in sides:

            @pl.when(core == side)
            def _():
                wait_bytes(stage.at[pl.ds(0, chips * per - tiles)], send.at[SPREAD + which])
                wait_bytes(
                    pieces.at[pl.ds(0, ngx - 1), pl.ds(0, tiles)], send.at[GATHER + which]
                )

    kinds_right.wait_send()
    kinds_left.wait_send()
    columns_sent(kind_cols_in, KINDS + 2)
    for step in range(ITERS):
        for face in started[step]:
            face.wait_send()
        columns_sent(cols_in.at[step], y_sem(step, 0))
        wait_bytes(mate_sum.at[step], send.at[mate_sem(step)])
        wait_bytes(sums.at[step, pl.ds(0, chips * ny - 1)], send.at[all_sem(step)])


def hand_over(g, m, v, out_g, out_m, out_v, held_g, held_m, held_v, sem):
    parts = [
        (g.at[pl.ds(k * 38, 38)], held_g.at[pl.ds(k * 38, 38)], out_g.at[pl.ds(k * 38, 38)])
        for k in range(5)
    ]
    parts.append((m, held_m, out_m))
    parts.append((v, held_v, out_v))
    inward = [pltpu.make_async_copy(p[0], p[1], sem.at[0, k]) for k, p in enumerate(parts)]
    outward = [pltpu.make_async_copy(p[1], p[2], sem.at[1, k]) for k, p in enumerate(parts)]
    for one in inward:
        one.start()
    for one, other in zip(inward, outward):
        one.wait()
        other.start()
    for one in outward:
        one.wait()


def chunk_tiles(chips):
    per = -(-220 // chips)
    return (per * 4 + 6) // 7, per - (per * 4 + 6) // 7


def solution(mesh):
    ngx, ny = mesh.shape["gx"], mesh.shape["gy"]
    nx, nz = (4, 8) if ngx == 64 else (1, ngx // 2)
    chips = ngx // 2
    per_a, per_b = chunk_tiles(chips)
    big_a, big_b = (per_a + 1) // 2, (per_b + 1) // 2

    def per_device(populations, mass, cell_type, bubble_id, slab_source, gas_density):
        vmem = pl.BlockSpec(memory_space=pltpu.VMEM)
        hbm = pl.BlockSpec(memory_space=pltpu.HBM)

        def tiles(count, dtype=F32):
            return pltpu.VMEM((count, 8, 128), dtype)

        g, m, v = pl.pallas_call(
            functools.partial(kernel, (nx, nz, ny)),
            out_shape=(
                jax.ShapeDtypeStruct((190, 8, 128), F32),
                jax.ShapeDtypeStruct((10, 8, 128), F32),
                jax.ShapeDtypeStruct((1, BUBBLES), F32),
            ),
            in_specs=[hbm] * 6,
            out_specs=(vmem, vmem, vmem),
            scratch_shapes=[
                tiles(chips * (per_a + per_b) + 1),
                tiles(20, jnp.int32),
                pltpu.SMEM((ngx,), jnp.int32),
                pltpu.SMEM((BUBBLES,), F32),
                pltpu.VMEM((ngx, big_a, 8, 128), F32),
                pltpu.VMEM((ngx, big_b, 8, 128), F32),
                pltpu.VMEM((ngx, big_a, 8, 128), F32),
                pltpu.VMEM((ngx, big_b, 8, 128), F32),
                tiles(chips * (per_a + per_b)),
                pltpu.VMEM((ITERS, 4, 20, 56, 128), F32),
                pltpu.VMEM((4, 56, 128), F32),
                pltpu.VMEM((19, 10, 8, 128), F32),
                pltpu.VMEM((19, 10, 8, 128), F32),
                pltpu.VMEM((3, 10, 8, 128), F32),
                tiles(10, jnp.int32),
                tiles(10, jnp.int32),
                tiles(10),
                tiles(10),
                tiles(10),
                tiles(10),
                tiles(10),
                tiles(10),
                tiles(BUBBLES),
                pltpu.VMEM((ITERS, 2, 40, 128), F32),
                pltpu.VMEM((ITERS, 2, 3, 40, 128), F32),
                pltpu.VMEM((2, 56, 128), F32),
                pltpu.VMEM((2, 40, 128), F32),
                pltpu.VMEM((2, 3, 40, 128), F32),
                pltpu.VMEM((2, 56, 128), F32),
                pltpu.VMEM((ITERS, 1, 128), F32),
                pltpu.VMEM((ITERS, chips * ny, 1, 128), F32),
                pltpu.VMEM((ITERS, 2, 1, 128), F32),
                pltpu.SemaphoreType.DMA((6,)),
                pltpu.SemaphoreType.DMA((8 + ITERS * 8,)),
                pltpu.SemaphoreType.DMA((8 + ITERS * 8,)),
                pltpu.SemaphoreType.REGULAR,
            ],
            compiler_params=pltpu.CompilerParams(
                collective_id=0, has_side_effects=True, vmem_limit_bytes=VMEM_LIMIT
            ),
        )(
            populations.reshape(190, 8, 128),
            mass.reshape(10, 8, 128),
            cell_type.reshape(10, 8, 128),
            bubble_id.reshape(10, 8, 128),
            slab_source,
            gas_density,
        )
        anywhere = pl.BlockSpec(memory_space=pl.ANY)
        g, m, v = pl.pallas_call(
            hand_over,
            out_shape=(
                jax.ShapeDtypeStruct((190, 8, 128), F32),
                jax.ShapeDtypeStruct((10, 8, 128), F32),
                jax.ShapeDtypeStruct((1, BUBBLES), F32),
            ),
            in_specs=[anywhere] * 3,
            out_specs=(hbm, hbm, hbm),
            scratch_shapes=[
                tiles(190),
                tiles(10),
                pltpu.VMEM((1, BUBBLES), F32),
                pltpu.SemaphoreType.DMA((2, 7)),
            ],
            compiler_params=pltpu.CompilerParams(vmem_limit_bytes=VMEM_LIMIT),
        )(g, m, v)
        return g.reshape(populations.shape), m.reshape(mass.shape), v.reshape(BUBBLES)

    return jax.shard_map(
        per_device,
        mesh=mesh,
        in_specs=(
            P(None, "gx", None, "gy"),
            P("gx", None, "gy"),
            P("gx", None, "gy"),
            P("gx", None, "gy"),
            P(),
            P(),
        ),
        out_specs=(P(None, "gx", None, "gy"), P("gx", None, "gy"), P()),
        check_vma=False,
    )
```

```python
import functools

import jax
import jax.numpy as jnp
from jax import lax
from jax.experimental import pallas as pl
from jax.experimental.pallas import tpu as pltpu
from jax.sharding import PartitionSpec as P

BUBBLES = 64
ITERS = 3
OMEGA = 1.6
VMEM_LIMIT = 56 * 2**20
MESH = pl.DeviceIdType.MESH
F32 = jnp.float32

LATTICE = (
    (0, 0, 0),
    (1, 0, 0),
    (-1, 0, 0),
    (0, 1, 0),
    (0, -1, 0),
    (0, 0, 1),
    (0, 0, -1),
    (1, 1, 0),
    (-1, -1, 0),
    (1, -1, 0),
    (-1, 1, 0),
    (1, 0, 1),
    (-1, 0, -1),
    (1, 0, -1),
    (-1, 0, 1),
    (0, 1, 1),
    (0, -1, -1),
    (0, 1, -1),
    (0, -1, 1),
)
HALF = 19
ORDER = (1, 7, 9, 11, 13, HALF, 2, 8, 10, 12, 14, 0, 3, 4, 5, 6, 15, 16, 17, 18)
AT = {field: pos for pos, field in enumerate(ORDER)}
COLS_UP = (3, 7, 10, 15, 17, HALF)
COLS_DOWN = (4, 8, 9, 16, 18, HALF)
PAIRS = ((1, 2), (3, 4), (5, 6), (7, 8), (9, 10), (11, 12), (13, 14), (15, 16), (17, 18))
PAD = 8


def pair_speeds(ux, uy, uz):
    return (ux, uy, uz, ux + uy, ux - uy, ux + uz, ux - uz, uy + uz, uy - uz)


def far_first(size):
    return sorted(range(size), key=lambda d: -min(d, size - d))


def kernel(
    shape,
    pop,
    mass,
    cell,
    label,
    source_in,
    density_in,
    out_g,
    out_m,
    out_v,
    stage,
    ints,
    source,
    gas_density,
    got_a,
    got_b,
    sorted_a,
    sorted_b,
    home,
    post,
    kinds,
    near,
    waiting,
    speed,
    bubble,
    fluid_mass,
    share,
    base_rho,
    gas_rho,
    gain,
    gas_here,
    cols_out,
    cols_in,
    cols,
    kind_cols_out,
    kind_cols_in,
    kind_cols,
    mate_sum,
    sums,
    part,
    fetch,
    send,
    recv,
    row_ready,
):
    nx, nz, ny = shape
    ngx = nx * nz * 2
    chips = nx * nz
    gx = lax.axis_index("gx")
    gy = lax.axis_index("gy")
    core = gx % 2
    chip = gx // 2
    pos_x = chip // nz
    pos_z = chip % nz
    mate = gx + 1 - 2 * core
    right = (gx + 1) % ngx
    left = (gx + ngx - 1) % ngx
    lane = lax.broadcasted_iota(jnp.int32, (8, 128), 1)

    SPREAD, GATHER, KINDS = 0, 2, 4

    def x_sem(step, side):
        return 8 + step * 8 + side

    def y_sem(step, side):
        return 8 + step * 8 + 2 + side

    def mate_sem(step):
        return 8 + step * 8 + 4

    def all_sem(step):
        return 8 + step * 8 + 5

    def remote(src, dst, sem, to_x, to_y):
        return pltpu.make_async_remote_copy(
            src_ref=src,
            dst_ref=dst,
            send_sem=send.at[sem],
            recv_sem=recv.at[sem],
            device_id=(to_x, to_y),
            device_id_type=MESH,
        )

    def wait_bytes(ref, sem):
        pltpu.make_async_copy(ref, ref, sem).wait()

    at_x = [lax.rem(pos_x + d, nx) * nz for d in range(nx)]
    at_z = [lax.rem(pos_z + d, nz) for d in range(nz)]
    at_y = [lax.rem(gy + d, ny) for d in range(ny)]
    far_chips = [(dz, dx) for dz in far_first(nz) for dx in far_first(nx)]
    peers = [
        (at_x[dx] + at_z[dz], other, dx == dz == 0 and other is core)
        for dz, dx in far_chips
        for other in (1 - core, core)
    ]

    def send_columns(out, into, sem, up_fields, down_fields):
        for z in range(5):
            up = jnp.zeros((8, 128), F32)
            down = jnp.zeros((8, 128), F32)
            for j, (high, low) in enumerate(zip(up_fields, down_fields)):
                for x in range(2):
                    spot = j * 4 + x + 1
                    at = pl.ds(PAD + z * 8, 8)
                    up = jnp.where(lane == spot, pltpu.roll(high(x + 1, at), spot + 1, 1), up)
                    down = jnp.where(lane == spot, pltpu.roll(low(x + 1, at), spot, 1), down)
            out[0, z * 8 : z * 8 + 8] = up
            out[1, z * 8 : z * 8 + 8] = down
        for side, there, to_y in ((0, gy < ny - 1, gy + 1), (1, gy > 0, gy - 1)):

            @pl.when(there)
            def _():
                for shift, to_x in ((-1, left), (0, gx), (1, right)):
                    remote(out.at[side], into.at[side, 1 - shift], sem + side, to_x, to_y).start()

    def wait_columns(into, whole, sem):
        for side, there in ((0, gy > 0), (1, gy < ny - 1)):

            @pl.when(there)
            def _():
                wait_bytes(into.at[side], recv.at[sem + side])

        slot = lane % 4
        for side in range(2):
            for z in range(5):
                of = pl.ds(z * 8, 8)
                before = pltpu.roll(into[side, 0, of], 126, 1)
                after = pltpu.roll(into[side, 2, of], 2, 1)
                whole[side, PAD + z * 8 : PAD + z * 8 + 8] = jnp.where(
                    slot == 0, before, jnp.where(slot == 3, after, into[side, 1, of])
                )

    def columns_sent(into, sem):
        for side, there in ((0, gy < ny - 1), (1, gy > 0)):

            @pl.when(there)
            def _():
                wait_bytes(into.at[side], send.at[sem + side])

    def post_columns(step):
        def fields(order):
            return [
                lambda slot, at, f=f: post[step, slot, AT[f], at] for f in order
            ]

        send_columns(
            cols_out.at[step], cols_in.at[step], y_sem(step, 0), fields(COLS_UP), fields(COLS_DOWN)
        )

    fetches = [
        pltpu.make_async_copy(src, dst, fetch.at[k])
        for k, (src, dst) in enumerate(
            (
                (cell, ints.at[0:10]),
                (label, ints.at[10:20]),
                (pop, stage.at[30:220]),
                (mass, stage.at[20:30]),
                (source_in, source),
                (density_in, gas_density),
            )
        )
    ]
    for one in fetches:
        one.start()

    barrier = pltpu.get_barrier_semaphore()

    for to_chip, to_core, near_by in peers:
        if not near_by:
            pl.semaphore_signal(
                barrier, inc=1, device_id=(to_chip * 2 + to_core, gy), device_id_type=MESH
            )
    for k in range(1, ny):
        pl.semaphore_signal(
            barrier, inc=1, device_id=(gx, (gy + k) % ny), device_id_type=MESH
        )

    walls = jnp.full((PAD, 128), -1.0, F32)
    for slot in range(4):
        kinds[slot, 0:PAD] = walls
        kinds[slot, PAD + 40 : PAD + 48] = walls
    for side in range(2):
        for edge in (cols, kind_cols):
            edge[side, 0:PAD] = walls
            edge[side, PAD + 40 : PAD + 48] = walls
    for one in fetches:
        one.wait()
    stage[0:20] = ints[...].astype(F32)
    pl.semaphore_wait(barrier, ngx - 1 + ny - 1)
    for k in range(1, ny):
        pl.semaphore_signal(
            row_ready, inc=1, device_id=(gx, (gy + k) % ny), device_id_type=MESH
        )

    chunks = []
    base = 0
    for per, got, pieces in zip(chunk_tiles(chips), (got_a, got_b), (sorted_a, sorted_b)):
        big = (per + 1) // 2
        chunks.append((base, per, big, ((0, big), (1, per - big)), got, pieces))
        base += per * chips

    def spread(which):
        base, per, big, sides, got, pieces = chunks[which]

        for own, _ in sides:

            @pl.when(core == own)
            def _():
                for dz, dx in far_chips:
                    to = at_x[dx] + at_z[dz]
                    for side, tiles in sides:
                        if dx == dz == 0 and side == own:
                            continue
                        remote(
                            stage.at[pl.ds(base + to * per + side * big, tiles)],
                            got.at[gx, pl.ds(0, tiles)],
                            SPREAD + which,
                            to * 2 + side,
                            gy,
                        ).start()

        got[gx] = stage[pl.ds(base + chip * per + core * big, big)]

    def pick(which):
        base, per, big, sides, got, pieces = chunks[which]
        for side, tiles in sides:

            @pl.when(core == side)
            def _():
                wait_bytes(got.at[pl.ds(0, ngx - 1), pl.ds(0, tiles)], recv.at[SPREAD + which])

        def one(k, carry):
            pieces[k] = got[source[k]]
            return carry

        lax.fori_loop(0, ngx, one, 0, unroll=8)

    def gather(which):
        base, per, big, sides, got, pieces = chunks[which]
        for side, tiles in sides:

            @pl.when(core == side)
            def _():
                at = pl.ds(base + chip * per + side * big, tiles)

                for dz, dx in far_chips:
                    for other in range(2):
                        if dx == dz == 0 and side == other:
                            continue
                        peer = (at_x[dx] + at_z[dz]) * 2 + other
                        remote(
                            pieces.at[peer, pl.ds(0, tiles)],
                            home.at[at],
                            GATHER + which,
                            peer,
                            gy,
                        ).start()
                home[at] = pieces[gx, 0:tiles]

    def gathered(which):
        base, per, big, sides, got, pieces = chunks[which]
        for side, tiles in sides:

            @pl.when(core == side)
            def _():
                wait_bytes(
                    home.at[pl.ds(base, chips * per - tiles)], recv.at[GATHER + which]
                )

    spread(0)
    spread(1)
    pick(0)
    gather(0)
    pick(1)
    gather(1)

    gathered(0)
    for x in range(2):
        for z in range(5):
            kinds[x + 1, PAD + z * 8 : PAD + z * 8 + 8] = home[x * 5 + z]
    rows = pl.ds(PAD, 40)
    kinds_right = remote(kinds.at[2, rows], kinds.at[0, rows], KINDS, right, gy)
    kinds_left = remote(kinds.at[1, rows], kinds.at[3, rows], KINDS + 1, left, gy)
    kinds_right.start()
    kinds_left.start()
    pl.semaphore_wait(row_ready, ny - 1)
    kind_fields = [lambda slot, at: kinds[slot, at]]
    send_columns(kind_cols_out, kind_cols_in, KINDS + 2, kind_fields, kind_fields)
    bubble[...] = home[10:20].astype(jnp.int32)
    fluid_mass[...] = home[20:30]

    def collide(step, i, g):
        x, z = i // 5, i % 5
        diff = [g[a] - g[b] for a, b in PAIRS]
        total = [g[a] + g[b] for a, b in PAIRS]
        faces = total[0] + total[1] + total[2]
        edges = (total[3] + total[4]) + (total[5] + total[6]) + (total[7] + total[8])
        rho = g[0] * (1.0 / 3.0) + faces * (1.0 / 18.0) + edges * (1.0 / 36.0)
        inv = 1.0 / rho
        ux = (diff[0] * (1.0 / 18.0) + (diff[3] + diff[4] + diff[5] + diff[6]) * (1.0 / 36.0)) * inv
        uy = (diff[1] * (1.0 / 18.0) + (diff[3] - diff[4] + diff[7] + diff[8]) * (1.0 / 36.0)) * inv
        uz = (diff[2] * (1.0 / 18.0) + (diff[5] - diff[6] + diff[7] - diff[8]) * (1.0 / 36.0)) * inv
        speed[0, i] = ux
        speed[1, i] = uy
        speed[2, i] = uz
        scaled = OMEGA * rho
        flat = scaled * (1.0 - 1.5 * (ux * ux + uy * uy + uz * uz))
        at = pl.ds(pl.multiple_of(PAD + z * 8, 8), 8)
        post[step, x + 1, AT[0], at] = flat + (1.0 - OMEGA) * g[0]
        square = 4.5 * scaled
        line = 3.0 * scaled
        for (a, b), along in zip(PAIRS, pair_speeds(ux, uy, uz)):
            even = flat + square * (along * along)
            odd = line * along
            post[step, x + 1, AT[a], at] = even + odd + (1.0 - OMEGA) * g[a]
            post[step, x + 1, AT[b], at] = even - odd + (1.0 - OMEGA) * g[b]
        return rho

    def put_half(step, i, value):
        x, z = i // 5, i % 5
        post[step, x + 1, AT[HALF], pl.ds(pl.multiple_of(PAD + z * 8, 8), 8)] = 0.5 * value

    def level(kind, liquid_mass, rho):
        phi = jnp.where(kind == 2.0, 1.0, jnp.where(kind == 1.0, liquid_mass / rho, 0.0))
        part_gas = jnp.where(kind == 0.0, 1.0, jnp.where(kind == 1.0, 1.0 - phi, 0.0))
        return phi, part_gas

    def send_faces(step):
        plus = remote(
            post.at[step, 2, pl.ds(0, 6), rows],
            post.at[step, 0, pl.ds(0, 6), rows],
            x_sem(step, 0),
            right,
            gy,
        )
        minus = remote(
            post.at[step, 1, pl.ds(5, 6), rows],
            post.at[step, 3, pl.ds(5, 6), rows],
            x_sem(step, 1),
            left,
            gy,
        )
        plus.start()
        minus.start()
        return plus, minus

    def shifted(value, cols, step_y, j, slot, at, outside):
        if step_y == 0:
            return value
        if step_y == 1:
            edge = pltpu.roll(cols[0, at], 128 - (j * 4 + slot), 1)
            if outside is not None:
                edge = jnp.where(outside[0], -1.0, edge)
            return jnp.where(lane == 0, edge, pltpu.roll(value, 1, 1))
        edge = pltpu.roll(cols[1, at], 127 - (j * 4 + slot), 1)
        if outside is not None:
            edge = jnp.where(outside[1], -1.0, edge)
        return jnp.where(lane == 127, edge, pltpu.roll(value, 127, 1))

    def find_near(i, carry):
        x, z = i // 5, i % 5
        row = PAD + z * 8
        for d in range(1, 19):
            step_x, step_y, step_z = LATTICE[d]
            slot = x + 1 - step_x
            at = pl.ds(row - step_z, 8)
            near[d, i] = shifted(
                kinds[slot, at], kind_cols, step_y, 0, slot, at, (gy == 0, gy == ny - 1)
            )
        return carry

    def twice_even(i):
        ux, uy, uz = speed[0, i], speed[1, i], speed[2, i]
        flat = 2.0 - 3.0 * (ux * ux + uy * uy + uz * uz)
        return [flat + 9.0 * (along * along) for along in pair_speeds(ux, uy, uz)]

    def stream(step, i):
        x, z = i // 5, i % 5
        row = PAD + z * 8
        own = pl.ds(pl.multiple_of(row, 8), 8)
        half = post[step, x + 1, AT[HALF], own]
        rest = post[step, x + 1, AT[0], own]
        waiting[0, i] = rest
        zero = jnp.zeros((8, 128), F32)
        rho_sum = [zero, zero]
        gas_sum = [zero, zero]
        gain_sum = [zero, zero]
        for k, ((a, b), even) in enumerate(zip(PAIRS, twice_even(i))):
            kind_of = 0 if k < 3 else 1
            here = {a: post[step, x + 1, AT[a], own], b: post[step, x + 1, AT[b], own]}
            for d, back in ((a, b), (b, a)):
                step_x, step_y, step_z = LATTICE[d]
                slot = x + 1 - step_x
                at = pl.ds(row - step_z, 8)
                j = 0 if step_y == 0 else (COLS_UP if step_y == 1 else COLS_DOWN).index(d)
                came = shifted(post[step, slot, AT[d], at], cols, step_y, j, slot, at, None)
                near_half = shifted(post[step, slot, AT[HALF], at], cols, step_y, 5, slot, at, None)
                kind = near[d, i]
                bounced = here[back]
                value = jnp.where(kind >= 1.0, came, bounced)
                gas = kind == 0.0
                known = jnp.where(gas, -bounced, value)
                waiting[d, i] = known
                rho_sum[kind_of] = rho_sum[kind_of] + known
                gas_sum[kind_of] = gas_sum[kind_of] + jnp.where(gas, even, 0.0)
                part_of = jnp.where(
                    kind == 2.0, 1.0, jnp.where(kind == 1.0, half + near_half, 0.0)
                )
                gain_sum[kind_of] = gain_sum[kind_of] + part_of * (value - bounced)
        base_rho[i] = (
            rest * (1.0 / 3.0) + rho_sum[0] * (1.0 / 18.0) + rho_sum[1] * (1.0 / 36.0)
        )
        gas_rho[i] = gas_sum[0] * (1.0 / 18.0) + gas_sum[1] * (1.0 / 36.0)
        gain[i] = gain_sum[0] * (1.0 / 18.0) + gain_sum[1] * (1.0 / 36.0)

    def arrived(i):
        density = gas_here[i]
        g = [waiting[0, i]] + [None] * 18
        for (a, b), even in zip(PAIRS, twice_even(i)):
            lift = density * even
            for d in (a, b):
                known = waiting[d, i]
                g[d] = jnp.where(near[d, i] == 0.0, known + lift, known)
        return g

    def lookup(table):
        def one(i, carry):
            gas_here[i] = jnp.take_along_axis(
                table, bubble[i], axis=1, mode="promise_in_bounds"
            )
            return carry

        lax.fori_loop(0, 10, one, 0, unroll=5)

    def member_sums():
        labels = [bubble[i] for i in range(10)]
        shares = [share[i] for i in range(10)]

        def one(b):
            parts = [jnp.where(which == b, part_of, 0.0) for which, part_of in zip(labels, shares)]
            while len(parts) > 1:
                parts = [sum(parts[k : k + 2]) for k in range(0, len(parts), 2)]
            return parts[0]

        def merged(bits, b):
            if bits == 0:
                return one(b)
            bit = bits - 1
            first, second = merged(bit, b), merged(bit, b + (1 << bit))
            odd = (lane >> bit) & 1 == 1
            keep = jnp.where(odd, second, first)
            move = jnp.where(odd, first, second)
            return keep + pltpu.roll(move, 128 - (1 << bit), 1)

        now = merged(6, 0)
        return now + pltpu.roll(now, 64, 1)

    def begin_sum(step, value):
        part[step, 0] = jnp.sum(value, axis=0, keepdims=True)
        remote(part.at[step, 0], mate_sum.at[step], mate_sem(step), mate, gy).start()

    def middle_sum(step):
        wait_bytes(mate_sum.at[step], recv.at[mate_sem(step)])
        value = part[step, 0] + mate_sum[step]
        part[step, 1] = value
        mine = chip * ny + gy
        sums[step, mine] = value

        for dz, dx in far_chips:
            to_x = (at_x[dx] + at_z[dz]) * 2 + core
            for dy in far_first(ny):
                if dx == dy == dz == 0:
                    continue
                remote(
                    part.at[step, 1], sums.at[step, mine], all_sem(step), to_x, at_y[dy]
                ).start()

    def end_sum(step):
        wait_bytes(sums.at[step, pl.ds(0, chips * ny - 1)], recv.at[all_sem(step)])
        return jnp.broadcast_to(jnp.sum(sums[step], axis=0), (8, 128))

    def first(i, carry):
        rho = collide(0, i, [home[30 + q * 10 + i] for q in range(19)])
        kind = home[i]
        phi, part_gas = level(kind, fluid_mass[i], rho)
        put_half(0, i, phi)
        share[i] = part_gas
        return carry

    bubble_lane = lane & (BUBBLES - 1)
    table = jnp.zeros((8, 128), F32)
    for b in range(BUBBLES):
        table = jnp.where(bubble_lane == b, gas_density[b], table)
    density_start = table
    lookup(table)

    gathered(1)
    lax.fori_loop(0, 10, first, 0)
    faces = send_faces(0)
    post_columns(0)
    started = [faces]
    kinds_right.wait_recv()
    kinds_left.wait_recv()
    wait_columns(kind_cols_in, kind_cols, KINDS + 2)
    lax.fori_loop(0, 10, find_near, 0)
    volume_start = member_sums()
    wait_columns(cols_in.at[0], cols, y_sem(0, 0))
    for face in faces:
        face.wait_recv()

    def stream_all(step):
        def one(i, carry):
            stream(step, i)
            return carry

        lax.fori_loop(0, 10, one, 0, unroll=5)

    stream_all(0)
    start_total = None
    for step in range(ITERS):

        def settle(i, carry):
            kind = home[i]
            rho = base_rho[i] + gas_here[i] * gas_rho[i]
            liquid_mass = jnp.where(
                kind == 1.0, fluid_mass[i] + gain[i], jnp.where(kind == 2.0, rho, 0.0)
            )
            fluid_mass[i] = liquid_mass
            phi, part_gas = level(kind, liquid_mass, rho)
            if step < ITERS - 1:
                put_half(step + 1, i, phi)
            share[i] = part_gas
            return carry

        lax.fori_loop(0, 10, settle, 0, unroll=5)
        volume = member_sums()
        if step == 0:
            volume = jnp.where(lane < BUBBLES, volume, volume_start)
        begin_sum(step, volume)

        if step < ITERS - 1:

            def again(i, carry):
                collide(step + 1, i, arrived(i))
                return carry

            lax.fori_loop(0, 10, again, 0)
            faces = send_faces(step + 1)
            started.append(faces)
            middle_sum(step)
            post_columns(step + 1)
            wait_columns(cols_in.at[step + 1], cols, y_sem(step + 1, 0))
            for face in faces:
                face.wait_recv()
            stream_all(step + 1)
        else:

            def last(i, carry):
                for q, value in enumerate(arrived(i)):
                    waiting[q, i] = value
                return carry

            lax.fori_loop(0, 10, last, 0)
            middle_sum(step)
            store_g = pltpu.make_async_copy(waiting, out_g, fetch.at[0])
            store_g.start()
        total = end_sum(step)
        if step == 0:
            other = pltpu.roll(total, 64, 1)
            start_total = jnp.where(lane < BUBBLES, other, total)
            total = jnp.where(lane < BUBBLES, total, other)
        lookup(density_start * start_total / total)

    out_m[0:10] = fluid_mass[...]
    out_m[10:20] = home[0:10]
    out_m[20:30] = gas_here[...]
    out_v[...] = total[0:1, :BUBBLES] * (BUBBLES / (ngx * ny * 2 * 40 * 128))

    store_g.wait()
    for which in range(2):
        base, per, big, sides, got, pieces = chunks[which]
        for side, tiles in sides:

            @pl.when(core == side)
            def _():
                wait_bytes(stage.at[pl.ds(0, chips * per - tiles)], send.at[SPREAD + which])
                wait_bytes(
                    pieces.at[pl.ds(0, ngx - 1), pl.ds(0, tiles)], send.at[GATHER + which]
                )

    kinds_right.wait_send()
    kinds_left.wait_send()
    columns_sent(kind_cols_in, KINDS + 2)
    for step in range(ITERS):
        for face in started[step]:
            face.wait_send()
        columns_sent(cols_in.at[step], y_sem(step, 0))
        wait_bytes(mate_sum.at[step], send.at[mate_sem(step)])
        wait_bytes(sums.at[step, pl.ds(0, chips * ny - 1)], send.at[all_sem(step)])


def hand_over(g, m, v, out_g, out_m, out_v, held_g, held_m, held_v, sem):
    cuts = (0, 4, 8, 12, 16, 19)
    groups = [pl.ds(a, b - a) for a, b in zip(cuts, cuts[1:])]
    inward = [pltpu.make_async_copy(m, held_m, sem.at[0, 5])]
    inward += [
        pltpu.make_async_copy(g.at[at], held_g.at[at], sem.at[0, k])
        for k, at in enumerate(groups)
    ]
    inward.append(pltpu.make_async_copy(v, held_v, sem.at[0, 6]))
    for one in inward:
        one.start()
    inward[0].wait()
    outward = [pltpu.make_async_copy(held_m.at[0:10], out_m, sem.at[1, 5])]
    outward[0].start()
    gas = held_m[10:20] == 0.0
    density = held_m[20:30]
    for k, (a, b) in enumerate(zip(cuts, cuts[1:])):
        inward[k + 1].wait()
        for q in range(a, b):
            held_g[q] = jnp.where(gas, density, held_g[q])
        outward.append(
            pltpu.make_async_copy(held_g.at[groups[k]], out_g.at[groups[k]], sem.at[1, k])
        )
        outward[-1].start()
    inward[-1].wait()
    outward.append(pltpu.make_async_copy(held_v, out_v, sem.at[1, 6]))
    outward[-1].start()
    for one in outward:
        one.wait()


def chunk_tiles(chips):
    per = -(-220 // chips)
    return (per * 4 + 6) // 7, per - (per * 4 + 6) // 7


def solution(mesh):
    ngx, ny = mesh.shape["gx"], mesh.shape["gy"]
    nx, nz = (4, 8) if ngx == 64 else (1, ngx // 2)
    chips = ngx // 2
    per_a, per_b = chunk_tiles(chips)
    big_a, big_b = (per_a + 1) // 2, (per_b + 1) // 2

    def per_device(populations, mass, cell_type, bubble_id, slab_source, gas_density):
        vmem = pl.BlockSpec(memory_space=pltpu.VMEM)
        hbm = pl.BlockSpec(memory_space=pltpu.HBM)

        def tiles(count, dtype=F32):
            return pltpu.VMEM((count, 8, 128), dtype)

        g, m, v = pl.pallas_call(
            functools.partial(kernel, (nx, nz, ny)),
            out_shape=(
                jax.ShapeDtypeStruct((19, 10, 8, 128), F32),
                jax.ShapeDtypeStruct((30, 8, 128), F32),
                jax.ShapeDtypeStruct((1, BUBBLES), F32),
            ),
            in_specs=[hbm] * 6,
            out_specs=(hbm, vmem, vmem),
            scratch_shapes=[
                tiles(chips * (per_a + per_b) + 1),
                tiles(20, jnp.int32),
                pltpu.SMEM((ngx,), jnp.int32),
                pltpu.SMEM((BUBBLES,), F32),
                pltpu.VMEM((ngx, big_a, 8, 128), F32),
                pltpu.VMEM((ngx, big_b, 8, 128), F32),
                pltpu.VMEM((ngx, big_a, 8, 128), F32),
                pltpu.VMEM((ngx, big_b, 8, 128), F32),
                tiles(chips * (per_a + per_b)),
                pltpu.VMEM((ITERS, 4, 20, 56, 128), F32),
                pltpu.VMEM((4, 56, 128), F32),
                pltpu.VMEM((19, 10, 8, 128), F32),
                pltpu.VMEM((19, 10, 8, 128), F32),
                pltpu.VMEM((3, 10, 8, 128), F32),
                tiles(10, jnp.int32),
                tiles(10),
                tiles(10),
                tiles(10),
                tiles(10),
                tiles(10),
                tiles(10),
                pltpu.VMEM((ITERS, 2, 40, 128), F32),
                pltpu.VMEM((ITERS, 2, 3, 40, 128), F32),
                pltpu.VMEM((2, 56, 128), F32),
                pltpu.VMEM((2, 40, 128), F32),
                pltpu.VMEM((2, 3, 40, 128), F32),
                pltpu.VMEM((2, 56, 128), F32),
                pltpu.VMEM((ITERS, 1, 128), F32),
                pltpu.VMEM((ITERS, chips * ny, 1, 128), F32),
                pltpu.VMEM((ITERS, 2, 1, 128), F32),
                pltpu.SemaphoreType.DMA((6,)),
                pltpu.SemaphoreType.DMA((8 + ITERS * 8,)),
                pltpu.SemaphoreType.DMA((8 + ITERS * 8,)),
                pltpu.SemaphoreType.REGULAR,
            ],
            compiler_params=pltpu.CompilerParams(
                collective_id=0, has_side_effects=True, vmem_limit_bytes=VMEM_LIMIT
            ),
        )(
            populations.reshape(190, 8, 128),
            mass.reshape(10, 8, 128),
            cell_type.reshape(10, 8, 128),
            bubble_id.reshape(10, 8, 128),
            slab_source,
            gas_density,
        )
        anywhere = pl.BlockSpec(memory_space=pl.ANY)
        g, m, v = pl.pallas_call(
            hand_over,
            out_shape=(
                jax.ShapeDtypeStruct((19, 10, 8, 128), F32),
                jax.ShapeDtypeStruct((10, 8, 128), F32),
                jax.ShapeDtypeStruct((1, BUBBLES), F32),
            ),
            in_specs=[anywhere] * 3,
            out_specs=(hbm, hbm, hbm),
            scratch_shapes=[
                pltpu.VMEM((19, 10, 8, 128), F32),
                tiles(30),
                pltpu.VMEM((1, BUBBLES), F32),
                pltpu.SemaphoreType.DMA((2, 7)),
            ],
            compiler_params=pltpu.CompilerParams(vmem_limit_bytes=VMEM_LIMIT),
        )(g, m, v)
        return g.reshape(populations.shape), m.reshape(mass.shape), v.reshape(BUBBLES)

    return jax.shard_map(
        per_device,
        mesh=mesh,
        in_specs=(
            P(None, "gx", None, "gy"),
            P("gx", None, "gy"),
            P("gx", None, "gy"),
            P("gx", None, "gy"),
            P(),
            P(),
        ),
        out_specs=(P(None, "gx", None, "gy"), P("gx", None, "gy"), P()),
        check_vma=False,
    )
```

```python
import functools

import jax
import jax.numpy as jnp
from jax import lax
from jax.experimental import pallas as pl
from jax.experimental.pallas import tpu as pltpu
from jax.sharding import PartitionSpec as P

BUBBLES = 64
ITERS = 3
OMEGA = 1.6
VMEM_LIMIT = 56 * 2**20
MESH = pl.DeviceIdType.MESH
F32 = jnp.float32

LATTICE = (
    (0, 0, 0),
    (1, 0, 0),
    (-1, 0, 0),
    (0, 1, 0),
    (0, -1, 0),
    (0, 0, 1),
    (0, 0, -1),
    (1, 1, 0),
    (-1, -1, 0),
    (1, -1, 0),
    (-1, 1, 0),
    (1, 0, 1),
    (-1, 0, -1),
    (1, 0, -1),
    (-1, 0, 1),
    (0, 1, 1),
    (0, -1, -1),
    (0, 1, -1),
    (0, -1, 1),
)
HALF = 19
ORDER = (1, 7, 9, 11, 13, HALF, 2, 8, 10, 12, 14, 0, 3, 4, 5, 6, 15, 16, 17, 18)
AT = {field: pos for pos, field in enumerate(ORDER)}
COLS_UP = (3, 7, 10, 15, 17, HALF)
COLS_DOWN = (4, 8, 9, 16, 18, HALF)
PAIRS = ((1, 2), (3, 4), (5, 6), (7, 8), (9, 10), (11, 12), (13, 14), (15, 16), (17, 18))
PAD = 8


def pair_speeds(ux, uy, uz):
    return (ux, uy, uz, ux + uy, ux - uy, ux + uz, ux - uz, uy + uz, uy - uz)


def far_first(size):
    return sorted(range(size), key=lambda d: -min(d, size - d))


def kernel(
    shape,
    pop,
    mass,
    cell,
    label,
    source_in,
    density_in,
    out_g,
    out_m,
    out_v,
    stage,
    ints,
    source,
    gas_density,
    got_a,
    got_b,
    sorted_a,
    sorted_b,
    home,
    post,
    kinds,
    near,
    waiting,
    speed,
    bubble,
    fluid_mass,
    share,
    base_rho,
    gas_rho,
    gain,
    gas_here,
    cols_out,
    cols_in,
    cols,
    kind_cols_out,
    kind_cols_in,
    kind_cols,
    mate_sum,
    sums,
    part,
    fetch,
    send,
    recv,
    row_ready,
):
    nx, nz, ny = shape
    ngx = nx * nz * 2
    chips = nx * nz
    gx = lax.axis_index("gx")
    gy = lax.axis_index("gy")
    core = gx % 2
    chip = gx // 2
    pos_x = chip // nz
    pos_z = chip % nz
    mate = gx + 1 - 2 * core
    right = (gx + 1) % ngx
    left = (gx + ngx - 1) % ngx
    lane = lax.broadcasted_iota(jnp.int32, (8, 128), 1)

    SPREAD, GATHER, KINDS = 0, 2, 4

    def x_sem(step, side):
        return 8 + step * 8 + side

    def y_sem(step, side):
        return 8 + step * 8 + 2 + side

    def mate_sem(step):
        return 8 + step * 8 + 4

    def all_sem(step):
        return 8 + step * 8 + 5

    def remote(src, dst, sem, to_x, to_y):
        return pltpu.make_async_remote_copy(
            src_ref=src,
            dst_ref=dst,
            send_sem=send.at[sem],
            recv_sem=recv.at[sem],
            device_id=(to_x, to_y),
            device_id_type=MESH,
        )

    def wait_bytes(ref, sem):
        pltpu.make_async_copy(ref, ref, sem).wait()

    at_x = [lax.rem(pos_x + d, nx) * nz for d in range(nx)]
    at_z = [lax.rem(pos_z + d, nz) for d in range(nz)]
    at_y = [lax.rem(gy + d, ny) for d in range(ny)]
    far_chips = [(dz, dx) for dz in far_first(nz) for dx in far_first(nx)]
    peers = [
        (at_x[dx] + at_z[dz], other, dx == dz == 0 and other is core)
        for dz, dx in far_chips
        for other in (1 - core, core)
    ]

    def send_columns(out, into, sem, up_fields, down_fields):
        for z in range(5):
            up = jnp.zeros((8, 128), F32)
            down = jnp.zeros((8, 128), F32)
            for j, (high, low) in enumerate(zip(up_fields, down_fields)):
                for x in range(2):
                    spot = j * 4 + x + 1
                    at = pl.ds(PAD + z * 8, 8)
                    up = jnp.where(lane == spot, pltpu.roll(high(x + 1, at), spot + 1, 1), up)
                    down = jnp.where(lane == spot, pltpu.roll(low(x + 1, at), spot, 1), down)
            out[0, z * 8 : z * 8 + 8] = up
            out[1, z * 8 : z * 8 + 8] = down
        for side, there, to_y in ((0, gy < ny - 1, gy + 1), (1, gy > 0, gy - 1)):

            @pl.when(there)
            def _():
                for shift, to_x in ((-1, left), (0, gx), (1, right)):
                    remote(out.at[side], into.at[side, 1 - shift], sem + side, to_x, to_y).start()

    def wait_columns(into, whole, sem):
        for side, there in ((0, gy > 0), (1, gy < ny - 1)):

            @pl.when(there)
            def _():
                wait_bytes(into.at[side], recv.at[sem + side])

        slot = lane % 4
        for side in range(2):
            for z in range(5):
                of = pl.ds(z * 8, 8)
                before = pltpu.roll(into[side, 0, of], 126, 1)
                after = pltpu.roll(into[side, 2, of], 2, 1)
                whole[side, PAD + z * 8 : PAD + z * 8 + 8] = jnp.where(
                    slot == 0, before, jnp.where(slot == 3, after, into[side, 1, of])
                )

    def columns_sent(into, sem):
        for side, there in ((0, gy < ny - 1), (1, gy > 0)):

            @pl.when(there)
            def _():
                wait_bytes(into.at[side], send.at[sem + side])

    def post_columns(step):
        def fields(order):
            return [
                lambda slot, at, f=f: post[step, slot, AT[f], at] for f in order
            ]

        send_columns(
            cols_out.at[step], cols_in.at[step], y_sem(step, 0), fields(COLS_UP), fields(COLS_DOWN)
        )

    fetches = [
        pltpu.make_async_copy(src, dst, fetch.at[k])
        for k, (src, dst) in enumerate(
            (
                (cell, ints.at[0:10]),
                (label, ints.at[10:20]),
                (pop, stage.at[30:220]),
                (mass, stage.at[20:30]),
                (source_in, source),
                (density_in, gas_density),
            )
        )
    ]
    for one in fetches:
        one.start()

    barrier = pltpu.get_barrier_semaphore()

    for to_chip, to_core, near_by in peers:
        if not near_by:
            pl.semaphore_signal(
                barrier, inc=1, device_id=(to_chip * 2 + to_core, gy), device_id_type=MESH
            )
    for k in range(1, ny):
        pl.semaphore_signal(
            barrier, inc=1, device_id=(gx, (gy + k) % ny), device_id_type=MESH
        )

    walls = jnp.full((PAD, 128), -1.0, F32)
    for slot in range(4):
        kinds[slot, 0:PAD] = walls
        kinds[slot, PAD + 40 : PAD + 48] = walls
    for side in range(2):
        for edge in (cols, kind_cols):
            edge[side, 0:PAD] = walls
            edge[side, PAD + 40 : PAD + 48] = walls
    for one in fetches:
        one.wait()
    stage[0:20] = ints[...].astype(F32)
    pl.semaphore_wait(barrier, ngx - 1 + ny - 1)
    for k in range(1, ny):
        pl.semaphore_signal(
            row_ready, inc=1, device_id=(gx, (gy + k) % ny), device_id_type=MESH
        )

    chunks = []
    base = 0
    for per, got, pieces in zip(chunk_tiles(chips), (got_a, got_b), (sorted_a, sorted_b)):
        big = (per + 1) // 2
        chunks.append((base, per, big, ((0, big), (1, per - big)), got, pieces))
        base += per * chips

    def spread(which):
        base, per, big, sides, got, pieces = chunks[which]

        for own, _ in sides:

            @pl.when(core == own)
            def _():
                for dz, dx in far_chips:
                    to = at_x[dx] + at_z[dz]
                    for side, tiles in sides:
                        if dx == dz == 0 and side == own:
                            continue
                        remote(
                            stage.at[pl.ds(base + to * per + side * big, tiles)],
                            got.at[gx, pl.ds(0, tiles)],
                            SPREAD + which,
                            to * 2 + side,
                            gy,
                        ).start()

        got[gx] = stage[pl.ds(base + chip * per + core * big, big)]

    def pick(which):
        base, per, big, sides, got, pieces = chunks[which]
        for side, tiles in sides:

            @pl.when(core == side)
            def _():
                wait_bytes(got.at[pl.ds(0, ngx - 1), pl.ds(0, tiles)], recv.at[SPREAD + which])

        def one(k, carry):
            pieces[k] = got[source[k]]
            return carry

        lax.fori_loop(0, ngx, one, 0, unroll=8)

    def gather(which):
        base, per, big, sides, got, pieces = chunks[which]
        for side, tiles in sides:

            @pl.when(core == side)
            def _():
                at = pl.ds(base + chip * per + side * big, tiles)

                for dz, dx in far_chips:
                    for other in range(2):
                        if dx == dz == 0 and side == other:
                            continue
                        peer = (at_x[dx] + at_z[dz]) * 2 + other
                        remote(
                            pieces.at[peer, pl.ds(0, tiles)],
                            home.at[at],
                            GATHER + which,
                            peer,
                            gy,
                        ).start()
                home[at] = pieces[gx, 0:tiles]

    def gathered(which):
        base, per, big, sides, got, pieces = chunks[which]
        for side, tiles in sides:

            @pl.when(core == side)
            def _():
                wait_bytes(
                    home.at[pl.ds(base, chips * per - tiles)], recv.at[GATHER + which]
                )

    spread(0)
    spread(1)
    pick(0)
    gather(0)
    pick(1)
    gather(1)

    gathered(0)
    for x in range(2):
        for z in range(5):
            kinds[x + 1, PAD + z * 8 : PAD + z * 8 + 8] = home[x * 5 + z]
    rows = pl.ds(PAD, 40)
    kinds_right = remote(kinds.at[2, rows], kinds.at[0, rows], KINDS, right, gy)
    kinds_left = remote(kinds.at[1, rows], kinds.at[3, rows], KINDS + 1, left, gy)
    kinds_right.start()
    kinds_left.start()
    pl.semaphore_wait(row_ready, ny - 1)
    kind_fields = [lambda slot, at: kinds[slot, at]]
    send_columns(kind_cols_out, kind_cols_in, KINDS + 2, kind_fields, kind_fields)
    bubble[...] = home[10:20].astype(jnp.int32)
    fluid_mass[...] = home[20:30]

    def collide(step, i, g):
        x, z = i // 5, i % 5
        diff = [g[a] - g[b] for a, b in PAIRS]
        total = [g[a] + g[b] for a, b in PAIRS]
        faces = total[0] + total[1] + total[2]
        edges = (total[3] + total[4]) + (total[5] + total[6]) + (total[7] + total[8])
        rho = g[0] * (1.0 / 3.0) + faces * (1.0 / 18.0) + edges * (1.0 / 36.0)
        inv = 1.0 / rho
        ux = (diff[0] * (1.0 / 18.0) + (diff[3] + diff[4] + diff[5] + diff[6]) * (1.0 / 36.0)) * inv
        uy = (diff[1] * (1.0 / 18.0) + (diff[3] - diff[4] + diff[7] + diff[8]) * (1.0 / 36.0)) * inv
        uz = (diff[2] * (1.0 / 18.0) + (diff[5] - diff[6] + diff[7] - diff[8]) * (1.0 / 36.0)) * inv
        speed[0, i] = ux
        speed[1, i] = uy
        speed[2, i] = uz
        scaled = OMEGA * rho
        flat = scaled * (1.0 - 1.5 * (ux * ux + uy * uy + uz * uz))
        at = pl.ds(pl.multiple_of(PAD + z * 8, 8), 8)
        post[step, x + 1, AT[0], at] = flat + (1.0 - OMEGA) * g[0]
        square = 4.5 * scaled
        line = 3.0 * scaled
        for (a, b), along in zip(PAIRS, pair_speeds(ux, uy, uz)):
            even = flat + square * (along * along)
            odd = line * along
            post[step, x + 1, AT[a], at] = even + odd + (1.0 - OMEGA) * g[a]
            post[step, x + 1, AT[b], at] = even - odd + (1.0 - OMEGA) * g[b]
        return rho

    def put_half(step, i, value):
        x, z = i // 5, i % 5
        post[step, x + 1, AT[HALF], pl.ds(pl.multiple_of(PAD + z * 8, 8), 8)] = 0.5 * value

    def level(kind, liquid_mass, rho):
        phi = jnp.where(kind == 2.0, 1.0, jnp.where(kind == 1.0, liquid_mass / rho, 0.0))
        part_gas = jnp.where(kind == 0.0, 1.0, jnp.where(kind == 1.0, 1.0 - phi, 0.0))
        return phi, part_gas

    def send_faces(step):
        plus = remote(
            post.at[step, 2, pl.ds(0, 6), rows],
            post.at[step, 0, pl.ds(0, 6), rows],
            x_sem(step, 0),
            right,
            gy,
        )
        minus = remote(
            post.at[step, 1, pl.ds(5, 6), rows],
            post.at[step, 3, pl.ds(5, 6), rows],
            x_sem(step, 1),
            left,
            gy,
        )
        plus.start()
        minus.start()
        return plus, minus

    def shifted(value, cols, step_y, j, slot, at, outside):
        if step_y == 0:
            return value
        if step_y == 1:
            edge = pltpu.roll(cols[0, at], 128 - (j * 4 + slot), 1)
            if outside is not None:
                edge = jnp.where(outside[0], -1.0, edge)
            return jnp.where(lane == 0, edge, pltpu.roll(value, 1, 1))
        edge = pltpu.roll(cols[1, at], 127 - (j * 4 + slot), 1)
        if outside is not None:
            edge = jnp.where(outside[1], -1.0, edge)
        return jnp.where(lane == 127, edge, pltpu.roll(value, 127, 1))

    def find_near(i, carry):
        x, z = i // 5, i % 5
        row = PAD + z * 8
        for d in range(1, 19):
            step_x, step_y, step_z = LATTICE[d]
            slot = x + 1 - step_x
            at = pl.ds(row - step_z, 8)
            near[d, i] = shifted(
                kinds[slot, at], kind_cols, step_y, 0, slot, at, (gy == 0, gy == ny - 1)
            )
        return carry

    def twice_even(i):
        ux, uy, uz = speed[0, i], speed[1, i], speed[2, i]
        flat = 2.0 - 3.0 * (ux * ux + uy * uy + uz * uz)
        return [flat + 9.0 * (along * along) for along in pair_speeds(ux, uy, uz)]

    def stream(step, i):
        x, z = i // 5, i % 5
        row = PAD + z * 8
        own = pl.ds(pl.multiple_of(row, 8), 8)
        half = post[step, x + 1, AT[HALF], own]
        rest = post[step, x + 1, AT[0], own]
        waiting[0, i] = rest
        zero = jnp.zeros((8, 128), F32)
        rho_sum = [zero, zero]
        gas_sum = [zero, zero]
        gain_sum = [zero, zero]
        for k, ((a, b), even) in enumerate(zip(PAIRS, twice_even(i))):
            kind_of = 0 if k < 3 else 1
            here = {a: post[step, x + 1, AT[a], own], b: post[step, x + 1, AT[b], own]}
            for d, back in ((a, b), (b, a)):
                step_x, step_y, step_z = LATTICE[d]
                slot = x + 1 - step_x
                at = pl.ds(row - step_z, 8)
                j = 0 if step_y == 0 else (COLS_UP if step_y == 1 else COLS_DOWN).index(d)
                came = shifted(post[step, slot, AT[d], at], cols, step_y, j, slot, at, None)
                near_half = shifted(post[step, slot, AT[HALF], at], cols, step_y, 5, slot, at, None)
                kind = near[d, i]
                bounced = here[back]
                value = jnp.where(kind >= 1.0, came, bounced)
                gas = kind == 0.0
                known = jnp.where(gas, -bounced, value)
                waiting[d, i] = known
                rho_sum[kind_of] = rho_sum[kind_of] + known
                gas_sum[kind_of] = gas_sum[kind_of] + jnp.where(gas, even, 0.0)
                part_of = jnp.where(
                    kind == 2.0, 1.0, jnp.where(kind == 1.0, half + near_half, 0.0)
                )
                gain_sum[kind_of] = gain_sum[kind_of] + part_of * (value - bounced)
        base_rho[i] = (
            rest * (1.0 / 3.0) + rho_sum[0] * (1.0 / 18.0) + rho_sum[1] * (1.0 / 36.0)
        )
        gas_rho[i] = gas_sum[0] * (1.0 / 18.0) + gas_sum[1] * (1.0 / 36.0)
        gain[i] = gain_sum[0] * (1.0 / 18.0) + gain_sum[1] * (1.0 / 36.0)

    def arrived(i):
        density = gas_here[i]
        g = [waiting[0, i]] + [None] * 18
        for (a, b), even in zip(PAIRS, twice_even(i)):
            lift = density * even
            for d in (a, b):
                known = waiting[d, i]
                g[d] = jnp.where(near[d, i] == 0.0, known + lift, known)
        return g

    def lookup(table):
        def one(i, carry):
            gas_here[i] = jnp.take_along_axis(
                table, bubble[i], axis=1, mode="promise_in_bounds"
            )
            return carry

        lax.fori_loop(0, 10, one, 0, unroll=5)

    def member_sums():
        labels = [bubble[i] for i in range(10)]
        shares = [share[i] for i in range(10)]

        def one(b):
            parts = [jnp.where(which == b, part_of, 0.0) for which, part_of in zip(labels, shares)]
            while len(parts) > 1:
                parts = [sum(parts[k : k + 2]) for k in range(0, len(parts), 2)]
            return parts[0]

        def merged(bits, b):
            if bits == 0:
                return one(b)
            bit = bits - 1
            first, second = merged(bit, b), merged(bit, b + (1 << bit))
            odd = (lane >> bit) & 1 == 1
            keep = jnp.where(odd, second, first)
            move = jnp.where(odd, first, second)
            return keep + pltpu.roll(move, 128 - (1 << bit), 1)

        now = merged(6, 0)
        return now + pltpu.roll(now, 64, 1)

    def begin_sum(step, value):
        part[step, 0] = jnp.sum(value, axis=0, keepdims=True)
        remote(part.at[step, 0], mate_sum.at[step], mate_sem(step), mate, gy).start()

    def middle_sum(step):
        wait_bytes(mate_sum.at[step], recv.at[mate_sem(step)])
        value = part[step, 0] + mate_sum[step]
        part[step, 1] = value
        mine = chip * ny + gy
        sums[step, mine] = value

        for dz, dx in far_chips:
            to_x = (at_x[dx] + at_z[dz]) * 2 + core
            for dy in far_first(ny):
                if dx == dy == dz == 0:
                    continue
                remote(
                    part.at[step, 1], sums.at[step, mine], all_sem(step), to_x, at_y[dy]
                ).start()

    def end_sum(step):
        wait_bytes(sums.at[step, pl.ds(0, chips * ny - 1)], recv.at[all_sem(step)])
        return jnp.broadcast_to(jnp.sum(sums[step], axis=0), (8, 128))

    def first(i, carry):
        rho = collide(0, i, [home[30 + q * 10 + i] for q in range(19)])
        kind = home[i]
        phi, part_gas = level(kind, fluid_mass[i], rho)
        put_half(0, i, phi)
        share[i] = part_gas
        return carry

    bubble_lane = lane & (BUBBLES - 1)
    table = jnp.zeros((8, 128), F32)
    for b in range(BUBBLES):
        table = jnp.where(bubble_lane == b, gas_density[b], table)
    density_start = table
    lookup(table)

    gathered(1)
    lax.fori_loop(0, 10, first, 0)
    faces = send_faces(0)
    post_columns(0)
    started = [faces]
    kinds_right.wait_recv()
    kinds_left.wait_recv()
    wait_columns(kind_cols_in, kind_cols, KINDS + 2)
    lax.fori_loop(0, 10, find_near, 0)
    volume_start = member_sums()
    wait_columns(cols_in.at[0], cols, y_sem(0, 0))
    for face in faces:
        face.wait_recv()

    def stream_all(step):
        def one(i, carry):
            stream(step, i)
            return carry

        lax.fori_loop(0, 10, one, 0, unroll=5)

    stream_all(0)
    start_total = None
    for step in range(ITERS):

        def settle(i, carry):
            kind = home[i]
            rho = base_rho[i] + gas_here[i] * gas_rho[i]
            liquid_mass = jnp.where(
                kind == 1.0, fluid_mass[i] + gain[i], jnp.where(kind == 2.0, rho, 0.0)
            )
            fluid_mass[i] = liquid_mass
            phi, part_gas = level(kind, liquid_mass, rho)
            if step < ITERS - 1:
                put_half(step + 1, i, phi)
            share[i] = part_gas
            return carry

        lax.fori_loop(0, 10, settle, 0, unroll=5)
        volume = member_sums()
        if step == 0:
            volume = jnp.where(lane < BUBBLES, volume, volume_start)
        begin_sum(step, volume)

        if step < ITERS - 1:

            def again(i, carry):
                collide(step + 1, i, arrived(i))
                return carry

            middle_sum(step)
            lax.fori_loop(0, 10, again, 0)
            faces = send_faces(step + 1)
            started.append(faces)
            post_columns(step + 1)
            wait_columns(cols_in.at[step + 1], cols, y_sem(step + 1, 0))
            for face in faces:
                face.wait_recv()
            stream_all(step + 1)
        else:

            def last(i, carry):
                for q, value in enumerate(arrived(i)):
                    waiting[q, i] = value
                return carry

            middle_sum(step)
            lax.fori_loop(0, 10, last, 0)
            store_g = pltpu.make_async_copy(waiting, out_g, fetch.at[0])
            store_g.start()
        total = end_sum(step)
        if step == 0:
            other = pltpu.roll(total, 64, 1)
            start_total = jnp.where(lane < BUBBLES, other, total)
            total = jnp.where(lane < BUBBLES, total, other)
        lookup(density_start * start_total / total)

    out_m[0:10] = fluid_mass[...]
    out_m[10:20] = home[0:10]
    out_m[20:30] = gas_here[...]
    out_v[...] = total[0:1, :BUBBLES] * (BUBBLES / (ngx * ny * 2 * 40 * 128))

    store_g.wait()
    for which in range(2):
        base, per, big, sides, got, pieces = chunks[which]
        for side, tiles in sides:

            @pl.when(core == side)
            def _():
                wait_bytes(stage.at[pl.ds(0, chips * per - tiles)], send.at[SPREAD + which])
                wait_bytes(
                    pieces.at[pl.ds(0, ngx - 1), pl.ds(0, tiles)], send.at[GATHER + which]
                )

    kinds_right.wait_send()
    kinds_left.wait_send()
    columns_sent(kind_cols_in, KINDS + 2)
    for step in range(ITERS):
        for face in started[step]:
            face.wait_send()
        columns_sent(cols_in.at[step], y_sem(step, 0))
        wait_bytes(mate_sum.at[step], send.at[mate_sem(step)])
        wait_bytes(sums.at[step, pl.ds(0, chips * ny - 1)], send.at[all_sem(step)])


def hand_over(g, m, v, out_g, out_m, out_v, held_g, held_m, held_v, sem):
    cuts = (0, 4, 8, 12, 16, 19)
    groups = [pl.ds(a, b - a) for a, b in zip(cuts, cuts[1:])]
    inward = [pltpu.make_async_copy(m, held_m, sem.at[0, 5])]
    inward += [
        pltpu.make_async_copy(g.at[at], held_g.at[at], sem.at[0, k])
        for k, at in enumerate(groups)
    ]
    inward.append(pltpu.make_async_copy(v, held_v, sem.at[0, 6]))
    for one in inward:
        one.start()
    inward[0].wait()
    outward = [pltpu.make_async_copy(held_m.at[0:10], out_m, sem.at[1, 5])]
    outward[0].start()
    gas = held_m[10:20] == 0.0
    density = held_m[20:30]
    for k, (a, b) in enumerate(zip(cuts, cuts[1:])):
        inward[k + 1].wait()
        for q in range(a, b):
            held_g[q] = jnp.where(gas, density, held_g[q])
        outward.append(
            pltpu.make_async_copy(held_g.at[groups[k]], out_g.at[groups[k]], sem.at[1, k])
        )
        outward[-1].start()
    inward[-1].wait()
    outward.append(pltpu.make_async_copy(held_v, out_v, sem.at[1, 6]))
    outward[-1].start()
    for one in outward:
        one.wait()


def chunk_tiles(chips):
    per = -(-220 // chips)
    return (per * 4 + 6) // 7, per - (per * 4 + 6) // 7


def solution(mesh):
    ngx, ny = mesh.shape["gx"], mesh.shape["gy"]
    nx, nz = (4, 8) if ngx == 64 else (1, ngx // 2)
    chips = ngx // 2
    per_a, per_b = chunk_tiles(chips)
    big_a, big_b = (per_a + 1) // 2, (per_b + 1) // 2

    def per_device(populations, mass, cell_type, bubble_id, slab_source, gas_density):
        vmem = pl.BlockSpec(memory_space=pltpu.VMEM)
        hbm = pl.BlockSpec(memory_space=pltpu.HBM)

        def tiles(count, dtype=F32):
            return pltpu.VMEM((count, 8, 128), dtype)

        g, m, v = pl.pallas_call(
            functools.partial(kernel, (nx, nz, ny)),
            out_shape=(
                jax.ShapeDtypeStruct((19, 10, 8, 128), F32),
                jax.ShapeDtypeStruct((30, 8, 128), F32),
                jax.ShapeDtypeStruct((1, BUBBLES), F32),
            ),
            in_specs=[hbm] * 6,
            out_specs=(hbm, vmem, vmem),
            scratch_shapes=[
                tiles(chips * (per_a + per_b) + 1),
                tiles(20, jnp.int32),
                pltpu.SMEM((ngx,), jnp.int32),
                pltpu.SMEM((BUBBLES,), F32),
                pltpu.VMEM((ngx, big_a, 8, 128), F32),
                pltpu.VMEM((ngx, big_b, 8, 128), F32),
                pltpu.VMEM((ngx, big_a, 8, 128), F32),
                pltpu.VMEM((ngx, big_b, 8, 128), F32),
                tiles(chips * (per_a + per_b)),
                pltpu.VMEM((ITERS, 4, 20, 56, 128), F32),
                pltpu.VMEM((4, 56, 128), F32),
                pltpu.VMEM((19, 10, 8, 128), F32),
                pltpu.VMEM((19, 10, 8, 128), F32),
                pltpu.VMEM((3, 10, 8, 128), F32),
                tiles(10, jnp.int32),
                tiles(10),
                tiles(10),
                tiles(10),
                tiles(10),
                tiles(10),
                tiles(10),
                pltpu.VMEM((ITERS, 2, 40, 128), F32),
                pltpu.VMEM((ITERS, 2, 3, 40, 128), F32),
                pltpu.VMEM((2, 56, 128), F32),
                pltpu.VMEM((2, 40, 128), F32),
                pltpu.VMEM((2, 3, 40, 128), F32),
                pltpu.VMEM((2, 56, 128), F32),
                pltpu.VMEM((ITERS, 1, 128), F32),
                pltpu.VMEM((ITERS, chips * ny, 1, 128), F32),
                pltpu.VMEM((ITERS, 2, 1, 128), F32),
                pltpu.SemaphoreType.DMA((6,)),
                pltpu.SemaphoreType.DMA((8 + ITERS * 8,)),
                pltpu.SemaphoreType.DMA((8 + ITERS * 8,)),
                pltpu.SemaphoreType.REGULAR,
            ],
            compiler_params=pltpu.CompilerParams(
                collective_id=0, has_side_effects=True, vmem_limit_bytes=VMEM_LIMIT
            ),
        )(
            populations.reshape(190, 8, 128),
            mass.reshape(10, 8, 128),
            cell_type.reshape(10, 8, 128),
            bubble_id.reshape(10, 8, 128),
            slab_source,
            gas_density,
        )
        anywhere = pl.BlockSpec(memory_space=pl.ANY)
        g, m, v = pl.pallas_call(
            hand_over,
            out_shape=(
                jax.ShapeDtypeStruct((19, 10, 8, 128), F32),
                jax.ShapeDtypeStruct((10, 8, 128), F32),
                jax.ShapeDtypeStruct((1, BUBBLES), F32),
            ),
            in_specs=[anywhere] * 3,
            out_specs=(hbm, hbm, hbm),
            scratch_shapes=[
                pltpu.VMEM((19, 10, 8, 128), F32),
                tiles(30),
                pltpu.VMEM((1, BUBBLES), F32),
                pltpu.SemaphoreType.DMA((2, 7)),
            ],
            compiler_params=pltpu.CompilerParams(vmem_limit_bytes=VMEM_LIMIT),
        )(g, m, v)
        return g.reshape(populations.shape), m.reshape(mass.shape), v.reshape(BUBBLES)

    return jax.shard_map(
        per_device,
        mesh=mesh,
        in_specs=(
            P(None, "gx", None, "gy"),
            P("gx", None, "gy"),
            P("gx", None, "gy"),
            P("gx", None, "gy"),
            P(),
            P(),
        ),
        out_specs=(P(None, "gx", None, "gy"), P("gx", None, "gy"), P()),
        check_vma=False,
    )
```

```python
import functools

import jax
import jax.numpy as jnp
from jax import lax
from jax.experimental import pallas as pl
from jax.experimental.pallas import tpu as pltpu
from jax.sharding import PartitionSpec as P

BUBBLES = 64
ITERS = 3
OMEGA = 1.6
VMEM_LIMIT = 56 * 2**20
MESH = pl.DeviceIdType.MESH
F32 = jnp.float32

LATTICE = (
    (0, 0, 0),
    (1, 0, 0),
    (-1, 0, 0),
    (0, 1, 0),
    (0, -1, 0),
    (0, 0, 1),
    (0, 0, -1),
    (1, 1, 0),
    (-1, -1, 0),
    (1, -1, 0),
    (-1, 1, 0),
    (1, 0, 1),
    (-1, 0, -1),
    (1, 0, -1),
    (-1, 0, 1),
    (0, 1, 1),
    (0, -1, -1),
    (0, 1, -1),
    (0, -1, 1),
)
HALF = 19
ORDER = (1, 7, 9, 11, 13, HALF, 2, 8, 10, 12, 14, 0, 3, 4, 5, 6, 15, 16, 17, 18)
AT = {field: pos for pos, field in enumerate(ORDER)}
COLS_UP = (3, 7, 10, 15, 17, HALF)
COLS_DOWN = (4, 8, 9, 16, 18, HALF)
PAIRS = ((1, 2), (3, 4), (5, 6), (7, 8), (9, 10), (11, 12), (13, 14), (15, 16), (17, 18))
PAD = 8


def pair_speeds(ux, uy, uz):
    return (ux, uy, uz, ux + uy, ux - uy, ux + uz, ux - uz, uy + uz, uy - uz)


def far_first(size):
    return sorted(range(size), key=lambda d: -min(d, size - d))


def kernel(
    shape,
    pop,
    mass,
    cell,
    label,
    source_in,
    density_in,
    out_g,
    out_m,
    out_v,
    stage,
    ints,
    source,
    gas_density,
    got_a,
    got_b,
    sorted_a,
    sorted_b,
    home,
    post,
    kinds,
    near,
    waiting,
    speed,
    bubble,
    fluid_mass,
    share,
    base_rho,
    gas_rho,
    gain,
    gas_here,
    cols_out,
    cols_in,
    cols,
    kind_cols_out,
    kind_cols_in,
    kind_cols,
    mate_sum,
    sums,
    part,
    fetch,
    send,
    recv,
    row_ready,
):
    nx, nz, ny = shape
    ngx = nx * nz * 2
    chips = nx * nz
    gx = lax.axis_index("gx")
    gy = lax.axis_index("gy")
    core = gx % 2
    chip = gx // 2
    pos_x = chip // nz
    pos_z = chip % nz
    mate = gx + 1 - 2 * core
    right = (gx + 1) % ngx
    left = (gx + ngx - 1) % ngx
    lane = lax.broadcasted_iota(jnp.int32, (8, 128), 1)

    SPREAD, GATHER, KINDS = 0, 2, 4

    def x_sem(step, side):
        return 8 + step * 8 + side

    def y_sem(step, side):
        return 8 + step * 8 + 2 + side

    def mate_sem(step):
        return 8 + step * 8 + 4

    def all_sem(step):
        return 8 + step * 8 + 5

    def remote(src, dst, sem, to_x, to_y):
        return pltpu.make_async_remote_copy(
            src_ref=src,
            dst_ref=dst,
            send_sem=send.at[sem],
            recv_sem=recv.at[sem],
            device_id=(to_x, to_y),
            device_id_type=MESH,
        )

    def wait_bytes(ref, sem):
        pltpu.make_async_copy(ref, ref, sem).wait()

    at_x = [lax.rem(pos_x + d, nx) * nz for d in range(nx)]
    at_z = [lax.rem(pos_z + d, nz) for d in range(nz)]
    at_y = [lax.rem(gy + d, ny) for d in range(ny)]
    far_chips = [(dz, dx) for dz in far_first(nz) for dx in far_first(nx)]
    peers = [
        (at_x[dx] + at_z[dz], other, dx == dz == 0 and other is core)
        for dz, dx in far_chips
        for other in (1 - core, core)
    ]

    def send_columns(out, into, sem, up_fields, down_fields):
        for z in range(5):
            up = jnp.zeros((8, 128), F32)
            down = jnp.zeros((8, 128), F32)
            for j, (high, low) in enumerate(zip(up_fields, down_fields)):
                for x in range(2):
                    spot = j * 4 + x + 1
                    at = pl.ds(PAD + z * 8, 8)
                    up = jnp.where(lane == spot, pltpu.roll(high(x + 1, at), spot + 1, 1), up)
                    down = jnp.where(lane == spot, pltpu.roll(low(x + 1, at), spot, 1), down)
            out[0, z * 8 : z * 8 + 8] = up
            out[1, z * 8 : z * 8 + 8] = down
        for side, there, to_y in ((0, gy < ny - 1, gy + 1), (1, gy > 0, gy - 1)):

            @pl.when(there)
            def _():
                for shift, to_x in ((-1, left), (0, gx), (1, right)):
                    remote(out.at[side], into.at[side, 1 - shift], sem + side, to_x, to_y).start()

    def wait_columns(into, whole, sem):
        for side, there in ((0, gy > 0), (1, gy < ny - 1)):

            @pl.when(there)
            def _():
                wait_bytes(into.at[side], recv.at[sem + side])

        slot = lane % 4
        for side in range(2):
            for z in range(5):
                of = pl.ds(z * 8, 8)
                before = pltpu.roll(into[side, 0, of], 126, 1)
                after = pltpu.roll(into[side, 2, of], 2, 1)
                whole[side, PAD + z * 8 : PAD + z * 8 + 8] = jnp.where(
                    slot == 0, before, jnp.where(slot == 3, after, into[side, 1, of])
                )

    def columns_sent(into, sem):
        for side, there in ((0, gy < ny - 1), (1, gy > 0)):

            @pl.when(there)
            def _():
                wait_bytes(into.at[side], send.at[sem + side])

    def post_columns(step):
        def fields(order):
            return [
                lambda slot, at, f=f: post[step, slot, AT[f], at] for f in order
            ]

        send_columns(
            cols_out.at[step], cols_in.at[step], y_sem(step, 0), fields(COLS_UP), fields(COLS_DOWN)
        )

    fetches = [
        pltpu.make_async_copy(src, dst, fetch.at[k])
        for k, (src, dst) in enumerate(
            (
                (cell, ints.at[0:10]),
                (label, ints.at[10:20]),
                (pop, stage.at[30:220]),
                (mass, stage.at[20:30]),
                (source_in, source),
                (density_in, gas_density),
            )
        )
    ]
    for one in fetches:
        one.start()

    barrier = pltpu.get_barrier_semaphore()

    for to_chip, to_core, near_by in peers:
        if not near_by:
            pl.semaphore_signal(
                barrier, inc=1, device_id=(to_chip * 2 + to_core, gy), device_id_type=MESH
            )
    for k in range(1, ny):
        pl.semaphore_signal(
            barrier, inc=1, device_id=(gx, (gy + k) % ny), device_id_type=MESH
        )

    walls = jnp.full((PAD, 128), -1.0, F32)
    for slot in range(4):
        kinds[slot, 0:PAD] = walls
        kinds[slot, PAD + 40 : PAD + 48] = walls
    for side in range(2):
        for edge in (cols, kind_cols):
            edge[side, 0:PAD] = walls
            edge[side, PAD + 40 : PAD + 48] = walls
    for one in fetches:
        one.wait()
    stage[0:20] = ints[...].astype(F32)
    pl.semaphore_wait(barrier, ngx - 1 + ny - 1)
    for k in range(1, ny):
        pl.semaphore_signal(
            row_ready, inc=1, device_id=(gx, (gy + k) % ny), device_id_type=MESH
        )

    chunks = []
    base = 0
    for per, got, pieces in zip(chunk_tiles(chips), (got_a, got_b), (sorted_a, sorted_b)):
        big = (per + 1) // 2
        chunks.append((base, per, big, ((0, big), (1, per - big)), got, pieces))
        base += per * chips

    def spread(which):
        base, per, big, sides, got, pieces = chunks[which]

        for own, _ in sides:

            @pl.when(core == own)
            def _():
                for dz, dx in far_chips:
                    to = at_x[dx] + at_z[dz]
                    for side, tiles in sides:
                        if dx == dz == 0 and side == own:
                            continue
                        remote(
                            stage.at[pl.ds(base + to * per + side * big, tiles)],
                            got.at[gx, pl.ds(0, tiles)],
                            SPREAD + which,
                            to * 2 + side,
                            gy,
                        ).start()

        got[gx] = stage[pl.ds(base + chip * per + core * big, big)]

    def pick(which):
        base, per, big, sides, got, pieces = chunks[which]
        for side, tiles in sides:

            @pl.when(core == side)
            def _():
                wait_bytes(got.at[pl.ds(0, ngx - 1), pl.ds(0, tiles)], recv.at[SPREAD + which])

        def one(k, carry):
            pieces[k] = got[source[k]]
            return carry

        lax.fori_loop(0, ngx, one, 0, unroll=8)

    def gather(which):
        base, per, big, sides, got, pieces = chunks[which]
        for side, tiles in sides:

            @pl.when(core == side)
            def _():
                at = pl.ds(base + chip * per + side * big, tiles)

                for dz, dx in far_chips:
                    for other in range(2):
                        if dx == dz == 0 and side == other:
                            continue
                        peer = (at_x[dx] + at_z[dz]) * 2 + other
                        remote(
                            pieces.at[peer, pl.ds(0, tiles)],
                            home.at[at],
                            GATHER + which,
                            peer,
                            gy,
                        ).start()
                home[at] = pieces[gx, 0:tiles]

    def gathered(which):
        base, per, big, sides, got, pieces = chunks[which]
        for side, tiles in sides:

            @pl.when(core == side)
            def _():
                wait_bytes(
                    home.at[pl.ds(base, chips * per - tiles)], recv.at[GATHER + which]
                )

    spread(0)
    spread(1)
    pick(0)
    gather(0)
    pick(1)
    gather(1)

    gathered(0)
    for x in range(2):
        for z in range(5):
            kinds[x + 1, PAD + z * 8 : PAD + z * 8 + 8] = home[x * 5 + z]
    rows = pl.ds(PAD, 40)
    kinds_right = remote(kinds.at[2, rows], kinds.at[0, rows], KINDS, right, gy)
    kinds_left = remote(kinds.at[1, rows], kinds.at[3, rows], KINDS + 1, left, gy)
    kinds_right.start()
    kinds_left.start()
    pl.semaphore_wait(row_ready, ny - 1)
    kind_fields = [lambda slot, at: kinds[slot, at]]
    send_columns(kind_cols_out, kind_cols_in, KINDS + 2, kind_fields, kind_fields)
    bubble[...] = home[10:20].astype(jnp.int32)
    fluid_mass[...] = home[20:30]

    def collide(step, i, g):
        x, z = i // 5, i % 5
        diff = [g[a] - g[b] for a, b in PAIRS]
        total = [g[a] + g[b] for a, b in PAIRS]
        faces = total[0] + total[1] + total[2]
        edges = (total[3] + total[4]) + (total[5] + total[6]) + (total[7] + total[8])
        rho = g[0] * (1.0 / 3.0) + faces * (1.0 / 18.0) + edges * (1.0 / 36.0)
        inv = 1.0 / rho
        ux = (diff[0] * (1.0 / 18.0) + (diff[3] + diff[4] + diff[5] + diff[6]) * (1.0 / 36.0)) * inv
        uy = (diff[1] * (1.0 / 18.0) + (diff[3] - diff[4] + diff[7] + diff[8]) * (1.0 / 36.0)) * inv
        uz = (diff[2] * (1.0 / 18.0) + (diff[5] - diff[6] + diff[7] - diff[8]) * (1.0 / 36.0)) * inv
        speed[0, i] = ux
        speed[1, i] = uy
        speed[2, i] = uz
        scaled = OMEGA * rho
        flat = scaled * (1.0 - 1.5 * (ux * ux + uy * uy + uz * uz))
        at = pl.ds(pl.multiple_of(PAD + z * 8, 8), 8)
        post[step, x + 1, AT[0], at] = flat + (1.0 - OMEGA) * g[0]
        square = 4.5 * scaled
        line = 3.0 * scaled
        for (a, b), along in zip(PAIRS, pair_speeds(ux, uy, uz)):
            even = flat + square * (along * along)
            odd = line * along
            post[step, x + 1, AT[a], at] = even + odd + (1.0 - OMEGA) * g[a]
            post[step, x + 1, AT[b], at] = even - odd + (1.0 - OMEGA) * g[b]
        return rho

    def put_half(step, i, value):
        x, z = i // 5, i % 5
        post[step, x + 1, AT[HALF], pl.ds(pl.multiple_of(PAD + z * 8, 8), 8)] = 0.5 * value

    def level(kind, liquid_mass, rho):
        phi = jnp.where(kind == 2.0, 1.0, jnp.where(kind == 1.0, liquid_mass / rho, 0.0))
        part_gas = jnp.where(kind == 0.0, 1.0, jnp.where(kind == 1.0, 1.0 - phi, 0.0))
        return phi, part_gas

    def send_faces(step):
        plus = remote(
            post.at[step, 2, pl.ds(0, 6), rows],
            post.at[step, 0, pl.ds(0, 6), rows],
            x_sem(step, 0),
            right,
            gy,
        )
        minus = remote(
            post.at[step, 1, pl.ds(5, 6), rows],
            post.at[step, 3, pl.ds(5, 6), rows],
            x_sem(step, 1),
            left,
            gy,
        )
        plus.start()
        minus.start()
        return plus, minus

    def shifted(value, cols, step_y, j, slot, at, outside):
        if step_y == 0:
            return value
        if step_y == 1:
            edge = pltpu.roll(cols[0, at], 128 - (j * 4 + slot), 1)
            if outside is not None:
                edge = jnp.where(outside[0], -1.0, edge)
            return jnp.where(lane == 0, edge, pltpu.roll(value, 1, 1))
        edge = pltpu.roll(cols[1, at], 127 - (j * 4 + slot), 1)
        if outside is not None:
            edge = jnp.where(outside[1], -1.0, edge)
        return jnp.where(lane == 127, edge, pltpu.roll(value, 127, 1))

    def find_near(i, carry):
        x, z = i // 5, i % 5
        row = PAD + z * 8
        for d in range(1, 19):
            step_x, step_y, step_z = LATTICE[d]
            slot = x + 1 - step_x
            at = pl.ds(row - step_z, 8)
            near[d, i] = shifted(
                kinds[slot, at], kind_cols, step_y, 0, slot, at, (gy == 0, gy == ny - 1)
            )
        return carry

    def twice_even(i):
        ux, uy, uz = speed[0, i], speed[1, i], speed[2, i]
        flat = 2.0 - 3.0 * (ux * ux + uy * uy + uz * uz)
        return [flat + 9.0 * (along * along) for along in pair_speeds(ux, uy, uz)]

    def stream(step, i):
        x, z = i // 5, i % 5
        row = PAD + z * 8
        own = pl.ds(pl.multiple_of(row, 8), 8)
        half = post[step, x + 1, AT[HALF], own]
        rest = post[step, x + 1, AT[0], own]
        waiting[0, i] = rest
        zero = jnp.zeros((8, 128), F32)
        rho_sum = [zero, zero]
        gas_sum = [zero, zero]
        gain_sum = [zero, zero]
        for k, ((a, b), even) in enumerate(zip(PAIRS, twice_even(i))):
            kind_of = 0 if k < 3 else 1
            here = {a: post[step, x + 1, AT[a], own], b: post[step, x + 1, AT[b], own]}
            for d, back in ((a, b), (b, a)):
                step_x, step_y, step_z = LATTICE[d]
                slot = x + 1 - step_x
                at = pl.ds(row - step_z, 8)
                j = 0 if step_y == 0 else (COLS_UP if step_y == 1 else COLS_DOWN).index(d)
                came = shifted(post[step, slot, AT[d], at], cols, step_y, j, slot, at, None)
                near_half = shifted(post[step, slot, AT[HALF], at], cols, step_y, 5, slot, at, None)
                kind = near[d, i]
                bounced = here[back]
                value = jnp.where(kind >= 1.0, came, bounced)
                gas = kind == 0.0
                known = jnp.where(gas, -bounced, value)
                waiting[d, i] = known
                rho_sum[kind_of] = rho_sum[kind_of] + known
                gas_sum[kind_of] = gas_sum[kind_of] + jnp.where(gas, even, 0.0)
                part_of = jnp.where(
                    kind == 2.0, 1.0, jnp.where(kind == 1.0, half + near_half, 0.0)
                )
                gain_sum[kind_of] = gain_sum[kind_of] + part_of * (value - bounced)
        base_rho[i] = (
            rest * (1.0 / 3.0) + rho_sum[0] * (1.0 / 18.0) + rho_sum[1] * (1.0 / 36.0)
        )
        gas_rho[i] = gas_sum[0] * (1.0 / 18.0) + gas_sum[1] * (1.0 / 36.0)
        gain[i] = gain_sum[0] * (1.0 / 18.0) + gain_sum[1] * (1.0 / 36.0)

    def arrived(i):
        density = gas_here[i]
        g = [waiting[0, i]] + [None] * 18
        for (a, b), even in zip(PAIRS, twice_even(i)):
            lift = density * even
            for d in (a, b):
                known = waiting[d, i]
                g[d] = jnp.where(near[d, i] == 0.0, known + lift, known)
        return g

    def lookup(table):
        def one(i, carry):
            gas_here[i] = jnp.take_along_axis(
                table, bubble[i], axis=1, mode="promise_in_bounds"
            )
            return carry

        lax.fori_loop(0, 10, one, 0, unroll=5)

    def member_sums():
        labels = [bubble[i] for i in range(10)]
        shares = [share[i] for i in range(10)]

        def one(b):
            parts = [jnp.where(which == b, part_of, 0.0) for which, part_of in zip(labels, shares)]
            while len(parts) > 1:
                parts = [sum(parts[k : k + 2]) for k in range(0, len(parts), 2)]
            return parts[0]

        def merged(bits, b):
            if bits == 0:
                return one(b)
            bit = bits - 1
            first, second = merged(bit, b), merged(bit, b + (1 << bit))
            odd = (lane >> bit) & 1 == 1
            keep = jnp.where(odd, second, first)
            move = jnp.where(odd, first, second)
            return keep + pltpu.roll(move, 128 - (1 << bit), 1)

        now = merged(6, 0)
        return now + pltpu.roll(now, 64, 1)

    def begin_sum(step, value):
        part[step, 0] = jnp.sum(value, axis=0, keepdims=True)
        remote(part.at[step, 0], mate_sum.at[step], mate_sem(step), mate, gy).start()

    def middle_sum(step):
        wait_bytes(mate_sum.at[step], recv.at[mate_sem(step)])
        value = part[step, 0] + mate_sum[step]
        part[step, 1] = value
        mine = chip * ny + gy
        sums[step, mine] = value

        for dz, dx in far_chips:
            to_x = (at_x[dx] + at_z[dz]) * 2 + core
            for dy in far_first(ny):
                if dx == dy == dz == 0:
                    continue
                remote(
                    part.at[step, 1], sums.at[step, mine], all_sem(step), to_x, at_y[dy]
                ).start()

    def end_sum(step):
        wait_bytes(sums.at[step, pl.ds(0, chips * ny - 1)], recv.at[all_sem(step)])
        return jnp.broadcast_to(jnp.sum(sums[step], axis=0), (8, 128))

    def first(i, carry):
        rho = collide(0, i, [home[30 + q * 10 + i] for q in range(19)])
        kind = home[i]
        phi, part_gas = level(kind, fluid_mass[i], rho)
        put_half(0, i, phi)
        share[i] = part_gas
        return carry

    bubble_lane = lane & (BUBBLES - 1)
    table = jnp.zeros((8, 128), F32)
    for b in range(BUBBLES):
        table = jnp.where(bubble_lane == b, gas_density[b], table)
    density_start = table
    lookup(table)

    gathered(1)
    lax.fori_loop(0, 10, first, 0, unroll=5)
    post_columns(0)
    faces = send_faces(0)
    started = [faces]
    kinds_right.wait_recv()
    kinds_left.wait_recv()
    wait_columns(kind_cols_in, kind_cols, KINDS + 2)
    lax.fori_loop(0, 10, find_near, 0, unroll=5)
    volume_start = member_sums()
    wait_columns(cols_in.at[0], cols, y_sem(0, 0))
    for face in faces:
        face.wait_recv()

    def stream_all(step):
        def one(i, carry):
            stream(step, i)
            return carry

        lax.fori_loop(0, 10, one, 0, unroll=5)

    stream_all(0)
    start_total = None
    for step in range(ITERS):

        def settle(i, carry):
            kind = home[i]
            rho = base_rho[i] + gas_here[i] * gas_rho[i]
            liquid_mass = jnp.where(
                kind == 1.0, fluid_mass[i] + gain[i], jnp.where(kind == 2.0, rho, 0.0)
            )
            fluid_mass[i] = liquid_mass
            phi, part_gas = level(kind, liquid_mass, rho)
            if step < ITERS - 1:
                put_half(step + 1, i, phi)
            share[i] = part_gas
            return carry

        lax.fori_loop(0, 10, settle, 0, unroll=5)
        volume = member_sums()
        if step == 0:
            volume = jnp.where(lane < BUBBLES, volume, volume_start)
        begin_sum(step, volume)

        if step < ITERS - 1:

            def again(i, carry):
                collide(step + 1, i, arrived(i))
                return carry

            middle_sum(step)
            lax.fori_loop(0, 10, again, 0)
            post_columns(step + 1)
            faces = send_faces(step + 1)
            started.append(faces)
            wait_columns(cols_in.at[step + 1], cols, y_sem(step + 1, 0))
            for face in faces:
                face.wait_recv()
            stream_all(step + 1)
        else:

            def last(i, carry):
                for q, value in enumerate(arrived(i)):
                    waiting[q, i] = value
                return carry

            middle_sum(step)
            lax.fori_loop(0, 10, last, 0)
            store_g = pltpu.make_async_copy(waiting, out_g, fetch.at[0])
            store_g.start()
        total = end_sum(step)
        if step == 0:
            other = pltpu.roll(total, 64, 1)
            start_total = jnp.where(lane < BUBBLES, other, total)
            total = jnp.where(lane < BUBBLES, total, other)
        lookup(density_start * start_total / total)

    out_m[0:10] = fluid_mass[...]
    out_m[10:20] = home[0:10]
    out_m[20:30] = gas_here[...]
    out_v[...] = total[0:1, :BUBBLES] * (BUBBLES / (ngx * ny * 2 * 40 * 128))

    store_g.wait()
    for which in range(2):
        base, per, big, sides, got, pieces = chunks[which]
        for side, tiles in sides:

            @pl.when(core == side)
            def _():
                wait_bytes(stage.at[pl.ds(0, chips * per - tiles)], send.at[SPREAD + which])
                wait_bytes(
                    pieces.at[pl.ds(0, ngx - 1), pl.ds(0, tiles)], send.at[GATHER + which]
                )

    kinds_right.wait_send()
    kinds_left.wait_send()
    columns_sent(kind_cols_in, KINDS + 2)
    for step in range(ITERS):
        for face in started[step]:
            face.wait_send()
        columns_sent(cols_in.at[step], y_sem(step, 0))
        wait_bytes(mate_sum.at[step], send.at[mate_sem(step)])
        wait_bytes(sums.at[step, pl.ds(0, chips * ny - 1)], send.at[all_sem(step)])


def hand_over(g, m, v, out_g, out_m, out_v, held_g, held_m, held_v, sem):
    cuts = (0, 4, 8, 12, 16, 19)
    groups = [pl.ds(a, b - a) for a, b in zip(cuts, cuts[1:])]
    inward = [pltpu.make_async_copy(m, held_m, sem.at[0, 5])]
    inward += [
        pltpu.make_async_copy(g.at[at], held_g.at[at], sem.at[0, k])
        for k, at in enumerate(groups)
    ]
    inward.append(pltpu.make_async_copy(v, held_v, sem.at[0, 6]))
    for one in inward:
        one.start()
    inward[0].wait()
    outward = [pltpu.make_async_copy(held_m.at[0:10], out_m, sem.at[1, 5])]
    outward[0].start()
    gas = held_m[10:20] == 0.0
    density = held_m[20:30]
    for k, (a, b) in enumerate(zip(cuts, cuts[1:])):
        inward[k + 1].wait()
        for q in range(a, b):
            held_g[q] = jnp.where(gas, density, held_g[q])
        outward.append(
            pltpu.make_async_copy(held_g.at[groups[k]], out_g.at[groups[k]], sem.at[1, k])
        )
        outward[-1].start()
    inward[-1].wait()
    outward.append(pltpu.make_async_copy(held_v, out_v, sem.at[1, 6]))
    outward[-1].start()
    for one in outward:
        one.wait()


def chunk_tiles(chips):
    per = -(-220 // chips)
    return (per * 4 + 6) // 7, per - (per * 4 + 6) // 7


def solution(mesh):
    ngx, ny = mesh.shape["gx"], mesh.shape["gy"]
    nx, nz = (4, 8) if ngx == 64 else (1, ngx // 2)
    chips = ngx // 2
    per_a, per_b = chunk_tiles(chips)
    big_a, big_b = (per_a + 1) // 2, (per_b + 1) // 2

    def per_device(populations, mass, cell_type, bubble_id, slab_source, gas_density):
        vmem = pl.BlockSpec(memory_space=pltpu.VMEM)
        hbm = pl.BlockSpec(memory_space=pltpu.HBM)

        def tiles(count, dtype=F32):
            return pltpu.VMEM((count, 8, 128), dtype)

        g, m, v = pl.pallas_call(
            functools.partial(kernel, (nx, nz, ny)),
            out_shape=(
                jax.ShapeDtypeStruct((19, 10, 8, 128), F32),
                jax.ShapeDtypeStruct((30, 8, 128), F32),
                jax.ShapeDtypeStruct((1, BUBBLES), F32),
            ),
            in_specs=[hbm] * 6,
            out_specs=(hbm, vmem, vmem),
            scratch_shapes=[
                tiles(chips * (per_a + per_b) + 1),
                tiles(20, jnp.int32),
                pltpu.SMEM((ngx,), jnp.int32),
                pltpu.SMEM((BUBBLES,), F32),
                pltpu.VMEM((ngx, big_a, 8, 128), F32),
                pltpu.VMEM((ngx, big_b, 8, 128), F32),
                pltpu.VMEM((ngx, big_a, 8, 128), F32),
                pltpu.VMEM((ngx, big_b, 8, 128), F32),
                tiles(chips * (per_a + per_b)),
                pltpu.VMEM((ITERS, 4, 20, 56, 128), F32),
                pltpu.VMEM((4, 56, 128), F32),
                pltpu.VMEM((19, 10, 8, 128), F32),
                pltpu.VMEM((19, 10, 8, 128), F32),
                pltpu.VMEM((3, 10, 8, 128), F32),
                tiles(10, jnp.int32),
                tiles(10),
                tiles(10),
                tiles(10),
                tiles(10),
                tiles(10),
                tiles(10),
                pltpu.VMEM((ITERS, 2, 40, 128), F32),
                pltpu.VMEM((ITERS, 2, 3, 40, 128), F32),
                pltpu.VMEM((2, 56, 128), F32),
                pltpu.VMEM((2, 40, 128), F32),
                pltpu.VMEM((2, 3, 40, 128), F32),
                pltpu.VMEM((2, 56, 128), F32),
                pltpu.VMEM((ITERS, 1, 128), F32),
                pltpu.VMEM((ITERS, chips * ny, 1, 128), F32),
                pltpu.VMEM((ITERS, 2, 1, 128), F32),
                pltpu.SemaphoreType.DMA((6,)),
                pltpu.SemaphoreType.DMA((8 + ITERS * 8,)),
                pltpu.SemaphoreType.DMA((8 + ITERS * 8,)),
                pltpu.SemaphoreType.REGULAR,
            ],
            compiler_params=pltpu.CompilerParams(
                collective_id=0, has_side_effects=True, vmem_limit_bytes=VMEM_LIMIT
            ),
        )(
            populations.reshape(190, 8, 128),
            mass.reshape(10, 8, 128),
            cell_type.reshape(10, 8, 128),
            bubble_id.reshape(10, 8, 128),
            slab_source,
            gas_density,
        )
        anywhere = pl.BlockSpec(memory_space=pl.ANY)
        g, m, v = pl.pallas_call(
            hand_over,
            out_shape=(
                jax.ShapeDtypeStruct((19, 10, 8, 128), F32),
                jax.ShapeDtypeStruct((10, 8, 128), F32),
                jax.ShapeDtypeStruct((1, BUBBLES), F32),
            ),
            in_specs=[anywhere] * 3,
            out_specs=(hbm, hbm, hbm),
            scratch_shapes=[
                pltpu.VMEM((19, 10, 8, 128), F32),
                tiles(30),
                pltpu.VMEM((1, BUBBLES), F32),
                pltpu.SemaphoreType.DMA((2, 7)),
            ],
            compiler_params=pltpu.CompilerParams(vmem_limit_bytes=VMEM_LIMIT),
        )(g, m, v)
        return g.reshape(populations.shape), m.reshape(mass.shape), v.reshape(BUBBLES)

    return jax.shard_map(
        per_device,
        mesh=mesh,
        in_specs=(
            P(None, "gx", None, "gy"),
            P("gx", None, "gy"),
            P("gx", None, "gy"),
            P("gx", None, "gy"),
            P(),
            P(),
        ),
        out_specs=(P(None, "gx", None, "gy"), P("gx", None, "gy"), P()),
        check_vma=False,
    )
```

```python
import functools

import jax
import jax.numpy as jnp
from jax import lax
from jax.experimental import pallas as pl
from jax.experimental.pallas import tpu as pltpu
from jax.sharding import PartitionSpec as P

BUBBLES = 64
ITERS = 3
OMEGA = 1.6
VMEM_LIMIT = 56 * 2**20
MESH = pl.DeviceIdType.MESH
F32 = jnp.float32

LATTICE = (
    (0, 0, 0),
    (1, 0, 0),
    (-1, 0, 0),
    (0, 1, 0),
    (0, -1, 0),
    (0, 0, 1),
    (0, 0, -1),
    (1, 1, 0),
    (-1, -1, 0),
    (1, -1, 0),
    (-1, 1, 0),
    (1, 0, 1),
    (-1, 0, -1),
    (1, 0, -1),
    (-1, 0, 1),
    (0, 1, 1),
    (0, -1, -1),
    (0, 1, -1),
    (0, -1, 1),
)
HALF = 19
ORDER = (1, 7, 9, 11, 13, HALF, 2, 8, 10, 12, 14, 0, 3, 4, 5, 6, 15, 16, 17, 18)
AT = {field: pos for pos, field in enumerate(ORDER)}
COLS_UP = (3, 7, 10, 15, 17, HALF)
COLS_DOWN = (4, 8, 9, 16, 18, HALF)
PAIRS = ((1, 2), (3, 4), (5, 6), (7, 8), (9, 10), (11, 12), (13, 14), (15, 16), (17, 18))
PAD = 8


def pair_speeds(ux, uy, uz):
    return (ux, uy, uz, ux + uy, ux - uy, ux + uz, ux - uz, uy + uz, uy - uz)


def far_first(size):
    return sorted(range(size), key=lambda d: -min(d, size - d))


def kernel(
    shape,
    pop,
    mass,
    cell,
    label,
    source_in,
    density_in,
    out_g,
    out_m,
    out_v,
    stage,
    ints,
    source,
    gas_density,
    got_a,
    got_b,
    sorted_a,
    sorted_b,
    home,
    post,
    kinds,
    near,
    waiting,
    speed,
    bubble,
    fluid_mass,
    share,
    base_rho,
    gas_rho,
    gain,
    gas_here,
    cols_out,
    cols_in,
    cols,
    kind_cols_out,
    kind_cols_in,
    kind_cols,
    mate_sum,
    sums,
    part,
    fetch,
    send,
    recv,
    row_ready,
):
    nx, nz, ny = shape
    ngx = nx * nz * 2
    chips = nx * nz
    gx = lax.axis_index("gx")
    gy = lax.axis_index("gy")
    core = gx % 2
    chip = gx // 2
    pos_x = chip // nz
    pos_z = chip % nz
    mate = gx + 1 - 2 * core
    right = (gx + 1) % ngx
    left = (gx + ngx - 1) % ngx
    lane = lax.broadcasted_iota(jnp.int32, (8, 128), 1)

    SPREAD, GATHER, KINDS = 0, 2, 4

    def x_sem(step, side):
        return 8 + step * 8 + side

    def y_sem(step, side):
        return 8 + step * 8 + 2 + side

    def mate_sem(step):
        return 8 + step * 8 + 4

    def all_sem(step):
        return 8 + step * 8 + 5

    def remote(src, dst, sem, to_x, to_y):
        return pltpu.make_async_remote_copy(
            src_ref=src,
            dst_ref=dst,
            send_sem=send.at[sem],
            recv_sem=recv.at[sem],
            device_id=(to_x, to_y),
            device_id_type=MESH,
        )

    def wait_bytes(ref, sem):
        pltpu.make_async_copy(ref, ref, sem).wait()

    at_x = [lax.rem(pos_x + d, nx) * nz for d in range(nx)]
    at_z = [lax.rem(pos_z + d, nz) for d in range(nz)]
    at_y = [lax.rem(gy + d, ny) for d in range(ny)]
    far_chips = [(dz, dx) for dz in far_first(nz) for dx in far_first(nx)]
    peers = [
        (at_x[dx] + at_z[dz], other, dx == dz == 0 and other is core)
        for dz, dx in far_chips
        for other in (1 - core, core)
    ]

    def send_columns(out, into, sem, up_fields, down_fields):
        for z in range(5):
            up = jnp.zeros((8, 128), F32)
            down = jnp.zeros((8, 128), F32)
            for j, (high, low) in enumerate(zip(up_fields, down_fields)):
                for x in range(2):
                    spot = j * 4 + x + 1
                    at = pl.ds(PAD + z * 8, 8)
                    up = jnp.where(lane == spot, pltpu.roll(high(x + 1, at), spot + 1, 1), up)
                    down = jnp.where(lane == spot, pltpu.roll(low(x + 1, at), spot, 1), down)
            out[0, z * 8 : z * 8 + 8] = up
            out[1, z * 8 : z * 8 + 8] = down
        for side, there, to_y in ((0, gy < ny - 1, gy + 1), (1, gy > 0, gy - 1)):

            @pl.when(there)
            def _():
                for shift, to_x in ((-1, left), (0, gx), (1, right)):
                    remote(out.at[side], into.at[side, 1 - shift], sem + side, to_x, to_y).start()

    def wait_columns(into, whole, sem):
        for side, there in ((0, gy > 0), (1, gy < ny - 1)):

            @pl.when(there)
            def _():
                wait_bytes(into.at[side], recv.at[sem + side])

        slot = lane % 4
        for side in range(2):
            for z in range(5):
                of = pl.ds(z * 8, 8)
                before = pltpu.roll(into[side, 0, of], 126, 1)
                after = pltpu.roll(into[side, 2, of], 2, 1)
                whole[side, PAD + z * 8 : PAD + z * 8 + 8] = jnp.where(
                    slot == 0, before, jnp.where(slot == 3, after, into[side, 1, of])
                )

    def columns_sent(into, sem):
        for side, there in ((0, gy < ny - 1), (1, gy > 0)):

            @pl.when(there)
            def _():
                wait_bytes(into.at[side], send.at[sem + side])

    def post_columns(step):
        def fields(order):
            return [
                lambda slot, at, f=f: post[step, slot, AT[f], at] for f in order
            ]

        send_columns(
            cols_out.at[step], cols_in.at[step], y_sem(step, 0), fields(COLS_UP), fields(COLS_DOWN)
        )

    fetches = [
        pltpu.make_async_copy(src, dst, fetch.at[k])
        for k, (src, dst) in enumerate(
            (
                (cell, ints.at[0:10]),
                (label, ints.at[10:20]),
                (pop, stage.at[30:220]),
                (mass, stage.at[20:30]),
                (source_in, source),
                (density_in, gas_density),
            )
        )
    ]
    for one in fetches:
        one.start()

    barrier = pltpu.get_barrier_semaphore()

    for to_chip, to_core, near_by in peers:
        if not near_by:
            pl.semaphore_signal(
                barrier, inc=1, device_id=(to_chip * 2 + to_core, gy), device_id_type=MESH
            )
    for k in range(1, ny):
        pl.semaphore_signal(
            barrier, inc=1, device_id=(gx, (gy + k) % ny), device_id_type=MESH
        )

    walls = jnp.full((PAD, 128), -1.0, F32)
    for slot in range(4):
        kinds[slot, 0:PAD] = walls
        kinds[slot, PAD + 40 : PAD + 48] = walls
    for side in range(2):
        for edge in (cols, kind_cols):
            edge[side, 0:PAD] = walls
            edge[side, PAD + 40 : PAD + 48] = walls
    for one in fetches:
        one.wait()
    stage[0:20] = ints[...].astype(F32)
    pl.semaphore_wait(barrier, ngx - 1 + ny - 1)
    for k in range(1, ny):
        pl.semaphore_signal(
            row_ready, inc=1, device_id=(gx, (gy + k) % ny), device_id_type=MESH
        )

    chunks = []
    base = 0
    for per, got, pieces in zip(chunk_tiles(chips), (got_a, got_b), (sorted_a, sorted_b)):
        big = (per + 1) // 2
        chunks.append((base, per, big, ((0, big), (1, per - big)), got, pieces))
        base += per * chips

    def spread(which):
        base, per, big, sides, got, pieces = chunks[which]

        for own, _ in sides:

            @pl.when(core == own)
            def _():
                for dz, dx in far_chips:
                    to = at_x[dx] + at_z[dz]
                    for side, tiles in sides:
                        if dx == dz == 0 and side == own:
                            continue
                        remote(
                            stage.at[pl.ds(base + to * per + side * big, tiles)],
                            got.at[gx, pl.ds(0, tiles)],
                            SPREAD + which,
                            to * 2 + side,
                            gy,
                        ).start()

        got[gx] = stage[pl.ds(base + chip * per + core * big, big)]

    def pick(which):
        base, per, big, sides, got, pieces = chunks[which]
        for side, tiles in sides:

            @pl.when(core == side)
            def _():
                wait_bytes(got.at[pl.ds(0, ngx - 1), pl.ds(0, tiles)], recv.at[SPREAD + which])

        def one(k, carry):
            pieces[k] = got[source[k]]
            return carry

        lax.fori_loop(0, ngx, one, 0, unroll=8)

    def gather(which):
        base, per, big, sides, got, pieces = chunks[which]
        for side, tiles in sides:

            @pl.when(core == side)
            def _():
                at = pl.ds(base + chip * per + side * big, tiles)

                for dz, dx in far_chips:
                    for other in range(2):
                        if dx == dz == 0 and side == other:
                            continue
                        peer = (at_x[dx] + at_z[dz]) * 2 + other
                        remote(
                            pieces.at[peer, pl.ds(0, tiles)],
                            home.at[at],
                            GATHER + which,
                            peer,
                            gy,
                        ).start()
                home[at] = pieces[gx, 0:tiles]

    def gathered(which):
        base, per, big, sides, got, pieces = chunks[which]
        for side, tiles in sides:

            @pl.when(core == side)
            def _():
                wait_bytes(
                    home.at[pl.ds(base, chips * per - tiles)], recv.at[GATHER + which]
                )

    spread(0)
    spread(1)
    pick(0)
    gather(0)
    pick(1)
    gather(1)

    gathered(0)
    for x in range(2):
        for z in range(5):
            kinds[x + 1, PAD + z * 8 : PAD + z * 8 + 8] = home[x * 5 + z]
    rows = pl.ds(PAD, 40)
    kinds_right = remote(kinds.at[2, rows], kinds.at[0, rows], KINDS, right, gy)
    kinds_left = remote(kinds.at[1, rows], kinds.at[3, rows], KINDS + 1, left, gy)
    kinds_right.start()
    kinds_left.start()
    pl.semaphore_wait(row_ready, ny - 1)
    kind_fields = [lambda slot, at: kinds[slot, at]]
    send_columns(kind_cols_out, kind_cols_in, KINDS + 2, kind_fields, kind_fields)
    bubble[...] = home[10:20].astype(jnp.int32)
    fluid_mass[...] = home[20:30]

    def collide(step, i, g):
        x, z = i // 5, i % 5
        diff = [g[a] - g[b] for a, b in PAIRS]
        total = [g[a] + g[b] for a, b in PAIRS]
        faces = total[0] + total[1] + total[2]
        edges = (total[3] + total[4]) + (total[5] + total[6]) + (total[7] + total[8])
        rho = g[0] * (1.0 / 3.0) + faces * (1.0 / 18.0) + edges * (1.0 / 36.0)
        inv = 1.0 / rho
        ux = (diff[0] * (1.0 / 18.0) + (diff[3] + diff[4] + diff[5] + diff[6]) * (1.0 / 36.0)) * inv
        uy = (diff[1] * (1.0 / 18.0) + (diff[3] - diff[4] + diff[7] + diff[8]) * (1.0 / 36.0)) * inv
        uz = (diff[2] * (1.0 / 18.0) + (diff[5] - diff[6] + diff[7] - diff[8]) * (1.0 / 36.0)) * inv
        speed[0, i] = ux
        speed[1, i] = uy
        speed[2, i] = uz
        scaled = OMEGA * rho
        flat = scaled * (1.0 - 1.5 * (ux * ux + uy * uy + uz * uz))
        at = pl.ds(pl.multiple_of(PAD + z * 8, 8), 8)
        post[step, x + 1, AT[0], at] = flat + (1.0 - OMEGA) * g[0]
        square = 4.5 * scaled
        line = 3.0 * scaled
        for (a, b), along in zip(PAIRS, pair_speeds(ux, uy, uz)):
            even = flat + square * (along * along)
            odd = line * along
            post[step, x + 1, AT[a], at] = even + odd + (1.0 - OMEGA) * g[a]
            post[step, x + 1, AT[b], at] = even - odd + (1.0 - OMEGA) * g[b]
        return rho

    def put_half(step, i, value):
        x, z = i // 5, i % 5
        post[step, x + 1, AT[HALF], pl.ds(pl.multiple_of(PAD + z * 8, 8), 8)] = 0.5 * value

    def level(kind, liquid_mass, rho):
        phi = jnp.where(kind == 2.0, 1.0, jnp.where(kind == 1.0, liquid_mass / rho, 0.0))
        part_gas = jnp.where(kind == 0.0, 1.0, jnp.where(kind == 1.0, 1.0 - phi, 0.0))
        return phi, part_gas

    def send_faces(step):
        plus = remote(
            post.at[step, 2, pl.ds(0, 6), rows],
            post.at[step, 0, pl.ds(0, 6), rows],
            x_sem(step, 0),
            right,
            gy,
        )
        minus = remote(
            post.at[step, 1, pl.ds(5, 6), rows],
            post.at[step, 3, pl.ds(5, 6), rows],
            x_sem(step, 1),
            left,
            gy,
        )
        plus.start()
        minus.start()
        return plus, minus

    def shifted(value, cols, step_y, j, slot, at, outside):
        if step_y == 0:
            return value
        if step_y == 1:
            edge = pltpu.roll(cols[0, at], 128 - (j * 4 + slot), 1)
            if outside is not None:
                edge = jnp.where(outside[0], -1.0, edge)
            return jnp.where(lane == 0, edge, pltpu.roll(value, 1, 1))
        edge = pltpu.roll(cols[1, at], 127 - (j * 4 + slot), 1)
        if outside is not None:
            edge = jnp.where(outside[1], -1.0, edge)
        return jnp.where(lane == 127, edge, pltpu.roll(value, 127, 1))

    def find_near(i, carry):
        x, z = i // 5, i % 5
        row = PAD + z * 8
        for d in range(1, 19):
            step_x, step_y, step_z = LATTICE[d]
            slot = x + 1 - step_x
            at = pl.ds(row - step_z, 8)
            near[d, i] = shifted(
                kinds[slot, at], kind_cols, step_y, 0, slot, at, (gy == 0, gy == ny - 1)
            )
        return carry

    def twice_even(i):
        ux, uy, uz = speed[0, i], speed[1, i], speed[2, i]
        flat = 2.0 - 3.0 * (ux * ux + uy * uy + uz * uz)
        return [flat + 9.0 * (along * along) for along in pair_speeds(ux, uy, uz)]

    def stream(step, i):
        x, z = i // 5, i % 5
        row = PAD + z * 8
        own = pl.ds(pl.multiple_of(row, 8), 8)
        half = post[step, x + 1, AT[HALF], own]
        rest = post[step, x + 1, AT[0], own]
        waiting[0, i] = rest
        zero = jnp.zeros((8, 128), F32)
        rho_sum = [zero, zero]
        gas_sum = [zero, zero]
        gain_sum = [zero, zero]
        for k, ((a, b), even) in enumerate(zip(PAIRS, twice_even(i))):
            kind_of = 0 if k < 3 else 1
            here = {a: post[step, x + 1, AT[a], own], b: post[step, x + 1, AT[b], own]}
            for d, back in ((a, b), (b, a)):
                step_x, step_y, step_z = LATTICE[d]
                slot = x + 1 - step_x
                at = pl.ds(row - step_z, 8)
                j = 0 if step_y == 0 else (COLS_UP if step_y == 1 else COLS_DOWN).index(d)
                came = shifted(post[step, slot, AT[d], at], cols, step_y, j, slot, at, None)
                near_half = shifted(post[step, slot, AT[HALF], at], cols, step_y, 5, slot, at, None)
                kind = near[d, i]
                bounced = here[back]
                value = jnp.where(kind >= 1.0, came, bounced)
                gas = kind == 0.0
                known = jnp.where(gas, -bounced, value)
                waiting[d, i] = known
                rho_sum[kind_of] = rho_sum[kind_of] + known
                gas_sum[kind_of] = gas_sum[kind_of] + jnp.where(gas, even, 0.0)
                part_of = jnp.where(
                    kind == 2.0, 1.0, jnp.where(kind == 1.0, half + near_half, 0.0)
                )
                gain_sum[kind_of] = gain_sum[kind_of] + part_of * (value - bounced)
        base_rho[i] = (
            rest * (1.0 / 3.0) + rho_sum[0] * (1.0 / 18.0) + rho_sum[1] * (1.0 / 36.0)
        )
        gas_rho[i] = gas_sum[0] * (1.0 / 18.0) + gas_sum[1] * (1.0 / 36.0)
        gain[i] = gain_sum[0] * (1.0 / 18.0) + gain_sum[1] * (1.0 / 36.0)

    def arrived(i):
        density = gas_here[i]
        g = [waiting[0, i]] + [None] * 18
        for (a, b), even in zip(PAIRS, twice_even(i)):
            lift = density * even
            for d in (a, b):
                known = waiting[d, i]
                g[d] = jnp.where(near[d, i] == 0.0, known + lift, known)
        return g

    def lookup(table):
        def one(i, carry):
            gas_here[i] = jnp.take_along_axis(
                table, bubble[i], axis=1, mode="promise_in_bounds"
            )
            return carry

        lax.fori_loop(0, 10, one, 0, unroll=5)

    def member_sums():
        labels = [bubble[i] for i in range(10)]
        shares = [share[i] for i in range(10)]

        def one(b):
            parts = [jnp.where(which == b, part_of, 0.0) for which, part_of in zip(labels, shares)]
            while len(parts) > 1:
                parts = [sum(parts[k : k + 2]) for k in range(0, len(parts), 2)]
            return parts[0]

        def merged(bits, b):
            if bits == 0:
                return one(b)
            bit = bits - 1
            first, second = merged(bit, b), merged(bit, b + (1 << bit))
            odd = (lane >> bit) & 1 == 1
            keep = jnp.where(odd, second, first)
            move = jnp.where(odd, first, second)
            return keep + pltpu.roll(move, 128 - (1 << bit), 1)

        now = merged(6, 0)
        return now + pltpu.roll(now, 64, 1)

    def begin_sum(step, value):
        part[step, 0] = jnp.sum(value, axis=0, keepdims=True)
        remote(part.at[step, 0], mate_sum.at[step], mate_sem(step), mate, gy).start()

    def middle_sum(step):
        wait_bytes(mate_sum.at[step], recv.at[mate_sem(step)])
        value = part[step, 0] + mate_sum[step]
        part[step, 1] = value
        mine = chip * ny + gy
        sums[step, mine] = value

        for dz, dx in far_chips:
            to_x = (at_x[dx] + at_z[dz]) * 2 + core
            for dy in far_first(ny):
                if dx == dy == dz == 0:
                    continue
                remote(
                    part.at[step, 1], sums.at[step, mine], all_sem(step), to_x, at_y[dy]
                ).start()

    def end_sum(step):
        wait_bytes(sums.at[step, pl.ds(0, chips * ny - 1)], recv.at[all_sem(step)])
        return jnp.broadcast_to(jnp.sum(sums[step], axis=0), (8, 128))

    def first(i, carry):
        rho = collide(0, i, [home[30 + q * 10 + i] for q in range(19)])
        kind = home[i]
        phi, part_gas = level(kind, fluid_mass[i], rho)
        put_half(0, i, phi)
        share[i] = part_gas
        return carry

    bubble_lane = lane & (BUBBLES - 1)
    table = jnp.zeros((8, 128), F32)
    for b in range(BUBBLES):
        table = jnp.where(bubble_lane == b, gas_density[b], table)
    density_start = table
    lookup(table)

    gathered(1)
    lax.fori_loop(0, 10, first, 0, unroll=5)
    post_columns(0)
    faces = send_faces(0)
    started = [faces]
    kinds_right.wait_recv()
    kinds_left.wait_recv()
    wait_columns(kind_cols_in, kind_cols, KINDS + 2)
    lax.fori_loop(0, 10, find_near, 0, unroll=5)
    volume_start = member_sums()
    wait_columns(cols_in.at[0], cols, y_sem(0, 0))
    for face in faces:
        face.wait_recv()

    def stream_all(step):
        def one(i, carry):
            stream(step, i)
            return carry

        lax.fori_loop(0, 10, one, 0, unroll=5)

    stream_all(0)
    start_total = None
    for step in range(ITERS):

        def settle(i, carry):
            kind = home[i]
            rho = base_rho[i] + gas_here[i] * gas_rho[i]
            liquid_mass = jnp.where(
                kind == 1.0, fluid_mass[i] + gain[i], jnp.where(kind == 2.0, rho, 0.0)
            )
            fluid_mass[i] = liquid_mass
            phi, part_gas = level(kind, liquid_mass, rho)
            if step < ITERS - 1:
                put_half(step + 1, i, phi)
            share[i] = part_gas
            return carry

        lax.fori_loop(0, 10, settle, 0, unroll=5)
        volume = member_sums()
        if step == 0:
            volume = jnp.where(lane < BUBBLES, volume, volume_start)
        begin_sum(step, volume)

        if step < ITERS - 1:

            def again(i, carry):
                collide(step + 1, i, arrived(i))
                return carry

            middle_sum(step)
            lax.fori_loop(0, 10, again, 0, unroll=5)
            post_columns(step + 1)
            faces = send_faces(step + 1)
            started.append(faces)
            wait_columns(cols_in.at[step + 1], cols, y_sem(step + 1, 0))
            for face in faces:
                face.wait_recv()
            stream_all(step + 1)
        else:

            def last(i, carry):
                for q, value in enumerate(arrived(i)):
                    waiting[q, i] = value
                return carry

            middle_sum(step)
            lax.fori_loop(0, 10, last, 0)
            store_g = pltpu.make_async_copy(waiting, out_g, fetch.at[0])
            store_g.start()
        total = end_sum(step)
        if step == 0:
            other = pltpu.roll(total, 64, 1)
            start_total = jnp.where(lane < BUBBLES, other, total)
            total = jnp.where(lane < BUBBLES, total, other)
        lookup(density_start * start_total / total)

    out_m[0:10] = fluid_mass[...]
    out_m[10:20] = home[0:10]
    out_m[20:30] = gas_here[...]
    out_v[...] = total[0:1, :BUBBLES] * (BUBBLES / (ngx * ny * 2 * 40 * 128))

    store_g.wait()
    for which in range(2):
        base, per, big, sides, got, pieces = chunks[which]
        for side, tiles in sides:

            @pl.when(core == side)
            def _():
                wait_bytes(stage.at[pl.ds(0, chips * per - tiles)], send.at[SPREAD + which])
                wait_bytes(
                    pieces.at[pl.ds(0, ngx - 1), pl.ds(0, tiles)], send.at[GATHER + which]
                )

    kinds_right.wait_send()
    kinds_left.wait_send()
    columns_sent(kind_cols_in, KINDS + 2)
    for step in range(ITERS):
        for face in started[step]:
            face.wait_send()
        columns_sent(cols_in.at[step], y_sem(step, 0))
        wait_bytes(mate_sum.at[step], send.at[mate_sem(step)])
        wait_bytes(sums.at[step, pl.ds(0, chips * ny - 1)], send.at[all_sem(step)])


def hand_over(g, m, v, out_g, out_m, out_v, held_g, held_m, held_v, sem):
    cuts = (0, 4, 8, 12, 16, 19)
    groups = [pl.ds(a, b - a) for a, b in zip(cuts, cuts[1:])]
    inward = [pltpu.make_async_copy(m, held_m, sem.at[0, 5])]
    inward += [
        pltpu.make_async_copy(g.at[at], held_g.at[at], sem.at[0, k])
        for k, at in enumerate(groups)
    ]
    inward.append(pltpu.make_async_copy(v, held_v, sem.at[0, 6]))
    for one in inward:
        one.start()
    inward[0].wait()
    outward = [pltpu.make_async_copy(held_m.at[0:10], out_m, sem.at[1, 5])]
    outward[0].start()
    gas = held_m[10:20] == 0.0
    density = held_m[20:30]
    for k, (a, b) in enumerate(zip(cuts, cuts[1:])):
        inward[k + 1].wait()
        for q in range(a, b):
            held_g[q] = jnp.where(gas, density, held_g[q])
        outward.append(
            pltpu.make_async_copy(held_g.at[groups[k]], out_g.at[groups[k]], sem.at[1, k])
        )
        outward[-1].start()
    inward[-1].wait()
    outward.append(pltpu.make_async_copy(held_v, out_v, sem.at[1, 6]))
    outward[-1].start()
    for one in outward:
        one.wait()


def chunk_tiles(chips):
    per = -(-220 // chips)
    return (per * 4 + 6) // 7, per - (per * 4 + 6) // 7


def solution(mesh):
    ngx, ny = mesh.shape["gx"], mesh.shape["gy"]
    nx, nz = (4, 8) if ngx == 64 else (1, ngx // 2)
    chips = ngx // 2
    per_a, per_b = chunk_tiles(chips)
    big_a, big_b = (per_a + 1) // 2, (per_b + 1) // 2

    def per_device(populations, mass, cell_type, bubble_id, slab_source, gas_density):
        vmem = pl.BlockSpec(memory_space=pltpu.VMEM)
        hbm = pl.BlockSpec(memory_space=pltpu.HBM)

        def tiles(count, dtype=F32):
            return pltpu.VMEM((count, 8, 128), dtype)

        g, m, v = pl.pallas_call(
            functools.partial(kernel, (nx, nz, ny)),
            out_shape=(
                jax.ShapeDtypeStruct((19, 10, 8, 128), F32),
                jax.ShapeDtypeStruct((30, 8, 128), F32),
                jax.ShapeDtypeStruct((1, BUBBLES), F32),
            ),
            in_specs=[hbm] * 6,
            out_specs=(hbm, vmem, vmem),
            scratch_shapes=[
                tiles(chips * (per_a + per_b) + 1),
                tiles(20, jnp.int32),
                pltpu.SMEM((ngx,), jnp.int32),
                pltpu.SMEM((BUBBLES,), F32),
                pltpu.VMEM((ngx, big_a, 8, 128), F32),
                pltpu.VMEM((ngx, big_b, 8, 128), F32),
                pltpu.VMEM((ngx, big_a, 8, 128), F32),
                pltpu.VMEM((ngx, big_b, 8, 128), F32),
                tiles(chips * (per_a + per_b)),
                pltpu.VMEM((ITERS, 4, 20, 56, 128), F32),
                pltpu.VMEM((4, 56, 128), F32),
                pltpu.VMEM((19, 10, 8, 128), F32),
                pltpu.VMEM((19, 10, 8, 128), F32),
                pltpu.VMEM((3, 10, 8, 128), F32),
                tiles(10, jnp.int32),
                tiles(10),
                tiles(10),
                tiles(10),
                tiles(10),
                tiles(10),
                tiles(10),
                pltpu.VMEM((ITERS, 2, 40, 128), F32),
                pltpu.VMEM((ITERS, 2, 3, 40, 128), F32),
                pltpu.VMEM((2, 56, 128), F32),
                pltpu.VMEM((2, 40, 128), F32),
                pltpu.VMEM((2, 3, 40, 128), F32),
                pltpu.VMEM((2, 56, 128), F32),
                pltpu.VMEM((ITERS, 1, 128), F32),
                pltpu.VMEM((ITERS, chips * ny, 1, 128), F32),
                pltpu.VMEM((ITERS, 2, 1, 128), F32),
                pltpu.SemaphoreType.DMA((6,)),
                pltpu.SemaphoreType.DMA((8 + ITERS * 8,)),
                pltpu.SemaphoreType.DMA((8 + ITERS * 8,)),
                pltpu.SemaphoreType.REGULAR,
            ],
            compiler_params=pltpu.CompilerParams(
                collective_id=0, has_side_effects=True, vmem_limit_bytes=VMEM_LIMIT
            ),
        )(
            populations.reshape(190, 8, 128),
            mass.reshape(10, 8, 128),
            cell_type.reshape(10, 8, 128),
            bubble_id.reshape(10, 8, 128),
            slab_source,
            gas_density,
        )
        anywhere = pl.BlockSpec(memory_space=pl.ANY)
        g, m, v = pl.pallas_call(
            hand_over,
            out_shape=(
                jax.ShapeDtypeStruct((19, 10, 8, 128), F32),
                jax.ShapeDtypeStruct((10, 8, 128), F32),
                jax.ShapeDtypeStruct((1, BUBBLES), F32),
            ),
            in_specs=[anywhere] * 3,
            out_specs=(hbm, hbm, hbm),
            scratch_shapes=[
                pltpu.VMEM((19, 10, 8, 128), F32),
                tiles(30),
                pltpu.VMEM((1, BUBBLES), F32),
                pltpu.SemaphoreType.DMA((2, 7)),
            ],
            compiler_params=pltpu.CompilerParams(vmem_limit_bytes=VMEM_LIMIT),
        )(g, m, v)
        return g.reshape(populations.shape), m.reshape(mass.shape), v.reshape(BUBBLES)

    return jax.shard_map(
        per_device,
        mesh=mesh,
        in_specs=(
            P(None, "gx", None, "gy"),
            P("gx", None, "gy"),
            P("gx", None, "gy"),
            P("gx", None, "gy"),
            P(),
            P(),
        ),
        out_specs=(P(None, "gx", None, "gy"), P("gx", None, "gy"), P()),
        check_vma=False,
    )
```
